32 devices in a mesh: rep: 2 (over y), grp: 2 (over core), ep: 8 (over z, x).
Axes of the slice: x: 2, y: 2, z: 4, core: 2. Of those that a mesh axis runs over, the one named last changes fastest.
Arguments:
- tokens: bfloat16 [4096, 2048], P(('rep', 'grp', 'ep')), parts along dimension 0, may hold values from -6 to 6
- cotangent: bfloat16 [4096, 2048], P(('rep', 'grp', 'ep')), parts along dimension 0, may hold values from -6 to 6
- routes: int32 [4096, 4], P(('rep', 'grp', 'ep')), parts along dimension 0, may hold values from 0 to 15, all different within a row; in each aligned block of 128 rows (0 to 127, 128 to 255, ...) at most 48 rows name the same one
- gates: bfloat16 [4096, 4], P(('rep', 'grp', 'ep')), parts along dimension 0, may hold values from 0.049804688 to 1
- w_gate: bfloat16 [16, 2048, 768], P(('grp', 'ep')), may hold values from -0.125 to 0.125
- w_up: bfloat16 [16, 2048, 768], P(('grp', 'ep')), may hold values from -0.125 to 0.125
- w_down: bfloat16 [16, 768, 2048], P(('grp', 'ep')), may hold values from -0.21875 to 0.21875
Outputs:
- mixed: bfloat16 [4096, 2048], P(('rep', 'grp', 'ep')), parts along dimension 0
- d_tokens: bfloat16 [4096, 2048], P(('rep', 'grp', 'ep')), parts along dimension 0
- d_gates: float32 [4096, 4], P(('rep', 'grp', 'ep')), parts along dimension 0
The draws below stay inside these ranges and needn't reach their ends.
There are 2 independent parts, one for each index of `rep`. The reference program is written for one: setup_inputs(seed, part) draws one part's arguments, and reference() takes and returns one part's arrays. A program takes and returns all parts, laid end to end along the dimension named above; an argument that names none is the same for every part. Nothing has to cross between parts.
Inputs may be any that keep to these rules, and one draw needn't show every extreme that they name: `routes`: each row names 4 different experts; of the 128 rows of one device at most 48 name one expert, a bound that some block reaches of them.
All inputs are finite; a program needn't handle non-finite values.
Results may differ from the reference program's by a relative error of at most 0.0058.
Values may be sent and summed in bfloat16 or wider, within the bound.
No kernel may reach another device: no remote copies, remote signals or barrier semaphores. Data moves between devices by JAX's collectives and lax.ppermute only.
A program may use at most 128 MiB of HBM per device.

```python
import math
import jax
import jax.numpy as jnp
import numpy as np
from jax import lax

D = 2048
FF = 768
TOP = 4
TOK_DEV = 128
EXPERTS = 16
TOKENS = 2048
CAP = 48
N_GRP = 2
N_EP = 8


def block_levels(rng, dims, cuts, smallest, largest):
    def one(position, shards_of):
        draws = jax.random.uniform(jax.random.fold_in(jax.random.fold_in(rng, 6), position), (shards_of,), jnp.float32, smallest / len(cuts), largest / len(cuts))
        return jnp.repeat(jnp.exp(draws), dims[position] // shards_of).reshape((-1,) + (1,) * (len(dims) - position - 1))

    loudness = one(*cuts[0])
    for cut in cuts[1:]:
        loudness = loudness * one(*cut)
    return loudness


def deal_out(key, own, number, rows, count, top, limit, lean):
    ranking = jax.random.permutation(key, count)
    heavy_load, common = shares(count, rows * top, limit, lean, True), shares(count, rows * top, limit, lean, False)
    places = jnp.arange(count)

    def named(tallies, offset_by):
        used = int((tallies > 0).sum())
        fixed = max(1, used // 4)
        passed = fixed + (places - fixed + offset_by * (used - fixed)) % max(1, count - fixed)
        return jnp.zeros((count,), jnp.int32).at[ranking[jnp.where(places < fixed, places, passed)]].set(jnp.asarray(tallies, jnp.int32))

    tallies = jnp.where(number % 4 == 0, named(heavy_load, number // 4), named(common, number - number // 4 - 1))
    mixed = jax.random.permutation(jax.random.fold_in(own, 3), count)
    donor, receiver = mixed[0:count // 2 * 2:2], mixed[1:count // 2 * 2:2]
    room = jnp.minimum(tallies[donor] - 1, limit - tallies[receiver]) // 2
    room = jnp.where((donor == ranking[0]) | (receiver == ranking[0]) | (tallies[receiver] == 0), 0, jnp.maximum(room, 0))
    passed = jax.random.randint(jax.random.fold_in(own, 4), (count // 2,), 0, 1 << 20) % (room + 1)
    tallies = tallies.at[donor].add(-passed).at[receiver].add(passed)
    members = jnp.searchsorted(jnp.cumsum(tallies), jnp.arange(rows * top), side="right").astype(jnp.int32)
    grid = members.reshape(top, rows).T
    grid = grid[jax.random.permutation(jax.random.fold_in(own, 1), rows)]
    offset_by = jax.random.randint(jax.random.fold_in(own, 2), (rows, 1), 0, top)
    return jnp.take_along_axis(grid, (jnp.arange(top)[None, :] + offset_by) % top, axis=1)


def shares(count, total, bound, slope, full):
    loads = [(1 << 20) // math.isqrt(grade ** slope) + 1 for grade in range(1, count + 1)]
    largest = bound if full else min(bound, max(-(-total // count), total * loads[0] // sum(loads)))
    least = 1 if total - largest >= count - 1 else 0
    holding, surplus = [largest] + [least] * (count - 1), total - largest - least * (count - 1)
    while surplus > 0:
        free = [i for i in range(1, count) if holding[i] < largest] or [i for i in range(1, count) if holding[i] < bound]
        mass, remaining = sum([loads[i] for i in free]), surplus
        for i in free:
            more = min(bound - holding[i], max(1, remaining * loads[i] // mass), surplus)
            holding[i] = holding[i] + more
            surplus = surplus - more
    return np.array(holding)


def scatter_about(stream_key, dims, deviation, reach, split=(), kind=jnp.bfloat16):
    loudness = block_levels(stream_key, dims, split, -0.22, 0.18) if split else 1.0
    values = jax.random.normal(stream_key, dims, jnp.float32) * deviation * loudness
    return jnp.minimum(jnp.maximum(values, -reach), reach).astype(kind)


def setup_inputs(seed: int = 0, part: int = 0) -> dict:
    seeds = jax.random.split(jax.random.key(seed), 8)
    part_splits = jax.random.split(jax.random.fold_in(seeds[7], part), 8)
    tokens = scatter_about(part_splits[0], (TOKENS, D), 1.0, 6.0, ((0, 16),))
    cotangent = scatter_about(part_splits[1], (TOKENS, D), 1.0, 6.0, ((0, 16),))
    routes_keys = jax.random.split(jax.random.fold_in(part_splits[2], 1), TOKENS // TOK_DEV)
    routes_turns = jax.random.permutation(jax.random.fold_in(part_splits[2], 3), TOKENS // TOK_DEV)
    routes = jax.vmap(lambda own, number: deal_out(jax.random.fold_in(part_splits[2], 2), own, number, TOK_DEV, EXPERTS, TOP, CAP, 2))(routes_keys, routes_turns).reshape((TOKENS, TOP))
    gates = jnp.clip(jnp.exp(math.log(1.0) - 2.9996462 * jax.random.uniform(part_splits[3], (TOKENS, TOP), jnp.float32) ** block_levels(part_splits[3], (TOKENS, TOP), ((0, 16),), -0.2, 0.2)), 0.049804688, 1.0).astype(jnp.bfloat16)
    w_gate = scatter_about(seeds[4], (EXPERTS, D, FF), D ** -0.5, 0.125, ((0, 16),))
    w_up = scatter_about(seeds[5], (EXPERTS, D, FF), D ** -0.5, 0.125, ((0, 16),))
    w_down = scatter_about(seeds[6], (EXPERTS, FF, D), FF ** -0.5, 0.21875, ((0, 16),))
    return {"tokens": tokens, "cotangent": cotangent, "routes": routes, "gates": gates, "w_gate": w_gate, "w_up": w_up, "w_down": w_down}


def expert_pass(rows_in, rows_grad, gate_mat, up_mat, down_mat):
    pre_gate = jnp.dot(rows_in, gate_mat, preferred_element_type=jnp.float32)
    pre_up = jnp.dot(rows_in, up_mat, preferred_element_type=jnp.float32)
    activated = jax.nn.silu(pre_gate)
    hidden = (activated * pre_up).astype(jnp.bfloat16)
    outputs = jnp.dot(hidden, down_mat, preferred_element_type=jnp.float32).astype(jnp.bfloat16)
    d_hidden = lax.dot_general(rows_grad, down_mat, (((1,), (1,)), ((), ())), preferred_element_type=jnp.float32)
    sigma = jax.nn.sigmoid(pre_gate)
    d_pre_gate = (d_hidden * pre_up * sigma * (1.0 + pre_gate * (1.0 - sigma))).astype(jnp.bfloat16)
    d_pre_up = (d_hidden * activated).astype(jnp.bfloat16)
    d_copy = lax.dot_general(d_pre_gate, gate_mat, (((1,), (1,)), ((), ())), preferred_element_type=jnp.float32)
    d_copy = d_copy + lax.dot_general(d_pre_up, up_mat, (((1,), (1,)), ((), ())), preferred_element_type=jnp.float32)
    return outputs, d_copy.astype(jnp.bfloat16)


def reference(tokens, cotangent, routes, gates, w_gate, w_up, w_down):
    token_count = tokens.shape[0]
    top_count = routes.shape[1]
    expert_count = w_gate.shape[0]
    slot_count = N_GRP * N_EP * CAP
    copy_count = token_count * top_count
    flat_experts = routes.reshape(-1)
    flat_gates = gates.reshape(-1).astype(jnp.float32)
    copy_ids = jnp.arange(copy_count, dtype=jnp.int32)
    width = tokens.shape[1]
    start = (jnp.zeros((token_count, width), jnp.float32), jnp.zeros((token_count, width), jnp.float32), jnp.zeros((copy_count,), jnp.float32))

    def serve(carry, expert):
        mixed_acc, grad_acc, gate_acc = carry
        chosen = flat_experts == expert
        rank = jnp.cumsum(chosen.astype(jnp.int32)) - 1
        where_to = jnp.where(chosen, rank, slot_count).astype(jnp.int32)
        slot_ids = jnp.zeros((slot_count + 1,), jnp.int32).at[where_to].set(copy_ids)[:slot_count]
        slot_live = jnp.zeros((slot_count + 1,), jnp.float32).at[where_to].set(1.0)[:slot_count]
        token_ids = (slot_ids // top_count).astype(jnp.int32)
        rows_in = tokens[token_ids]
        rows_grad = cotangent[token_ids]
        outputs, d_copy = expert_pass(rows_in, rows_grad, w_gate[expert], w_up[expert], w_down[expert])
        weight = flat_gates[slot_ids] * slot_live
        mixed_acc = mixed_acc.at[token_ids].add(weight[:, None] * outputs.astype(jnp.float32))
        grad_acc = grad_acc.at[token_ids].add(weight[:, None] * d_copy.astype(jnp.float32))
        inner = jnp.sum(rows_grad.astype(jnp.float32) * outputs.astype(jnp.float32), axis=1) * slot_live
        gate_acc = gate_acc.at[slot_ids].add(inner)
        return (mixed_acc, grad_acc, gate_acc), None

    final, unused = lax.scan(serve, start, jnp.arange(expert_count, dtype=jnp.int32))
    mixed_acc, grad_acc, gate_acc = final
    return mixed_acc.astype(jnp.bfloat16), grad_acc.astype(jnp.bfloat16), gate_acc.reshape(token_count, top_count)
```

```python
import jax
import jax.numpy as jnp
from jax import lax
from jax.sharding import PartitionSpec as P


def expert_pass(rows_in, rows_grad, gate_mat, up_mat, down_mat):
    pre_gate = jnp.dot(rows_in, gate_mat, preferred_element_type=jnp.float32)
    pre_up = jnp.dot(rows_in, up_mat, preferred_element_type=jnp.float32)
    activated = jax.nn.silu(pre_gate)
    hidden = (activated * pre_up).astype(jnp.bfloat16)
    outputs = jnp.dot(hidden, down_mat, preferred_element_type=jnp.float32).astype(jnp.bfloat16)
    d_hidden = lax.dot_general(
        rows_grad, down_mat, (((1,), (1,)), ((), ())), preferred_element_type=jnp.float32
    )
    sigma = jax.nn.sigmoid(pre_gate)
    d_pre_gate = (d_hidden * pre_up * sigma * (1.0 + pre_gate * (1.0 - sigma))).astype(jnp.bfloat16)
    d_pre_up = (d_hidden * activated).astype(jnp.bfloat16)
    both_pre = jnp.concatenate([d_pre_gate, d_pre_up], axis=1)
    both_mats = jnp.concatenate([gate_mat, up_mat], axis=1)
    d_copy = lax.dot_general(
        both_pre, both_mats, (((1,), (1,)), ((), ())), preferred_element_type=jnp.float32
    )
    return (outputs, d_copy.astype(jnp.bfloat16))


def run_items(pieces, gate_mat, up_mat, down_mat):
    rows_in, rows_grad = pieces
    lead_shape = rows_in.shape[:2]
    width = rows_in.shape[2]
    outputs, d_copy = expert_pass(
        rows_in.reshape(-1, width), rows_grad.reshape(-1, width), gate_mat, up_mat, down_mat
    )
    return (outputs.reshape(lead_shape + (width,)), d_copy.reshape(lead_shape + (width,)))


def ranks_of(chosen_hot):
    running = jnp.cumsum(chosen_hot, axis=-2)
    return jnp.sum(chosen_hot * running, axis=-1) - 1


def body_exchange(tokens, cotangent, routes, gates, w_gate, w_up, w_down):
    token_count = tokens.shape[0]
    width = tokens.shape[1]
    top_count = routes.shape[1]
    copy_count = token_count * top_count
    gate_mat = w_gate[0]
    up_mat = w_up[0]
    down_mat = w_down[0]
    expert_count = lax.axis_size(("grp", "ep"))
    capacity = max(2, 3 * token_count * top_count // (2 * expert_count))
    flat_experts = routes.reshape(-1)
    chosen_hot = (
        flat_experts[:, None] == jnp.arange(expert_count, dtype=jnp.int32)[None, :]
    ).astype(jnp.int32)
    slot_of = flat_experts * capacity + ranks_of(chosen_hot)
    token_of = jnp.arange(copy_count, dtype=jnp.int32) // top_count
    slot_token = jnp.zeros((expert_count * capacity,), jnp.int32).at[slot_of].set(token_of)
    slot_live = jnp.zeros((expert_count * capacity,), jnp.bool_).at[slot_of].set(True)
    send_in = jnp.where(
        slot_live[:, None], tokens[slot_token], jnp.zeros((), tokens.dtype)
    ).reshape(expert_count, capacity, width)
    send_grad = jnp.where(
        slot_live[:, None], cotangent[slot_token], jnp.zeros((), cotangent.dtype)
    ).reshape(expert_count, capacity, width)
    outputs, d_copy = run_items(
        (
            lax.all_to_all(send_in, ("grp", "ep"), split_axis=0, concat_axis=0, tiled=True),
            lax.all_to_all(send_grad, ("grp", "ep"), split_axis=0, concat_axis=0, tiled=True),
        ),
        gate_mat,
        up_mat,
        down_mat,
    )
    back_out = lax.all_to_all(outputs, ("grp", "ep"), split_axis=0, concat_axis=0, tiled=True)
    back_grad = lax.all_to_all(d_copy, ("grp", "ep"), split_axis=0, concat_axis=0, tiled=True)
    copy_out = back_out.reshape(-1, width)[slot_of].reshape(token_count, top_count, width)
    copy_grad = back_grad.reshape(-1, width)[slot_of].reshape(token_count, top_count, width)
    weight = gates.astype(jnp.float32)
    mixed = jnp.sum(weight[:, :, None] * copy_out.astype(jnp.float32), axis=1)
    d_tokens = jnp.sum(weight[:, :, None] * copy_grad.astype(jnp.float32), axis=1)
    d_gates = jnp.einsum("tkd,td->tk", copy_out, cotangent, preferred_element_type=jnp.float32)
    return (mixed.astype(jnp.bfloat16), d_tokens.astype(jnp.bfloat16), d_gates)


def ring_order(count):
    return list(range(0, count, 2)) + list(range(count - 1, 0, -2))


def ring_shift(array, count, step):
    order = ring_order(count)
    pairs = [(order[i], order[(i + step) % count]) for i in range(count)]
    return lax.ppermute(array, "ep", pairs)


def ring_gather(shard, count, far_step):
    held = {0: shard}
    for step in (far_step, -far_step):
        hops = count // 2 if step == far_step else (count - 1) // 2
        moving = shard
        for hop in range(1, hops + 1):
            moving = ring_shift(moving, count, step)
            held[(-step * hop) % count] = moving
    return [held[place] for place in range(count)]


def ring_reduce(share_of, count, far_step):
    arrived = []
    for step in (far_step, -far_step):
        hops = count // 2 if step == far_step else (count - 1) // 2
        moving = None
        for hop in range(hops, 0, -1):
            moving = ring_shift(share_of((step * hop) % count, moving), count, step)
        arrived.append(moving)
    total = share_of(0, arrived[0], arrived[1])
    return total


def swap_cores(array):
    return lax.ppermute(array, "grp", [(0, 1), (1, 0)])


def body_ring(tokens, cotangent, routes, gates, w_gate, w_up, w_down):
    token_count = tokens.shape[0]
    width = tokens.shape[1]
    top_count = routes.shape[1]
    chips = lax.axis_size("ep")
    expert_count = lax.axis_size(("grp", "ep"))
    capacity = max(2, 3 * token_count * top_count // (2 * expert_count))
    f32, bf16 = jnp.float32, jnp.bfloat16

    in_shards = ring_gather(tokens, chips, 1)
    grad_shards = ring_gather(cotangent, chips, -1)
    gate_mats = (w_gate[0], swap_cores(w_gate[0]))
    up_mats = (w_up[0], swap_cores(w_up[0]))
    down_mats = (w_down[0], swap_cores(w_down[0]))

    core = lax.axis_index("grp")
    chip = lax.axis_index("ep")
    order = jnp.array(ring_order(chips), jnp.int32)
    place = jnp.argmax(order == chip).astype(jnp.int32)
    sources = order[(place + jnp.arange(chips, dtype=jnp.int32)) % chips]
    table = jnp.concatenate([routes.astype(f32), gates.astype(f32)], axis=1).T
    tables = lax.all_gather(table, "ep", axis=0)[sources]
    named = tables[:, :top_count].astype(jnp.int32)
    weights = tables[:, top_count:]
    mine = jnp.stack([core * chips + chip, (1 - core) * chips + chip])
    hits = named[:, None] == mine[None, :, None, None]
    weight = jnp.sum(jnp.where(hits, weights[:, None], 0.0), axis=2)
    hit = jnp.any(hits, axis=2)
    before = (
        jnp.arange(token_count)[:, None] <= jnp.arange(token_count)[None, :]
    ).astype(bf16)
    rank = jnp.dot(
        hit.astype(bf16).reshape(-1, token_count), before, preferred_element_type=f32
    ).reshape(hit.shape).astype(jnp.int32) - 1
    slots = jnp.arange(capacity, dtype=jnp.int32)
    picks = hit[:, :, None, :] & (rank[:, :, None, :] == slots[None, None, :, None])
    rows_per = 2 * capacity
    pick = picks.astype(bf16).reshape(chips, rows_per, token_count)
    spread = jnp.where(picks, weight[:, :, None, :], 0.0).astype(bf16).reshape(
        chips, rows_per, token_count
    )

    def gather_rows(shards):
        parts = [
            jnp.dot(pick[s], shards[s], preferred_element_type=f32).astype(bf16)
            for s in range(chips)
        ]
        stacked = jnp.stack(parts).reshape(chips, 2, capacity, width)
        return [stacked[:, e].reshape(chips * capacity, width) for e in range(2)]

    def scatter_rows(outputs):
        blocks = [o.reshape(chips, capacity, width) for o in outputs]

        def share_of(s, *partials):
            block = jnp.concatenate([b[s] for b in blocks], axis=0)
            total = lax.dot_general(
                spread[s], block, (((0,), (0,)), ((), ())), preferred_element_type=f32
            )
            for partial in partials:
                if partial is not None:
                    total = total + partial.astype(f32)
            return total.astype(bf16)

        return share_of

    rows_in = gather_rows(in_shards)
    pre_gate = [jnp.dot(rows_in[e], gate_mats[e], preferred_element_type=f32) for e in range(2)]
    pre_up = [jnp.dot(rows_in[e], up_mats[e], preferred_element_type=f32) for e in range(2)]
    activated = [jax.nn.silu(v) for v in pre_gate]
    hidden = [(activated[e] * pre_up[e]).astype(bf16) for e in range(2)]
    outputs = [
        jnp.dot(hidden[e], down_mats[e], preferred_element_type=f32).astype(bf16)
        for e in range(2)
    ]
    mixed = ring_reduce(scatter_rows(outputs), chips, 1)

    rows_grad = gather_rows(grad_shards)
    last = (((1,), (1,)), ((), ()))
    d_copies = []
    inner = []
    for e in range(2):
        d_hidden = lax.dot_general(rows_grad[e], down_mats[e], last, preferred_element_type=f32)
        sigma = jax.nn.sigmoid(pre_gate[e])
        d_pre_gate = (d_hidden * pre_up[e] * sigma * (1.0 + pre_gate[e] * (1.0 - sigma))).astype(bf16)
        d_pre_up = (d_hidden * activated[e]).astype(bf16)
        d_copy = lax.dot_general(d_pre_gate, gate_mats[e], last, preferred_element_type=f32)
        d_copy = d_copy + lax.dot_general(d_pre_up, up_mats[e], last, preferred_element_type=f32)
        d_copies.append(d_copy.astype(bf16))
        inner.append(
            jnp.sum(rows_grad[e].astype(f32) * outputs[e].astype(f32), axis=1).reshape(
                chips, capacity
            )
        )
    d_tokens = ring_reduce(scatter_rows(d_copies), chips, -1)

    inner = jnp.stack(inner, axis=1)
    per_token = jnp.sum(jnp.where(picks, inner[:, :, :, None], 0.0), axis=2)
    by_chip = jnp.zeros_like(per_token).at[sources].set(per_token)
    returned = lax.all_to_all(by_chip, "ep", split_axis=0, concat_axis=0, tiled=True)
    chip_ids = jnp.arange(chips, dtype=jnp.int32)
    served = jnp.stack([core * chips + chip_ids, (1 - core) * chips + chip_ids], axis=1)
    chosen = routes.T[None, None] == served[:, :, None, None]
    d_gates = jnp.sum(jnp.where(chosen, returned[:, :, None, :], 0.0), axis=(0, 1)).T
    return (mixed, d_tokens, d_gates)


def solution(mesh):
    plan = body_ring if mesh.shape["ep"] <= 8 and mesh.shape["grp"] == 2 else body_exchange
    return jax.shard_map(
        plan,
        mesh=mesh,
        in_specs=(
            P(("rep", "grp", "ep"), None),
            P(("rep", "grp", "ep"), None),
            P(("rep", "grp", "ep"), None),
            P(("rep", "grp", "ep"), None),
            P(("grp", "ep"), None, None),
            P(("grp", "ep"), None, None),
            P(("grp", "ep"), None, None),
        ),
        out_specs=(
            P(("rep", "grp", "ep"), None),
            P(("rep", "grp", "ep"), None),
            P(("rep", "grp", "ep"), None),
        ),
        check_vma=False,
    )
```

```python
import jax
import jax.numpy as jnp
from jax import lax
from jax.experimental import pallas as pl
from jax.experimental.pallas import tpu as pltpu
from jax.sharding import PartitionSpec as P


def expert_pass(rows_in, rows_grad, gate_mat, up_mat, down_mat):
    pre_gate = jnp.dot(rows_in, gate_mat, preferred_element_type=jnp.float32)
    pre_up = jnp.dot(rows_in, up_mat, preferred_element_type=jnp.float32)
    activated = jax.nn.silu(pre_gate)
    hidden = (activated * pre_up).astype(jnp.bfloat16)
    outputs = jnp.dot(hidden, down_mat, preferred_element_type=jnp.float32).astype(jnp.bfloat16)
    d_hidden = lax.dot_general(
        rows_grad, down_mat, (((1,), (1,)), ((), ())), preferred_element_type=jnp.float32
    )
    sigma = jax.nn.sigmoid(pre_gate)
    d_pre_gate = (d_hidden * pre_up * sigma * (1.0 + pre_gate * (1.0 - sigma))).astype(jnp.bfloat16)
    d_pre_up = (d_hidden * activated).astype(jnp.bfloat16)
    both_pre = jnp.concatenate([d_pre_gate, d_pre_up], axis=1)
    both_mats = jnp.concatenate([gate_mat, up_mat], axis=1)
    d_copy = lax.dot_general(
        both_pre, both_mats, (((1,), (1,)), ((), ())), preferred_element_type=jnp.float32
    )
    return (outputs, d_copy.astype(jnp.bfloat16))


def run_items(pieces, gate_mat, up_mat, down_mat):
    rows_in, rows_grad = pieces
    lead_shape = rows_in.shape[:2]
    width = rows_in.shape[2]
    outputs, d_copy = expert_pass(
        rows_in.reshape(-1, width), rows_grad.reshape(-1, width), gate_mat, up_mat, down_mat
    )
    return (outputs.reshape(lead_shape + (width,)), d_copy.reshape(lead_shape + (width,)))


def ranks_of(chosen_hot):
    running = jnp.cumsum(chosen_hot, axis=-2)
    return jnp.sum(chosen_hot * running, axis=-1) - 1


def body_exchange(tokens, cotangent, routes, gates, w_gate, w_up, w_down):
    token_count = tokens.shape[0]
    width = tokens.shape[1]
    top_count = routes.shape[1]
    copy_count = token_count * top_count
    gate_mat = w_gate[0]
    up_mat = w_up[0]
    down_mat = w_down[0]
    expert_count = lax.axis_size(("grp", "ep"))
    capacity = max(2, 3 * token_count * top_count // (2 * expert_count))
    flat_experts = routes.reshape(-1)
    chosen_hot = (
        flat_experts[:, None] == jnp.arange(expert_count, dtype=jnp.int32)[None, :]
    ).astype(jnp.int32)
    slot_of = flat_experts * capacity + ranks_of(chosen_hot)
    token_of = jnp.arange(copy_count, dtype=jnp.int32) // top_count
    slot_token = jnp.zeros((expert_count * capacity,), jnp.int32).at[slot_of].set(token_of)
    slot_live = jnp.zeros((expert_count * capacity,), jnp.bool_).at[slot_of].set(True)
    send_in = jnp.where(
        slot_live[:, None], tokens[slot_token], jnp.zeros((), tokens.dtype)
    ).reshape(expert_count, capacity, width)
    send_grad = jnp.where(
        slot_live[:, None], cotangent[slot_token], jnp.zeros((), cotangent.dtype)
    ).reshape(expert_count, capacity, width)
    outputs, d_copy = run_items(
        (
            lax.all_to_all(send_in, ("grp", "ep"), split_axis=0, concat_axis=0, tiled=True),
            lax.all_to_all(send_grad, ("grp", "ep"), split_axis=0, concat_axis=0, tiled=True),
        ),
        gate_mat,
        up_mat,
        down_mat,
    )
    back_out = lax.all_to_all(outputs, ("grp", "ep"), split_axis=0, concat_axis=0, tiled=True)
    back_grad = lax.all_to_all(d_copy, ("grp", "ep"), split_axis=0, concat_axis=0, tiled=True)
    copy_out = back_out.reshape(-1, width)[slot_of].reshape(token_count, top_count, width)
    copy_grad = back_grad.reshape(-1, width)[slot_of].reshape(token_count, top_count, width)
    weight = gates.astype(jnp.float32)
    mixed = jnp.sum(weight[:, :, None] * copy_out.astype(jnp.float32), axis=1)
    d_tokens = jnp.sum(weight[:, :, None] * copy_grad.astype(jnp.float32), axis=1)
    d_gates = jnp.einsum("tkd,td->tk", copy_out, cotangent, preferred_element_type=jnp.float32)
    return (mixed.astype(jnp.bfloat16), d_tokens.astype(jnp.bfloat16), d_gates)


def ring_order(count):
    return list(range(0, count, 2)) + list(range(count - 1, 0, -2))


def ring_shift(array, count, step):
    order = ring_order(count)
    pairs = [(order[i], order[(i + step) % count]) for i in range(count)]
    return lax.ppermute(array, "ep", pairs)


def ring_gather(shard, count, far_step):
    held = {0: shard}
    for step in (far_step, -far_step):
        hops = count // 2 if step == far_step else (count - 1) // 2
        moving = shard
        for hop in range(1, hops + 1):
            moving = ring_shift(moving, count, step)
            held[(-step * hop) % count] = moving
    return [held[place] for place in range(count)]


def after(array, *others):
    for other in others:
        array = array + other[:1, :1] * 0
    return array


def ring_reduce(share_of, count, far_step, first=(), seen=None):
    arrived = []
    for step in (far_step, -far_step):
        hops = count // 2 if step == far_step else (count - 1) // 2
        moving = None
        for hop in range(hops, 0, -1):
            share = share_of((step * hop) % count, moving)
            if moving is None:
                share = after(share, *first)
            moving = ring_shift(share, count, step)
            if seen is not None and hop == max(1, hops - 1):
                seen.append(moving)
        arrived.append(moving)
    total = share_of(0, arrived[0], arrived[1])
    return total


VMEM_LIMIT = 48 * 1024 * 1024
LAST = (((1,), (1,)), ((), ()))


def cut(size, most):
    return max(w for w in range(128, most + 1, 128) if size % w == 0)


def call_kernel(kernel, operands, kinds, outs, scratch, flops):
    spaces = {"any": pl.ANY, "vmem": pltpu.VMEM}
    return pl.pallas_call(
        kernel,
        out_shape=outs,
        in_specs=[pl.BlockSpec(memory_space=spaces[k]) for k in kinds],
        out_specs=[pl.BlockSpec(memory_space=pltpu.VMEM) for _ in outs],
        scratch_shapes=scratch,
        compiler_params=pltpu.CompilerParams(vmem_limit_bytes=VMEM_LIMIT),
        cost_estimate=pl.CostEstimate(flops=flops, bytes_accessed=1 << 20, transcendentals=0),
    )(*operands)


def pack_rows(parts, packed):
    half = parts[0].shape[0] // 2
    for e in range(2):
        for s, part in enumerate(parts):
            packed[e, s * half : (s + 1) * half, :] = part[e * half : (e + 1) * half, :]


def run_hidden(parts, gate_mats, up_mats):
    count, rows, width = len(parts), parts[0].shape[0], parts[0].shape[1]
    units = gate_mats[0].shape[1]
    total = count * rows // 2
    tile = cut(units, 256)
    tiles = units // tile

    def kernel(*refs):
        part_refs, mats = refs[:count], refs[count : count + 4]
        hidden_ref, slope_ref, act_ref, packed, held, sems = refs[count + 4 :]
        copies = {}
        for e in range(2):
            for n in range(tiles):
                for m in range(2):
                    copies[e, n, m] = pltpu.make_async_copy(
                        mats[2 * m + e].at[:, n * tile : (n + 1) * tile],
                        held.at[e, n, m],
                        sems.at[e, n, m],
                    )
                    copies[e, n, m].start()
        pack_rows(part_refs, packed)
        for e in range(2):
            for n in range(tiles):
                span = slice(n * tile, (n + 1) * tile)
                copies[e, n, 0].wait()
                gate = jnp.dot(packed[e], held[e, n, 0], preferred_element_type=jnp.float32)
                copies[e, n, 1].wait()
                up = jnp.dot(packed[e], held[e, n, 1], preferred_element_type=jnp.float32)
                sigma = 1.0 / (1.0 + jnp.exp(-gate))
                act = gate * sigma
                hidden_ref[e, :, span] = (act * up).astype(jnp.bfloat16)
                slope_ref[e, :, span] = up * sigma * (1.0 + gate * (1.0 - sigma))
                act_ref[e, :, span] = act

    return call_kernel(
        kernel,
        [*parts, *gate_mats, *up_mats],
        ["vmem"] * count + ["any"] * 4,
        [
            jax.ShapeDtypeStruct((2, total, units), jnp.bfloat16),
            jax.ShapeDtypeStruct((2, total, units), jnp.float32),
            jax.ShapeDtypeStruct((2, total, units), jnp.float32),
        ],
        [
            pltpu.VMEM((2, total, width), jnp.bfloat16),
            pltpu.VMEM((2, tiles, 2, width, tile), jnp.bfloat16),
            pltpu.SemaphoreType.DMA((2, tiles, 2)),
        ],
        8 * total * width * units,
    )


def run_down(hidden, down_mats, count):
    _, total, units = hidden.shape
    width = down_mats[0].shape[1]
    half = total // count
    tile = cut(width, 512)
    tiles = width // tile

    def kernel(hidden_ref, own_ref, other_ref, out_ref, held, sems):
        copies = {}
        for e, mat in enumerate((own_ref, other_ref)):
            for n in range(tiles):
                copies[e, n] = pltpu.make_async_copy(
                    mat.at[:, n * tile : (n + 1) * tile], held.at[e, n], sems.at[e, n]
                )
                copies[e, n].start()
        for e in range(2):
            for n in range(tiles):
                copies[e, n].wait()
                out = jnp.dot(hidden_ref[e], held[e, n], preferred_element_type=jnp.float32)
                out_ref[:, e * half : (e + 1) * half, n * tile : (n + 1) * tile] = (
                    out.astype(jnp.bfloat16).reshape(count, half, tile)
                )

    return call_kernel(
        kernel,
        [hidden, *down_mats],
        ["vmem", "any", "any"],
        [jax.ShapeDtypeStruct((count, 2 * half, width), jnp.bfloat16)],
        [
            pltpu.VMEM((2, tiles, units, tile), jnp.bfloat16),
            pltpu.SemaphoreType.DMA((2, tiles)),
        ],
        4 * total * width * units,
    )[0]


def run_d_hidden(parts, outputs, pick, slope, activated, down_mats):
    count, rows, width = len(parts), parts[0].shape[0], parts[0].shape[1]
    half = rows // 2
    _, total, units = slope.shape
    tile = cut(units, 256)
    tiles = units // tile
    tokens = pick.shape[2]

    def kernel(*refs):
        part_refs = refs[:count]
        out_ref, pick_ref, slope_ref, act_ref, own_ref, other_ref = refs[count : count + 6]
        d_gate_ref, d_up_ref, token_ref, packed, held, sems = refs[count + 6 :]
        copies = {}
        for e, mat in enumerate((own_ref, other_ref)):
            for n in range(tiles):
                copies[e, n] = pltpu.make_async_copy(
                    mat.at[n * tile : (n + 1) * tile, :], held.at[e, n], sems.at[e, n]
                )
                copies[e, n].start()
        pack_rows(part_refs, packed)
        for e in range(2):
            for n in range(tiles):
                span = slice(n * tile, (n + 1) * tile)
                copies[e, n].wait()
                d_hidden = lax.dot_general(
                    packed[e], held[e, n], LAST, preferred_element_type=jnp.float32
                )
                d_gate_ref[e, :, span] = (d_hidden * slope_ref[e, :, span]).astype(jnp.bfloat16)
                d_up_ref[e, :, span] = (d_hidden * act_ref[e, :, span]).astype(jnp.bfloat16)
        for s in range(count):
            inner = jnp.sum(
                part_refs[s][...].astype(jnp.float32) * out_ref[s].astype(jnp.float32),
                axis=1,
                keepdims=True,
            )
            spread = pick_ref[s].astype(jnp.float32) * inner
            for e in range(2):
                token_ref[s, e : e + 1, :] = jnp.sum(
                    spread[e * half : (e + 1) * half], axis=0, keepdims=True
                )

    return call_kernel(
        kernel,
        [*parts, outputs, pick, slope, activated, *down_mats],
        ["vmem"] * (count + 4) + ["any"] * 2,
        [
            jax.ShapeDtypeStruct((2, total, units), jnp.bfloat16),
            jax.ShapeDtypeStruct((2, total, units), jnp.bfloat16),
            jax.ShapeDtypeStruct((count, 2, tokens), jnp.float32),
        ],
        [
            pltpu.VMEM((2, total, width), jnp.bfloat16),
            pltpu.VMEM((2, tiles, tile, width), jnp.bfloat16),
            pltpu.SemaphoreType.DMA((2, tiles)),
        ],
        4 * total * width * units,
    )


def run_d_copy(d_pre_gate, d_pre_up, gate_mats, up_mats, count):
    _, total, units = d_pre_gate.shape
    width = gate_mats[0].shape[0]
    half = total // count
    tile = cut(width, 512)
    tiles = width // tile

    def kernel(d_gate_ref, d_up_ref, *refs):
        mats = refs[:4]
        out_ref, held, sems = refs[4:]
        copies = {}
        for e in range(2):
            for n in range(tiles):
                for m in range(2):
                    copies[e, n, m] = pltpu.make_async_copy(
                        mats[2 * m + e].at[n * tile : (n + 1) * tile, :],
                        held.at[e, n, m],
                        sems.at[e, n, m],
                    )
                    copies[e, n, m].start()
        for e in range(2):
            for n in range(tiles):
                copies[e, n, 0].wait()
                out = lax.dot_general(
                    d_gate_ref[e], held[e, n, 0], LAST, preferred_element_type=jnp.float32
                )
                copies[e, n, 1].wait()
                out = out + lax.dot_general(
                    d_up_ref[e], held[e, n, 1], LAST, preferred_element_type=jnp.float32
                )
                out_ref[:, e * half : (e + 1) * half, n * tile : (n + 1) * tile] = (
                    out.astype(jnp.bfloat16).reshape(count, half, tile)
                )

    return call_kernel(
        kernel,
        [d_pre_gate, d_pre_up, *gate_mats, *up_mats],
        ["vmem", "vmem"] + ["any"] * 4,
        [jax.ShapeDtypeStruct((count, 2 * half, width), jnp.bfloat16)],
        [
            pltpu.VMEM((2, tiles, 2, tile, units), jnp.bfloat16),
            pltpu.SemaphoreType.DMA((2, tiles, 2)),
        ],
        8 * total * width * units,
    )[0]


def swap_cores(array):
    return lax.ppermute(array, "grp", [(0, 1), (1, 0)])


def body_ring(tokens, cotangent, routes, gates, w_gate, w_up, w_down):
    token_count = tokens.shape[0]
    width = tokens.shape[1]
    top_count = routes.shape[1]
    chips = lax.axis_size("ep")
    expert_count = lax.axis_size(("grp", "ep"))
    capacity = max(2, 3 * token_count * top_count // (2 * expert_count))
    f32, bf16 = jnp.float32, jnp.bfloat16

    in_shards = ring_gather(tokens, chips, 1)
    late = min(2, (chips - 1) // 2)
    grad_shards = ring_gather(
        after(cotangent, in_shards[-late % chips], in_shards[late]), chips, -1
    )
    gate_mats = (w_gate[0], swap_cores(w_gate[0]))
    up_mats = (w_up[0], swap_cores(w_up[0]))
    down_mats = (w_down[0], swap_cores(w_down[0]))

    core = lax.axis_index("grp")
    chip = lax.axis_index("ep")
    order = jnp.array(ring_order(chips), jnp.int32)
    place = jnp.argmax(order == chip).astype(jnp.int32)
    sources = order[(place + jnp.arange(chips, dtype=jnp.int32)) % chips]
    table = jnp.concatenate([routes.astype(f32), gates.astype(f32)], axis=1).T
    copies = jnp.broadcast_to(table[None], (chips,) + table.shape)
    tables = lax.all_to_all(copies, "ep", split_axis=0, concat_axis=0, tiled=True)[sources]
    named = tables[:, :top_count].astype(jnp.int32)
    weights = tables[:, top_count:]
    mine = jnp.stack([core * chips + chip, (1 - core) * chips + chip])
    hits = named[:, None] == mine[None, :, None, None]
    weight = jnp.sum(jnp.where(hits, weights[:, None], 0.0), axis=2)
    hit = jnp.any(hits, axis=2)
    before = (
        jnp.arange(token_count)[:, None] <= jnp.arange(token_count)[None, :]
    ).astype(bf16)
    rank = jnp.dot(
        hit.astype(bf16).reshape(-1, token_count), before, preferred_element_type=f32
    ).reshape(hit.shape).astype(jnp.int32) - 1
    slots = jnp.arange(capacity, dtype=jnp.int32)
    picks = hit[:, :, None, :] & (rank[:, :, None, :] == slots[None, None, :, None])
    rows_per = 2 * capacity
    pick = picks.astype(bf16).reshape(chips, rows_per, token_count)
    spread = jnp.where(picks, weight[:, :, None, :], 0.0).astype(bf16).reshape(
        chips, rows_per, token_count
    )

    def gather_rows(shards):
        return [
            jnp.dot(pick[s], shards[s], preferred_element_type=f32).astype(bf16)
            for s in range(chips)
        ]

    def scatter_rows(blocks):
        def share_of(s, *partials):
            total = lax.dot_general(
                spread[s], blocks[s], (((0,), (0,)), ((), ())), preferred_element_type=f32
            )
            for partial in partials:
                if partial is not None:
                    total = total + partial.astype(f32)
            return total.astype(bf16)

        return share_of

    rows_in = gather_rows(in_shards)
    hidden, slope, activated = run_hidden(rows_in, gate_mats, up_mats)
    outputs = run_down(hidden, down_mats, chips)
    seen = []
    mixed = ring_reduce(scatter_rows(outputs), chips, 1, seen=seen)

    rows_grad = gather_rows(grad_shards)
    d_pre_gate, d_pre_up, per_token = run_d_hidden(
        rows_grad, outputs, pick, slope, activated, down_mats
    )
    d_copies = run_d_copy(d_pre_gate, d_pre_up, gate_mats, up_mats, chips)
    d_tokens = ring_reduce(scatter_rows(d_copies), chips, -1, first=seen)

    by_chip = jnp.zeros_like(per_token).at[sources].set(per_token)
    returned = lax.all_to_all(by_chip, "ep", split_axis=0, concat_axis=0, tiled=True)
    chip_ids = jnp.arange(chips, dtype=jnp.int32)
    served = jnp.stack([core * chips + chip_ids, (1 - core) * chips + chip_ids], axis=1)
    chosen = routes.T[None, None] == served[:, :, None, None]
    d_gates = jnp.sum(jnp.where(chosen, returned[:, :, None, :], 0.0), axis=(0, 1)).T
    return (mixed, d_tokens, d_gates)


def solution(mesh):
    plan = body_ring if mesh.shape["ep"] <= 8 and mesh.shape["grp"] == 2 else body_exchange
    return jax.shard_map(
        plan,
        mesh=mesh,
        in_specs=(
            P(("rep", "grp", "ep"), None),
            P(("rep", "grp", "ep"), None),
            P(("rep", "grp", "ep"), None),
            P(("rep", "grp", "ep"), None),
            P(("grp", "ep"), None, None),
            P(("grp", "ep"), None, None),
            P(("grp", "ep"), None, None),
        ),
        out_specs=(
            P(("rep", "grp", "ep"), None),
            P(("rep", "grp", "ep"), None),
            P(("rep", "grp", "ep"), None),
        ),
        check_vma=False,
    )
```

```python
import jax
import jax.numpy as jnp
from jax import lax
from jax.experimental import pallas as pl
from jax.experimental.pallas import tpu as pltpu
from jax.sharding import PartitionSpec as P


def expert_pass(rows_in, rows_grad, gate_mat, up_mat, down_mat):
    pre_gate = jnp.dot(rows_in, gate_mat, preferred_element_type=jnp.float32)
    pre_up = jnp.dot(rows_in, up_mat, preferred_element_type=jnp.float32)
    activated = jax.nn.silu(pre_gate)
    hidden = (activated * pre_up).astype(jnp.bfloat16)
    outputs = jnp.dot(hidden, down_mat, preferred_element_type=jnp.float32).astype(jnp.bfloat16)
    d_hidden = lax.dot_general(
        rows_grad, down_mat, (((1,), (1,)), ((), ())), preferred_element_type=jnp.float32
    )
    sigma = jax.nn.sigmoid(pre_gate)
    d_pre_gate = (d_hidden * pre_up * sigma * (1.0 + pre_gate * (1.0 - sigma))).astype(jnp.bfloat16)
    d_pre_up = (d_hidden * activated).astype(jnp.bfloat16)
    both_pre = jnp.concatenate([d_pre_gate, d_pre_up], axis=1)
    both_mats = jnp.concatenate([gate_mat, up_mat], axis=1)
    d_copy = lax.dot_general(
        both_pre, both_mats, (((1,), (1,)), ((), ())), preferred_element_type=jnp.float32
    )
    return (outputs, d_copy.astype(jnp.bfloat16))


def run_items(pieces, gate_mat, up_mat, down_mat):
    rows_in, rows_grad = pieces
    lead_shape = rows_in.shape[:2]
    width = rows_in.shape[2]
    outputs, d_copy = expert_pass(
        rows_in.reshape(-1, width), rows_grad.reshape(-1, width), gate_mat, up_mat, down_mat
    )
    return (outputs.reshape(lead_shape + (width,)), d_copy.reshape(lead_shape + (width,)))


def ranks_of(chosen_hot):
    running = jnp.cumsum(chosen_hot, axis=-2)
    return jnp.sum(chosen_hot * running, axis=-1) - 1


def body_exchange(tokens, cotangent, routes, gates, w_gate, w_up, w_down):
    token_count = tokens.shape[0]
    width = tokens.shape[1]
    top_count = routes.shape[1]
    copy_count = token_count * top_count
    gate_mat = w_gate[0]
    up_mat = w_up[0]
    down_mat = w_down[0]
    expert_count = lax.axis_size(("grp", "ep"))
    capacity = max(2, 3 * token_count * top_count // (2 * expert_count))
    flat_experts = routes.reshape(-1)
    chosen_hot = (
        flat_experts[:, None] == jnp.arange(expert_count, dtype=jnp.int32)[None, :]
    ).astype(jnp.int32)
    slot_of = flat_experts * capacity + ranks_of(chosen_hot)
    token_of = jnp.arange(copy_count, dtype=jnp.int32) // top_count
    slot_token = jnp.zeros((expert_count * capacity,), jnp.int32).at[slot_of].set(token_of)
    slot_live = jnp.zeros((expert_count * capacity,), jnp.bool_).at[slot_of].set(True)
    send_in = jnp.where(
        slot_live[:, None], tokens[slot_token], jnp.zeros((), tokens.dtype)
    ).reshape(expert_count, capacity, width)
    send_grad = jnp.where(
        slot_live[:, None], cotangent[slot_token], jnp.zeros((), cotangent.dtype)
    ).reshape(expert_count, capacity, width)
    outputs, d_copy = run_items(
        (
            lax.all_to_all(send_in, ("grp", "ep"), split_axis=0, concat_axis=0, tiled=True),
            lax.all_to_all(send_grad, ("grp", "ep"), split_axis=0, concat_axis=0, tiled=True),
        ),
        gate_mat,
        up_mat,
        down_mat,
    )
    back_out = lax.all_to_all(outputs, ("grp", "ep"), split_axis=0, concat_axis=0, tiled=True)
    back_grad = lax.all_to_all(d_copy, ("grp", "ep"), split_axis=0, concat_axis=0, tiled=True)
    copy_out = back_out.reshape(-1, width)[slot_of].reshape(token_count, top_count, width)
    copy_grad = back_grad.reshape(-1, width)[slot_of].reshape(token_count, top_count, width)
    weight = gates.astype(jnp.float32)
    mixed = jnp.sum(weight[:, :, None] * copy_out.astype(jnp.float32), axis=1)
    d_tokens = jnp.sum(weight[:, :, None] * copy_grad.astype(jnp.float32), axis=1)
    d_gates = jnp.einsum("tkd,td->tk", copy_out, cotangent, preferred_element_type=jnp.float32)
    return (mixed.astype(jnp.bfloat16), d_tokens.astype(jnp.bfloat16), d_gates)


def ring_order(count):
    return list(range(0, count, 2)) + list(range(count - 1, 0, -2))


def ring_shift(array, count, step):
    order = ring_order(count)
    pairs = [(order[i], order[(i + step) % count]) for i in range(count)]
    return lax.ppermute(array, "ep", pairs)


def ring_gather(shard, count, far_step, behind={}):
    held = {0: shard}
    latest = {}
    for step in (far_step, -far_step):
        hops = count // 2 if step == far_step else (count - 1) // 2
        moving = held_back(shard, behind[step]) if step in behind else shard
        for hop in range(1, hops + 1):
            moving = ring_shift(moving, count, step)
            held[(-step * hop) % count] = moving
        latest[step] = (moving,)
    return [held[place] for place in range(count)], latest


def after(array, *others):
    for other in others:
        array = array + other[(slice(0, 1),) * other.ndim].reshape((1,) * array.ndim).astype(array.dtype) * 0
    return array


def held_back(array, others):
    def kernel(*refs):
        pass

    return pl.pallas_call(
        kernel,
        out_shape=jax.ShapeDtypeStruct(array.shape, array.dtype),
        in_specs=[pl.BlockSpec(memory_space=pl.ANY) for _ in range(1 + len(others))],
        out_specs=pl.BlockSpec(memory_space=pl.ANY),
        input_output_aliases={0: 0},
    )(array, *others)


def ring_reduce(share_of, count, far_step, behind={}):
    arrived = {}
    for step in (far_step, -far_step):
        hops = count // 2 if step == far_step else (count - 1) // 2
        moving = None
        steps = []
        for hop in range(hops, 0, -1):
            waits = behind.get((step, hops - hop), ())
            share = share_of((step * hop) % count, moving, waits)
            moving = ring_shift(share, count, step)
            steps.append(moving)
        arrived[step] = steps
    total = share_of(0, arrived[far_step][-1], (arrived[-far_step][-1],), True)
    return total, arrived


VMEM_LIMIT = 48 * 1024 * 1024
LAST = (((1,), (1,)), ((), ()))


def cut(size, most):
    return max(w for w in range(128, most + 1, 128) if size % w == 0)


def call_kernel(kernel, operands, kinds, outs, scratch, flops, behind=()):
    spaces = {"any": pl.ANY, "vmem": pltpu.VMEM, "smem": pltpu.SMEM}
    count = len(operands)
    operands = [*operands, *behind]
    kinds = [*kinds, *["any" for _ in behind]]

    def body(*refs):
        kernel(*refs[:count], *refs[len(operands) :])

    return pl.pallas_call(
        body,
        out_shape=outs,
        in_specs=[pl.BlockSpec(memory_space=spaces[k]) for k in kinds],
        out_specs=[pl.BlockSpec(memory_space=pltpu.VMEM) for _ in outs],
        scratch_shapes=scratch,
        compiler_params=pltpu.CompilerParams(vmem_limit_bytes=VMEM_LIMIT),
        cost_estimate=pl.CostEstimate(flops=flops, bytes_accessed=1 << 20, transcendentals=0),
    )(*operands)


def pack_rows(parts, packed):
    half = parts[0].shape[0] // 2
    for e in range(2):
        for s, part in enumerate(parts):
            packed[e, s * half : (s + 1) * half, :] = part[e * half : (e + 1) * half, :]


def source_at(distance, chip, count):
    place = jnp.where(chip % 2 == 0, chip // 2, count - (chip + 1) // 2)
    place = (place + distance) % count
    return jnp.where(place < count // 2, 2 * place, 2 * (count - place) - 1)


def run_routing(ids, tables, top_count, capacity):
    count, _, tokens = tables.shape
    f32, bf16 = jnp.float32, jnp.bfloat16

    def kernel(ids_ref, table_ref, pick_ref, spread_ref):
        core, chip = ids_ref[0], ids_ref[1]
        first = lax.broadcasted_iota(jnp.int32, (tokens, tokens), 0)
        second = lax.broadcasted_iota(jnp.int32, (tokens, tokens), 1)
        before = (first <= second).astype(f32).astype(bf16)
        slot = lax.broadcasted_iota(jnp.int32, (capacity, tokens), 0).astype(f32)
        hits, weights = [], []
        for s in range(count):
            table = table_ref[source_at(s, chip, count)]
            for e in range(2):
                expert = jnp.where(core == e, chip, count + chip).astype(f32)
                hit = (table[:top_count] == expert).astype(f32)
                hits.append(jnp.sum(hit, axis=0, keepdims=True))
                weights.append(
                    jnp.sum(hit * table[top_count : 2 * top_count], axis=0, keepdims=True)
                )
        rank = jnp.dot(
            jnp.concatenate(hits, axis=0).astype(bf16), before, preferred_element_type=f32
        )
        for s in range(count):
            for e in range(2):
                i = 2 * s + e
                chosen = jnp.where(slot == rank[i : i + 1] - 1.0, hits[i], 0.0)
                span = slice(e * capacity, (e + 1) * capacity)
                pick_ref[s, span, :] = chosen.astype(bf16)
                spread_ref[s, span, :] = (chosen * weights[i]).astype(bf16)

    shape = jax.ShapeDtypeStruct((count, 2 * capacity, tokens), bf16)
    return call_kernel(kernel, [ids, tables], ["smem", "vmem"], [shape, shape], [], 1 << 20)


def run_hidden(parts, gate_mats, up_mats):
    count, rows, width = len(parts), parts[0].shape[0], parts[0].shape[1]
    units = gate_mats[0].shape[1]
    total = count * rows // 2
    tile = cut(units, 256)
    tiles = units // tile

    def kernel(*refs):
        part_refs, mats = refs[:count], refs[count : count + 4]
        hidden_ref, slope_ref, act_ref, packed, held, sems = refs[count + 4 :]
        copies = {}
        for e in range(2):
            for m in range(2):
                copies[e, m] = pltpu.make_async_copy(
                    mats[2 * m + e], held.at[e, m], sems.at[e, m]
                )
                copies[e, m].start()
        pack_rows(part_refs, packed)
        for e in range(2):
            for m in range(2):
                copies[e, m].wait()
            for n in range(tiles):
                span = slice(n * tile, (n + 1) * tile)
                gate = jnp.dot(packed[e], held[e, 0, :, span], preferred_element_type=jnp.float32)
                up = jnp.dot(packed[e], held[e, 1, :, span], preferred_element_type=jnp.float32)
                sigma = 1.0 / (1.0 + jnp.exp(-gate))
                act = gate * sigma
                hidden_ref[e, :, span] = (act * up).astype(jnp.bfloat16)
                slope_ref[e, :, span] = up * sigma * (1.0 + gate * (1.0 - sigma))
                act_ref[e, :, span] = act

    return call_kernel(
        kernel,
        [*parts, *gate_mats, *up_mats],
        ["vmem"] * count + ["any"] * 4,
        [
            jax.ShapeDtypeStruct((2, total, units), jnp.bfloat16),
            jax.ShapeDtypeStruct((2, total, units), jnp.float32),
            jax.ShapeDtypeStruct((2, total, units), jnp.float32),
        ],
        [
            pltpu.VMEM((2, total, width), jnp.bfloat16),
            pltpu.VMEM((2, 2, width, units), jnp.bfloat16),
            pltpu.SemaphoreType.DMA((2, 2)),
        ],
        8 * total * width * units,
    )


def run_down(hidden, down_mats, count):
    _, total, units = hidden.shape
    width = down_mats[0].shape[1]
    half = total // count
    tile = cut(width, 512)
    tiles = width // tile

    def kernel(hidden_ref, own_ref, other_ref, out_ref, held, sems):
        copies = {}
        for e, mat in enumerate((own_ref, other_ref)):
            copies[e] = pltpu.make_async_copy(mat, held.at[e], sems.at[e])
            copies[e].start()
        for e in range(2):
            copies[e].wait()
            for n in range(tiles):
                columns = held[e, :, n * tile : (n + 1) * tile]
                out = jnp.dot(hidden_ref[e], columns, preferred_element_type=jnp.float32)
                out_ref[:, e * half : (e + 1) * half, n * tile : (n + 1) * tile] = (
                    out.astype(jnp.bfloat16).reshape(count, half, tile)
                )

    return call_kernel(
        kernel,
        [hidden, *down_mats],
        ["vmem", "any", "any"],
        [jax.ShapeDtypeStruct((count, 2 * half, width), jnp.bfloat16)],
        [
            pltpu.VMEM((2, units, width), jnp.bfloat16),
            pltpu.SemaphoreType.DMA((2,)),
        ],
        4 * total * width * units,
    )[0]


def run_d_hidden(ids, parts, outputs, pick, slope, activated, down_mats, behind):
    count, rows, width = len(parts), parts[0].shape[0], parts[0].shape[1]
    half = rows // 2
    _, total, units = slope.shape
    tile = cut(units, 256)
    tiles = units // tile
    tokens = pick.shape[2]

    def kernel(*refs):
        ids_ref, refs = refs[0], refs[1:]
        part_refs = refs[:count]
        out_ref, pick_ref, slope_ref, act_ref, own_ref, other_ref = refs[count : count + 6]
        d_gate_ref, d_up_ref, token_ref, packed, held, sems = refs[count + 6 :]
        copies = {}
        for e, mat in enumerate((own_ref, other_ref)):
            for n in range(tiles):
                copies[e, n] = pltpu.make_async_copy(
                    mat.at[n * tile : (n + 1) * tile, :], held.at[e, n], sems.at[e, n]
                )
                copies[e, n].start()
        pack_rows(part_refs, packed)
        for e in range(2):
            for n in range(tiles):
                span = slice(n * tile, (n + 1) * tile)
                copies[e, n].wait()
                d_hidden = lax.dot_general(
                    packed[e], held[e, n], LAST, preferred_element_type=jnp.float32
                )
                d_gate_ref[e, :, span] = (d_hidden * slope_ref[e, :, span]).astype(jnp.bfloat16)
                d_up_ref[e, :, span] = (d_hidden * act_ref[e, :, span]).astype(jnp.bfloat16)
        for s in range(count):
            inner = jnp.sum(
                part_refs[s][...].astype(jnp.float32) * out_ref[s].astype(jnp.float32),
                axis=1,
                keepdims=True,
            )
            spread = pick_ref[s].astype(jnp.float32) * inner
            sums = [
                jnp.sum(spread[e * half : (e + 1) * half], axis=0, keepdims=True)
                for e in range(2)
            ]
            token_ref[source_at(s, ids_ref[1], count)] = jnp.concatenate(sums, axis=0)

    return call_kernel(
        kernel,
        [ids, *parts, outputs, pick, slope, activated, *down_mats],
        ["smem"] + ["vmem"] * (count + 4) + ["any"] * 2,
        [
            jax.ShapeDtypeStruct((2, total, units), jnp.bfloat16),
            jax.ShapeDtypeStruct((2, total, units), jnp.bfloat16),
            jax.ShapeDtypeStruct((count, 2, tokens), jnp.float32),
        ],
        [
            pltpu.VMEM((2, total, width), jnp.bfloat16),
            pltpu.VMEM((2, tiles, tile, width), jnp.bfloat16),
            pltpu.SemaphoreType.DMA((2, tiles)),
        ],
        4 * total * width * units,
        behind,
    )


def run_d_copy(d_pre_gate, d_pre_up, gate_mats, up_mats, count, behind):
    _, total, units = d_pre_gate.shape
    width = gate_mats[0].shape[0]
    half = total // count
    tile = cut(width, 512)
    tiles = width // tile

    def kernel(d_gate_ref, d_up_ref, *refs):
        mats = refs[:4]
        out_ref, held, sems = refs[4:]
        copies = {}
        for e in range(2):
            for n in range(tiles):
                for m in range(2):
                    copies[e, n, m] = pltpu.make_async_copy(
                        mats[2 * m + e].at[n * tile : (n + 1) * tile, :],
                        held.at[e, n, m],
                        sems.at[e, n, m],
                    )
                    copies[e, n, m].start()
        for e in range(2):
            for n in range(tiles):
                copies[e, n, 0].wait()
                out = lax.dot_general(
                    d_gate_ref[e], held[e, n, 0], LAST, preferred_element_type=jnp.float32
                )
                copies[e, n, 1].wait()
                out = out + lax.dot_general(
                    d_up_ref[e], held[e, n, 1], LAST, preferred_element_type=jnp.float32
                )
                out_ref[:, e * half : (e + 1) * half, n * tile : (n + 1) * tile] = (
                    out.astype(jnp.bfloat16).reshape(count, half, tile)
                )

    return call_kernel(
        kernel,
        [d_pre_gate, d_pre_up, *gate_mats, *up_mats],
        ["vmem", "vmem"] + ["any"] * 4,
        [jax.ShapeDtypeStruct((count, 2 * half, width), jnp.bfloat16)],
        [
            pltpu.VMEM((2, tiles, 2, tile, units), jnp.bfloat16),
            pltpu.SemaphoreType.DMA((2, tiles, 2)),
        ],
        8 * total * width * units,
        behind,
    )[0]


def swap_cores(array):
    return lax.ppermute(array, "grp", [(0, 1), (1, 0)])


def body_ring(tokens, cotangent, routes, gates, w_gate, w_up, w_down):
    token_count = tokens.shape[0]
    width = tokens.shape[1]
    top_count = routes.shape[1]
    chips = lax.axis_size("ep")
    expert_count = lax.axis_size(("grp", "ep"))
    capacity = max(2, 3 * token_count * top_count // (2 * expert_count))
    f32, bf16 = jnp.float32, jnp.bfloat16

    in_shards, in_latest = ring_gather(tokens, chips, 1)
    grad_shards, grad_latest = ring_gather(cotangent, chips, -1, in_latest)
    gate_mats = (w_gate[0], swap_cores(w_gate[0]))
    up_mats = (w_up[0], swap_cores(w_up[0]))
    down_mats = (w_down[0], swap_cores(w_down[0]))

    core = lax.axis_index("grp")
    chip = lax.axis_index("ep")
    ids = jnp.stack([core, chip]).astype(jnp.int32)
    table = jnp.concatenate([routes.astype(f32), gates.astype(f32)], axis=1).T
    table = after(table, in_shards[1], in_shards[-1])
    copies = jnp.broadcast_to(table[None], (chips,) + table.shape)
    tables = lax.all_to_all(copies, "ep", split_axis=0, concat_axis=0, tiled=True)
    pick, spread = run_routing(ids, tables, top_count, capacity)

    def gather_rows(shards):
        return [
            jnp.dot(pick[s], shards[s], preferred_element_type=f32).astype(bf16)
            for s in range(chips)
        ]

    def scatter_rows(blocks):
        def share_of(s, partial, waits=(), add_waits=False):
            total = lax.dot_general(
                spread[s], blocks[s], (((0,), (0,)), ((), ())), preferred_element_type=f32
            )
            if partial is not None:
                total = total + partial.astype(f32)
            if add_waits:
                return (total + waits[0].astype(f32)).astype(bf16)
            return after(total.astype(bf16), *waits)

        return share_of

    rows_in = gather_rows(in_shards)
    hidden, slope, activated = run_hidden(rows_in, gate_mats, up_mats)
    outputs = run_down(hidden, down_mats, chips)
    behind = {(step, 0): grad_latest[step] for step in (1, -1)}
    mixed, mixed_hops = ring_reduce(scatter_rows(outputs), chips, 1, behind)

    rows_grad = gather_rows(grad_shards)
    hop_of = lambda hop: [mixed_hops[step][min(hop, len(mixed_hops[step]) - 1)] for step in (1, -1)]
    d_pre_gate, d_pre_up, per_token = run_d_hidden(
        ids, rows_grad, outputs, pick, slope, activated, down_mats, hop_of(0)
    )
    d_copies = run_d_copy(d_pre_gate, d_pre_up, gate_mats, up_mats, chips, hop_of(1))

    returned = lax.all_to_all(per_token, "ep", split_axis=0, concat_axis=0, tiled=True)
    behind = {(step, 0): (mixed_hops[step][-1],) for step in (1, -1)}
    d_tokens, _ = ring_reduce(scatter_rows(d_copies), chips, -1, behind)
    chip_ids = jnp.arange(chips, dtype=jnp.int32)
    served = jnp.stack([core * chips + chip_ids, (1 - core) * chips + chip_ids], axis=1)
    chosen = routes.T[None, None] == served[:, :, None, None]
    d_gates = jnp.sum(jnp.where(chosen, returned[:, :, None, :], 0.0), axis=(0, 1)).T
    return (mixed, d_tokens, d_gates)


def solution(mesh):
    plan = body_ring if mesh.shape["ep"] <= 8 and mesh.shape["grp"] == 2 else body_exchange
    return jax.shard_map(
        plan,
        mesh=mesh,
        in_specs=(
            P(("rep", "grp", "ep"), None),
            P(("rep", "grp", "ep"), None),
            P(("rep", "grp", "ep"), None),
            P(("rep", "grp", "ep"), None),
            P(("grp", "ep"), None, None),
            P(("grp", "ep"), None, None),
            P(("grp", "ep"), None, None),
        ),
        out_specs=(
            P(("rep", "grp", "ep"), None),
            P(("rep", "grp", "ep"), None),
            P(("rep", "grp", "ep"), None),
        ),
        check_vma=False,
    )
```

```python
import jax
import jax.numpy as jnp
from jax import lax
from jax.experimental import pallas as pl
from jax.experimental.pallas import tpu as pltpu
from jax.sharding import PartitionSpec as P


def expert_pass(rows_in, rows_grad, gate_mat, up_mat, down_mat):
    pre_gate = jnp.dot(rows_in, gate_mat, preferred_element_type=jnp.float32)
    pre_up = jnp.dot(rows_in, up_mat, preferred_element_type=jnp.float32)
    activated = jax.nn.silu(pre_gate)
    hidden = (activated * pre_up).astype(jnp.bfloat16)
    outputs = jnp.dot(hidden, down_mat, preferred_element_type=jnp.float32).astype(jnp.bfloat16)
    d_hidden = lax.dot_general(
        rows_grad, down_mat, (((1,), (1,)), ((), ())), preferred_element_type=jnp.float32
    )
    sigma = jax.nn.sigmoid(pre_gate)
    d_pre_gate = (d_hidden * pre_up * sigma * (1.0 + pre_gate * (1.0 - sigma))).astype(jnp.bfloat16)
    d_pre_up = (d_hidden * activated).astype(jnp.bfloat16)
    both_pre = jnp.concatenate([d_pre_gate, d_pre_up], axis=1)
    both_mats = jnp.concatenate([gate_mat, up_mat], axis=1)
    d_copy = lax.dot_general(
        both_pre, both_mats, (((1,), (1,)), ((), ())), preferred_element_type=jnp.float32
    )
    return (outputs, d_copy.astype(jnp.bfloat16))


def run_items(pieces, gate_mat, up_mat, down_mat):
    rows_in, rows_grad = pieces
    lead_shape = rows_in.shape[:2]
    width = rows_in.shape[2]
    outputs, d_copy = expert_pass(
        rows_in.reshape(-1, width), rows_grad.reshape(-1, width), gate_mat, up_mat, down_mat
    )
    return (outputs.reshape(lead_shape + (width,)), d_copy.reshape(lead_shape + (width,)))


def ranks_of(chosen_hot):
    running = jnp.cumsum(chosen_hot, axis=-2)
    return jnp.sum(chosen_hot * running, axis=-1) - 1


def body_exchange(tokens, cotangent, routes, gates, w_gate, w_up, w_down):
    token_count = tokens.shape[0]
    width = tokens.shape[1]
    top_count = routes.shape[1]
    copy_count = token_count * top_count
    gate_mat = w_gate[0]
    up_mat = w_up[0]
    down_mat = w_down[0]
    expert_count = lax.axis_size(("grp", "ep"))
    capacity = max(2, 3 * token_count * top_count // (2 * expert_count))
    flat_experts = routes.reshape(-1)
    chosen_hot = (
        flat_experts[:, None] == jnp.arange(expert_count, dtype=jnp.int32)[None, :]
    ).astype(jnp.int32)
    slot_of = flat_experts * capacity + ranks_of(chosen_hot)
    token_of = jnp.arange(copy_count, dtype=jnp.int32) // top_count
    slot_token = jnp.zeros((expert_count * capacity,), jnp.int32).at[slot_of].set(token_of)
    slot_live = jnp.zeros((expert_count * capacity,), jnp.bool_).at[slot_of].set(True)
    send_in = jnp.where(
        slot_live[:, None], tokens[slot_token], jnp.zeros((), tokens.dtype)
    ).reshape(expert_count, capacity, width)
    send_grad = jnp.where(
        slot_live[:, None], cotangent[slot_token], jnp.zeros((), cotangent.dtype)
    ).reshape(expert_count, capacity, width)
    outputs, d_copy = run_items(
        (
            lax.all_to_all(send_in, ("grp", "ep"), split_axis=0, concat_axis=0, tiled=True),
            lax.all_to_all(send_grad, ("grp", "ep"), split_axis=0, concat_axis=0, tiled=True),
        ),
        gate_mat,
        up_mat,
        down_mat,
    )
    back_out = lax.all_to_all(outputs, ("grp", "ep"), split_axis=0, concat_axis=0, tiled=True)
    back_grad = lax.all_to_all(d_copy, ("grp", "ep"), split_axis=0, concat_axis=0, tiled=True)
    copy_out = back_out.reshape(-1, width)[slot_of].reshape(token_count, top_count, width)
    copy_grad = back_grad.reshape(-1, width)[slot_of].reshape(token_count, top_count, width)
    weight = gates.astype(jnp.float32)
    mixed = jnp.sum(weight[:, :, None] * copy_out.astype(jnp.float32), axis=1)
    d_tokens = jnp.sum(weight[:, :, None] * copy_grad.astype(jnp.float32), axis=1)
    d_gates = jnp.einsum("tkd,td->tk", copy_out, cotangent, preferred_element_type=jnp.float32)
    return (mixed.astype(jnp.bfloat16), d_tokens.astype(jnp.bfloat16), d_gates)


def ring_order(count):
    return list(range(0, count, 2)) + list(range(count - 1, 0, -2))


def ring_shift(array, count, step):
    order = ring_order(count)
    pairs = [(order[i], order[(i + step) % count]) for i in range(count)]
    return lax.ppermute(array, "ep", pairs)


def ring_gather(shard, count, far_step, behind={}):
    held = {0: shard}
    arrivals = {}
    for step in (far_step, -far_step):
        hops = count // 2 if step == far_step else (count - 1) // 2
        moving = shard
        arrivals[step] = []
        for hop in range(1, hops + 1):
            if (step, hop) in behind:
                moving = held_back(moving, behind[step, hop])
                if hop > 1:
                    held[(-step * (hop - 1)) % count] = moving
            moving = ring_shift(moving, count, step)
            held[(-step * hop) % count] = moving
            arrivals[step].append(moving)
    return [held[place] for place in range(count)], arrivals


def after(array, *others):
    for other in others:
        array = array + other[(slice(0, 1),) * other.ndim].reshape((1,) * array.ndim).astype(array.dtype) * 0
    return array


def held_back(array, others):
    def kernel(*refs):
        pass

    return pl.pallas_call(
        kernel,
        out_shape=jax.ShapeDtypeStruct(array.shape, array.dtype),
        in_specs=[pl.BlockSpec(memory_space=pl.ANY) for _ in range(1 + len(others))],
        out_specs=pl.BlockSpec(memory_space=pl.ANY),
        input_output_aliases={0: 0},
    )(array, *others)


def ring_reduce(share_of, count, far_step, behind={}):
    arrived = {}
    for step in (far_step, -far_step):
        hops = count // 2 if step == far_step else (count - 1) // 2
        moving = None
        steps = []
        for hop in range(hops, 0, -1):
            waits = behind.get((step, hops - hop), ())
            share = share_of((step * hop) % count, moving, waits)
            moving = ring_shift(share, count, step)
            steps.append(moving)
        arrived[step] = steps
    total = share_of(0, arrived[far_step][-1], (arrived[-far_step][-1],), True)
    return total, arrived


VMEM_LIMIT = 48 * 1024 * 1024
LAST = (((1,), (1,)), ((), ()))


def cut(size, most):
    return max(w for w in range(128, most + 1, 128) if size % w == 0)


def call_kernel(kernel, operands, kinds, outs, scratch, flops, behind=()):
    spaces = {"any": pl.ANY, "vmem": pltpu.VMEM, "smem": pltpu.SMEM}
    count = len(operands)
    operands = [*operands, *behind]
    kinds = [*kinds, *["any" for _ in behind]]

    def body(*refs):
        kernel(*refs[:count], *refs[len(operands) :])

    return pl.pallas_call(
        body,
        out_shape=outs,
        in_specs=[pl.BlockSpec(memory_space=spaces[k]) for k in kinds],
        out_specs=[pl.BlockSpec(memory_space=pltpu.VMEM) for _ in outs],
        scratch_shapes=scratch,
        compiler_params=pltpu.CompilerParams(vmem_limit_bytes=VMEM_LIMIT),
        cost_estimate=pl.CostEstimate(flops=flops, bytes_accessed=1 << 20, transcendentals=0),
    )(*operands)


def pack_rows(parts, packed):
    half = parts[0].shape[0] // 2
    for e in range(2):
        for s, part in enumerate(parts):
            packed[e, s * half : (s + 1) * half, :] = part[e * half : (e + 1) * half, :]


def source_at(distance, chip, count):
    place = jnp.where(chip % 2 == 0, chip // 2, count - (chip + 1) // 2)
    place = (place + distance) % count
    return jnp.where(place < count // 2, 2 * place, 2 * (count - place) - 1)


def run_routing(ids, tables, top_count, capacity):
    count, _, tokens = tables.shape
    f32, bf16 = jnp.float32, jnp.bfloat16

    def kernel(ids_ref, table_ref, pick_ref, spread_ref):
        core, chip = ids_ref[0], ids_ref[1]
        first = lax.broadcasted_iota(jnp.int32, (tokens, tokens), 0)
        second = lax.broadcasted_iota(jnp.int32, (tokens, tokens), 1)
        before = (first <= second).astype(f32).astype(bf16)
        slot = lax.broadcasted_iota(jnp.int32, (capacity, tokens), 0).astype(f32)
        hits, weights = [], []
        for s in range(count):
            table = table_ref[source_at(s, chip, count)]
            for e in range(2):
                expert = jnp.where(core == e, chip, count + chip).astype(f32)
                hit = (table[:top_count] == expert).astype(f32)
                hits.append(jnp.sum(hit, axis=0, keepdims=True))
                weights.append(
                    jnp.sum(hit * table[top_count : 2 * top_count], axis=0, keepdims=True)
                )
        rank = jnp.dot(
            jnp.concatenate(hits, axis=0).astype(bf16), before, preferred_element_type=f32
        )
        for s in range(count):
            for e in range(2):
                i = 2 * s + e
                chosen = jnp.where(slot == rank[i : i + 1] - 1.0, hits[i], 0.0)
                span = slice(e * capacity, (e + 1) * capacity)
                pick_ref[s, span, :] = chosen.astype(bf16)
                spread_ref[s, span, :] = (chosen * weights[i]).astype(bf16)

    shape = jax.ShapeDtypeStruct((count, 2 * capacity, tokens), bf16)
    return call_kernel(kernel, [ids, tables], ["smem", "vmem"], [shape, shape], [], 1 << 20)


def run_hidden(parts, gate_mats, up_mats):
    count, rows, width = len(parts), parts[0].shape[0], parts[0].shape[1]
    units = gate_mats[0].shape[1]
    total = count * rows // 2
    tile = cut(units, 256)
    tiles = units // tile

    def kernel(*refs):
        part_refs, mats = refs[:count], refs[count : count + 4]
        hidden_ref, slope_ref, act_ref, packed, held, sems = refs[count + 4 :]
        copies = {}
        for e in range(2):
            for m in range(2):
                copies[e, m] = pltpu.make_async_copy(
                    mats[2 * m + e], held.at[e, m], sems.at[e, m]
                )
                copies[e, m].start()
        pack_rows(part_refs, packed)
        for e in range(2):
            for m in range(2):
                copies[e, m].wait()
            for n in range(tiles):
                span = slice(n * tile, (n + 1) * tile)
                gate = jnp.dot(packed[e], held[e, 0, :, span], preferred_element_type=jnp.float32)
                up = jnp.dot(packed[e], held[e, 1, :, span], preferred_element_type=jnp.float32)
                sigma = 1.0 / (1.0 + jnp.exp(-gate))
                act = gate * sigma
                hidden_ref[e, :, span] = (act * up).astype(jnp.bfloat16)
                slope_ref[e, :, span] = up * sigma * (1.0 + gate * (1.0 - sigma))
                act_ref[e, :, span] = act

    return call_kernel(
        kernel,
        [*parts, *gate_mats, *up_mats],
        ["vmem"] * count + ["any"] * 4,
        [
            jax.ShapeDtypeStruct((2, total, units), jnp.bfloat16),
            jax.ShapeDtypeStruct((2, total, units), jnp.float32),
            jax.ShapeDtypeStruct((2, total, units), jnp.float32),
        ],
        [
            pltpu.VMEM((2, total, width), jnp.bfloat16),
            pltpu.VMEM((2, 2, width, units), jnp.bfloat16),
            pltpu.SemaphoreType.DMA((2, 2)),
        ],
        8 * total * width * units,
    )


def run_down(hidden, down_mats, count):
    _, total, units = hidden.shape
    width = down_mats[0].shape[1]
    half = total // count
    tile = cut(width, 512)
    tiles = width // tile

    def kernel(hidden_ref, own_ref, other_ref, out_ref, held, sems):
        copies = {}
        for e, mat in enumerate((own_ref, other_ref)):
            copies[e] = pltpu.make_async_copy(mat, held.at[e], sems.at[e])
            copies[e].start()
        for e in range(2):
            copies[e].wait()
            for n in range(tiles):
                columns = held[e, :, n * tile : (n + 1) * tile]
                out = jnp.dot(hidden_ref[e], columns, preferred_element_type=jnp.float32)
                out_ref[:, e * half : (e + 1) * half, n * tile : (n + 1) * tile] = (
                    out.astype(jnp.bfloat16).reshape(count, half, tile)
                )

    return call_kernel(
        kernel,
        [hidden, *down_mats],
        ["vmem", "any", "any"],
        [jax.ShapeDtypeStruct((count, 2 * half, width), jnp.bfloat16)],
        [
            pltpu.VMEM((2, units, width), jnp.bfloat16),
            pltpu.SemaphoreType.DMA((2,)),
        ],
        4 * total * width * units,
    )[0]


def run_d_hidden(ids, parts, outputs, pick, slope, activated, down_mats, behind):
    count, rows, width = len(parts), parts[0].shape[0], parts[0].shape[1]
    half = rows // 2
    _, total, units = slope.shape
    tile = cut(units, 256)
    tiles = units // tile
    tokens = pick.shape[2]

    def kernel(*refs):
        ids_ref, refs = refs[0], refs[1:]
        part_refs = refs[:count]
        out_ref, pick_ref, slope_ref, act_ref, own_ref, other_ref = refs[count : count + 6]
        d_gate_ref, d_up_ref, token_ref, packed, held, sems = refs[count + 6 :]
        copies = {}
        for e, mat in enumerate((own_ref, other_ref)):
            for n in range(tiles):
                copies[e, n] = pltpu.make_async_copy(
                    mat.at[n * tile : (n + 1) * tile, :], held.at[e, n], sems.at[e, n]
                )
                copies[e, n].start()
        pack_rows(part_refs, packed)
        for e in range(2):
            for n in range(tiles):
                span = slice(n * tile, (n + 1) * tile)
                copies[e, n].wait()
                d_hidden = lax.dot_general(
                    packed[e], held[e, n], LAST, preferred_element_type=jnp.float32
                )
                d_gate_ref[e, :, span] = (d_hidden * slope_ref[e, :, span]).astype(jnp.bfloat16)
                d_up_ref[e, :, span] = (d_hidden * act_ref[e, :, span]).astype(jnp.bfloat16)
        for s in range(count):
            inner = jnp.sum(
                part_refs[s][...].astype(jnp.float32) * out_ref[s].astype(jnp.float32),
                axis=1,
                keepdims=True,
            )
            spread = pick_ref[s].astype(jnp.float32) * inner
            sums = [
                jnp.sum(spread[e * half : (e + 1) * half], axis=0, keepdims=True)
                for e in range(2)
            ]
            token_ref[source_at(s, ids_ref[1], count)] = jnp.concatenate(sums, axis=0)

    return call_kernel(
        kernel,
        [ids, *parts, outputs, pick, slope, activated, *down_mats],
        ["smem"] + ["vmem"] * (count + 4) + ["any"] * 2,
        [
            jax.ShapeDtypeStruct((2, total, units), jnp.bfloat16),
            jax.ShapeDtypeStruct((2, total, units), jnp.bfloat16),
            jax.ShapeDtypeStruct((count, 2, tokens), jnp.float32),
        ],
        [
            pltpu.VMEM((2, total, width), jnp.bfloat16),
            pltpu.VMEM((2, tiles, tile, width), jnp.bfloat16),
            pltpu.SemaphoreType.DMA((2, tiles)),
        ],
        4 * total * width * units,
        behind,
    )


def run_d_copy(d_pre_gate, d_pre_up, gate_mats, up_mats, count, behind):
    _, total, units = d_pre_gate.shape
    width = gate_mats[0].shape[0]
    half = total // count
    tile = cut(width, 512)
    tiles = width // tile

    def kernel(d_gate_ref, d_up_ref, *refs):
        mats = refs[:4]
        out_ref, held, sems = refs[4:]
        copies = {}
        for e in range(2):
            for n in range(tiles):
                for m in range(2):
                    copies[e, n, m] = pltpu.make_async_copy(
                        mats[2 * m + e].at[n * tile : (n + 1) * tile, :],
                        held.at[e, n, m],
                        sems.at[e, n, m],
                    )
                    copies[e, n, m].start()
        for e in range(2):
            for n in range(tiles):
                copies[e, n, 0].wait()
                out = lax.dot_general(
                    d_gate_ref[e], held[e, n, 0], LAST, preferred_element_type=jnp.float32
                )
                copies[e, n, 1].wait()
                out = out + lax.dot_general(
                    d_up_ref[e], held[e, n, 1], LAST, preferred_element_type=jnp.float32
                )
                out_ref[:, e * half : (e + 1) * half, n * tile : (n + 1) * tile] = (
                    out.astype(jnp.bfloat16).reshape(count, half, tile)
                )

    return call_kernel(
        kernel,
        [d_pre_gate, d_pre_up, *gate_mats, *up_mats],
        ["vmem", "vmem"] + ["any"] * 4,
        [jax.ShapeDtypeStruct((count, 2 * half, width), jnp.bfloat16)],
        [
            pltpu.VMEM((2, tiles, 2, tile, units), jnp.bfloat16),
            pltpu.SemaphoreType.DMA((2, tiles, 2)),
        ],
        8 * total * width * units,
        behind,
    )[0]


def swap_cores(array):
    return lax.ppermute(array, "grp", [(0, 1), (1, 0)])


def body_ring(tokens, cotangent, routes, gates, w_gate, w_up, w_down):
    token_count = tokens.shape[0]
    width = tokens.shape[1]
    top_count = routes.shape[1]
    chips = lax.axis_size("ep")
    expert_count = lax.axis_size(("grp", "ep"))
    capacity = max(2, 3 * token_count * top_count // (2 * expert_count))
    f32, bf16 = jnp.float32, jnp.bfloat16

    core = lax.axis_index("grp")
    chip = lax.axis_index("ep")
    ids = jnp.stack([core, chip]).astype(jnp.int32)
    table = jnp.concatenate([routes.astype(f32), gates.astype(f32)], axis=1).T
    copies = jnp.broadcast_to(table[None], (chips,) + table.shape)
    tables = lax.all_to_all(copies, "ep", split_axis=0, concat_axis=0, tiled=True)
    pick, spread = run_routing(ids, tables, top_count, capacity)

    behind = {(step, 2): (tables,) for step in (1, -1)}
    in_shards, in_hops = ring_gather(tokens, chips, 1, behind)
    behind = {(step, 1): (in_hops[step][0],) for step in (1, -1)}
    grad_shards, _ = ring_gather(cotangent, chips, -1, behind)
    gate_mats = (w_gate[0], swap_cores(w_gate[0]))
    up_mats = (w_up[0], swap_cores(w_up[0]))
    down_mats = (w_down[0], swap_cores(w_down[0]))

    def gather_rows(shards):
        return [
            jnp.dot(pick[s], shards[s], preferred_element_type=f32).astype(bf16)
            for s in range(chips)
        ]

    def scatter_rows(blocks):
        def share_of(s, partial, waits=(), add_waits=False):
            total = lax.dot_general(
                spread[s], blocks[s], (((0,), (0,)), ((), ())), preferred_element_type=f32
            )
            if partial is not None:
                total = total + partial.astype(f32)
            if add_waits:
                return (total + waits[0].astype(f32)).astype(bf16)
            return after(total.astype(bf16), *waits)

        return share_of

    rows_in = gather_rows(in_shards)
    hidden, slope, activated = run_hidden(rows_in, gate_mats, up_mats)
    outputs = run_down(hidden, down_mats, chips)
    rows_grad = gather_rows(grad_shards)
    d_pre_gate, d_pre_up, per_token = run_d_hidden(
        ids, rows_grad, outputs, pick, slope, activated, down_mats, ()
    )
    behind = {(step, 1): (per_token,) for step in (1, -1)}
    mixed, mixed_hops = ring_reduce(scatter_rows(outputs), chips, 1, behind)
    d_copies = run_d_copy(
        d_pre_gate, d_pre_up, gate_mats, up_mats, chips, [mixed_hops[step][0] for step in (1, -1)]
    )

    returned = lax.all_to_all(per_token, "ep", split_axis=0, concat_axis=0, tiled=True)
    behind = {
        (step, hop): (mixed_hops[step][hop + 1],)
        for step in (1, -1)
        for hop in range(len(mixed_hops[step]) - 1)
    }
    d_tokens, _ = ring_reduce(scatter_rows(d_copies), chips, -1, behind)
    chip_ids = jnp.arange(chips, dtype=jnp.int32)
    served = jnp.stack([core * chips + chip_ids, (1 - core) * chips + chip_ids], axis=1)
    chosen = routes.T[None, None] == served[:, :, None, None]
    d_gates = jnp.sum(jnp.where(chosen, returned[:, :, None, :], 0.0), axis=(0, 1)).T
    return (mixed, d_tokens, d_gates)


def solution(mesh):
    plan = body_ring if mesh.shape["ep"] <= 8 and mesh.shape["grp"] == 2 else body_exchange
    return jax.shard_map(
        plan,
        mesh=mesh,
        in_specs=(
            P(("rep", "grp", "ep"), None),
            P(("rep", "grp", "ep"), None),
            P(("rep", "grp", "ep"), None),
            P(("rep", "grp", "ep"), None),
            P(("grp", "ep"), None, None),
            P(("grp", "ep"), None, None),
            P(("grp", "ep"), None, None),
        ),
        out_specs=(
            P(("rep", "grp", "ep"), None),
            P(("rep", "grp", "ep"), None),
            P(("rep", "grp", "ep"), None),
        ),
        check_vma=False,
    )
```

```python
import jax
import jax.numpy as jnp
from jax import lax
from jax.experimental import pallas as pl
from jax.experimental.pallas import tpu as pltpu
from jax.sharding import PartitionSpec as P


def expert_pass(rows_in, rows_grad, gate_mat, up_mat, down_mat):
    pre_gate = jnp.dot(rows_in, gate_mat, preferred_element_type=jnp.float32)
    pre_up = jnp.dot(rows_in, up_mat, preferred_element_type=jnp.float32)
    activated = jax.nn.silu(pre_gate)
    hidden = (activated * pre_up).astype(jnp.bfloat16)
    outputs = jnp.dot(hidden, down_mat, preferred_element_type=jnp.float32).astype(jnp.bfloat16)
    d_hidden = lax.dot_general(
        rows_grad, down_mat, (((1,), (1,)), ((), ())), preferred_element_type=jnp.float32
    )
    sigma = jax.nn.sigmoid(pre_gate)
    d_pre_gate = (d_hidden * pre_up * sigma * (1.0 + pre_gate * (1.0 - sigma))).astype(jnp.bfloat16)
    d_pre_up = (d_hidden * activated).astype(jnp.bfloat16)
    both_pre = jnp.concatenate([d_pre_gate, d_pre_up], axis=1)
    both_mats = jnp.concatenate([gate_mat, up_mat], axis=1)
    d_copy = lax.dot_general(
        both_pre, both_mats, (((1,), (1,)), ((), ())), preferred_element_type=jnp.float32
    )
    return (outputs, d_copy.astype(jnp.bfloat16))


def run_items(pieces, gate_mat, up_mat, down_mat):
    rows_in, rows_grad = pieces
    lead_shape = rows_in.shape[:2]
    width = rows_in.shape[2]
    outputs, d_copy = expert_pass(
        rows_in.reshape(-1, width), rows_grad.reshape(-1, width), gate_mat, up_mat, down_mat
    )
    return (outputs.reshape(lead_shape + (width,)), d_copy.reshape(lead_shape + (width,)))


def ranks_of(chosen_hot):
    running = jnp.cumsum(chosen_hot, axis=-2)
    return jnp.sum(chosen_hot * running, axis=-1) - 1


def body_exchange(tokens, cotangent, routes, gates, w_gate, w_up, w_down):
    token_count = tokens.shape[0]
    width = tokens.shape[1]
    top_count = routes.shape[1]
    copy_count = token_count * top_count
    gate_mat = w_gate[0]
    up_mat = w_up[0]
    down_mat = w_down[0]
    expert_count = lax.axis_size(("grp", "ep"))
    capacity = max(2, 3 * token_count * top_count // (2 * expert_count))
    flat_experts = routes.reshape(-1)
    chosen_hot = (
        flat_experts[:, None] == jnp.arange(expert_count, dtype=jnp.int32)[None, :]
    ).astype(jnp.int32)
    slot_of = flat_experts * capacity + ranks_of(chosen_hot)
    token_of = jnp.arange(copy_count, dtype=jnp.int32) // top_count
    slot_token = jnp.zeros((expert_count * capacity,), jnp.int32).at[slot_of].set(token_of)
    slot_live = jnp.zeros((expert_count * capacity,), jnp.bool_).at[slot_of].set(True)
    send_in = jnp.where(
        slot_live[:, None], tokens[slot_token], jnp.zeros((), tokens.dtype)
    ).reshape(expert_count, capacity, width)
    send_grad = jnp.where(
        slot_live[:, None], cotangent[slot_token], jnp.zeros((), cotangent.dtype)
    ).reshape(expert_count, capacity, width)
    outputs, d_copy = run_items(
        (
            lax.all_to_all(send_in, ("grp", "ep"), split_axis=0, concat_axis=0, tiled=True),
            lax.all_to_all(send_grad, ("grp", "ep"), split_axis=0, concat_axis=0, tiled=True),
        ),
        gate_mat,
        up_mat,
        down_mat,
    )
    back_out = lax.all_to_all(outputs, ("grp", "ep"), split_axis=0, concat_axis=0, tiled=True)
    back_grad = lax.all_to_all(d_copy, ("grp", "ep"), split_axis=0, concat_axis=0, tiled=True)
    copy_out = back_out.reshape(-1, width)[slot_of].reshape(token_count, top_count, width)
    copy_grad = back_grad.reshape(-1, width)[slot_of].reshape(token_count, top_count, width)
    weight = gates.astype(jnp.float32)
    mixed = jnp.sum(weight[:, :, None] * copy_out.astype(jnp.float32), axis=1)
    d_tokens = jnp.sum(weight[:, :, None] * copy_grad.astype(jnp.float32), axis=1)
    d_gates = jnp.einsum("tkd,td->tk", copy_out, cotangent, preferred_element_type=jnp.float32)
    return (mixed.astype(jnp.bfloat16), d_tokens.astype(jnp.bfloat16), d_gates)


def ring_order(count):
    return list(range(0, count, 2)) + list(range(count - 1, 0, -2))


def ring_shift(array, count, step):
    order = ring_order(count)
    pairs = [(order[i], order[(i + step) % count]) for i in range(count)]
    return lax.ppermute(array, "ep", pairs)


def ring_gather(shard, count, far_step, behind={}):
    held = {0: shard}
    arrivals = {}
    for step in (far_step, -far_step):
        hops = count // 2 if step == far_step else (count - 1) // 2
        moving = shard
        arrivals[step] = []
        for hop in range(1, hops + 1):
            if (step, hop) in behind:
                moving = held_back(moving, behind[step, hop])
                if hop > 1:
                    held[(-step * (hop - 1)) % count] = moving
            moving = ring_shift(moving, count, step)
            held[(-step * hop) % count] = moving
            arrivals[step].append(moving)
    return [held[place] for place in range(count)], arrivals


def held_back(array, others):
    def kernel(*refs):
        pass

    return pl.pallas_call(
        kernel,
        out_shape=jax.ShapeDtypeStruct(array.shape, array.dtype),
        in_specs=[pl.BlockSpec(memory_space=pl.ANY) for _ in range(1 + len(others))],
        out_specs=pl.BlockSpec(memory_space=pl.ANY),
        input_output_aliases={0: 0},
    )(array, *others)


def copied(array, others):
    def kernel(*refs):
        copy = pltpu.make_async_copy(refs[0], refs[-2], refs[-1])
        copy.start()
        copy.wait()

    return pl.pallas_call(
        kernel,
        out_shape=jax.ShapeDtypeStruct(array.shape, array.dtype),
        in_specs=[pl.BlockSpec(memory_space=pl.ANY) for _ in range(1 + len(others))],
        out_specs=pl.BlockSpec(memory_space=pl.ANY),
        scratch_shapes=[pltpu.SemaphoreType.DMA],
    )(array, *others)


def ring_reduce(share_of, count, far_step, behind={}):
    arrived = {}
    for step in (far_step, -far_step):
        hops = count // 2 if step == far_step else (count - 1) // 2
        moving = None
        steps = []
        for hop in range(hops, 0, -1):
            waits = behind.get((step, hops - hop), ())
            share = share_of((step * hop) % count, moving, waits)
            moving = ring_shift(share, count, step)
            steps.append(moving)
        arrived[step] = steps
    total = share_of(0, arrived[far_step][-1], (arrived[-far_step][-1],), True)
    return total, arrived


VMEM_LIMIT = 48 * 1024 * 1024
LAST = (((1,), (1,)), ((), ()))


def cut(size, most):
    return max(w for w in range(128, most + 1, 128) if size % w == 0)


def call_kernel(kernel, operands, kinds, outs, scratch, flops, behind=()):
    spaces = {"any": pl.ANY, "vmem": pltpu.VMEM, "smem": pltpu.SMEM}
    count = len(operands)
    operands = [*operands, *behind]
    kinds = [*kinds, *["any" for _ in behind]]

    def body(*refs):
        kernel(*refs[:count], *refs[len(operands) :])

    return pl.pallas_call(
        body,
        out_shape=outs,
        in_specs=[pl.BlockSpec(memory_space=spaces[k]) for k in kinds],
        out_specs=[pl.BlockSpec(memory_space=pltpu.VMEM) for _ in outs],
        scratch_shapes=scratch,
        compiler_params=pltpu.CompilerParams(vmem_limit_bytes=VMEM_LIMIT),
        cost_estimate=pl.CostEstimate(flops=flops, bytes_accessed=1 << 20, transcendentals=0),
    )(*operands)


def pack_rows(parts, packed):
    half = parts[0].shape[0] // 2
    for e in range(2):
        for s, part in enumerate(parts):
            packed[e, s * half : (s + 1) * half, :] = part[e * half : (e + 1) * half, :]


def source_at(distance, chip, count):
    place = jnp.where(chip % 2 == 0, chip // 2, count - (chip + 1) // 2)
    place = (place + distance) % count
    return jnp.where(place < count // 2, 2 * place, 2 * (count - place) - 1)


def run_routing(ids, tables, top_count, capacity):
    count, _, tokens = tables.shape
    f32, bf16 = jnp.float32, jnp.bfloat16

    def kernel(ids_ref, table_ref, pick_ref, spread_ref):
        core, chip = ids_ref[0], ids_ref[1]
        first = lax.broadcasted_iota(jnp.int32, (tokens, tokens), 0)
        second = lax.broadcasted_iota(jnp.int32, (tokens, tokens), 1)
        before = (first <= second).astype(f32).astype(bf16)
        slot = lax.broadcasted_iota(jnp.int32, (capacity, tokens), 0).astype(f32)
        hits, weights = [], []
        for s in range(count):
            table = table_ref[source_at(s, chip, count)]
            for e in range(2):
                expert = jnp.where(core == e, chip, count + chip).astype(f32)
                hit = (table[:top_count] == expert).astype(f32)
                hits.append(jnp.sum(hit, axis=0, keepdims=True))
                weights.append(
                    jnp.sum(hit * table[top_count : 2 * top_count], axis=0, keepdims=True)
                )
        rank = jnp.dot(
            jnp.concatenate(hits, axis=0).astype(bf16), before, preferred_element_type=f32
        )
        for s in range(count):
            for e in range(2):
                i = 2 * s + e
                chosen = jnp.where(slot == rank[i : i + 1] - 1.0, hits[i], 0.0)
                span = slice(e * capacity, (e + 1) * capacity)
                pick_ref[s, span, :] = chosen.astype(bf16)
                spread_ref[s, span, :] = (chosen * weights[i]).astype(bf16)

    shape = jax.ShapeDtypeStruct((count, 2 * capacity, tokens), bf16)
    return call_kernel(kernel, [ids, tables], ["smem", "vmem"], [shape, shape], [], 1 << 20)


def run_hidden(parts, gate_mats, up_mats):
    count, rows, width = len(parts), parts[0].shape[0], parts[0].shape[1]
    units = gate_mats[0].shape[1]
    total = count * rows // 2
    tile = cut(units, 256)
    tiles = units // tile

    def kernel(*refs):
        part_refs, mats = refs[:count], refs[count : count + 4]
        hidden_ref, slope_ref, act_ref, packed, held, sems = refs[count + 4 :]
        copies = {}
        for e in range(2):
            for m in range(2):
                copies[e, m] = pltpu.make_async_copy(
                    mats[2 * m + e], held.at[e, m], sems.at[e, m]
                )
                copies[e, m].start()
        pack_rows(part_refs, packed)
        for e in range(2):
            for m in range(2):
                copies[e, m].wait()
            for n in range(tiles):
                span = slice(n * tile, (n + 1) * tile)
                gate = jnp.dot(packed[e], held[e, 0, :, span], preferred_element_type=jnp.float32)
                up = jnp.dot(packed[e], held[e, 1, :, span], preferred_element_type=jnp.float32)
                sigma = 1.0 / (1.0 + jnp.exp(-gate))
                act = gate * sigma
                hidden_ref[e, :, span] = (act * up).astype(jnp.bfloat16)
                slope_ref[e, :, span] = up * sigma * (1.0 + gate * (1.0 - sigma))
                act_ref[e, :, span] = act

    return call_kernel(
        kernel,
        [*parts, *gate_mats, *up_mats],
        ["vmem"] * count + ["any"] * 4,
        [
            jax.ShapeDtypeStruct((2, total, units), jnp.bfloat16),
            jax.ShapeDtypeStruct((2, total, units), jnp.float32),
            jax.ShapeDtypeStruct((2, total, units), jnp.float32),
        ],
        [
            pltpu.VMEM((2, total, width), jnp.bfloat16),
            pltpu.VMEM((2, 2, width, units), jnp.bfloat16),
            pltpu.SemaphoreType.DMA((2, 2)),
        ],
        8 * total * width * units,
    )


def run_down(hidden, down_mats, count):
    _, total, units = hidden.shape
    width = down_mats[0].shape[1]
    half = total // count
    tile = cut(width, 512)
    tiles = width // tile

    def kernel(hidden_ref, own_ref, other_ref, out_ref, held, sems):
        copies = {}
        for e, mat in enumerate((own_ref, other_ref)):
            copies[e] = pltpu.make_async_copy(mat, held.at[e], sems.at[e])
            copies[e].start()
        for e in range(2):
            copies[e].wait()
            for n in range(tiles):
                columns = held[e, :, n * tile : (n + 1) * tile]
                out = jnp.dot(hidden_ref[e], columns, preferred_element_type=jnp.float32)
                out_ref[:, e * half : (e + 1) * half, n * tile : (n + 1) * tile] = (
                    out.astype(jnp.bfloat16).reshape(count, half, tile)
                )

    return call_kernel(
        kernel,
        [hidden, *down_mats],
        ["vmem", "any", "any"],
        [jax.ShapeDtypeStruct((count, 2 * half, width), jnp.bfloat16)],
        [
            pltpu.VMEM((2, units, width), jnp.bfloat16),
            pltpu.SemaphoreType.DMA((2,)),
        ],
        4 * total * width * units,
    )[0]


def run_d_hidden(ids, parts, outputs, pick, slope, activated, down_mats, behind):
    count, rows, width = len(parts), parts[0].shape[0], parts[0].shape[1]
    half = rows // 2
    _, total, units = slope.shape
    tile = cut(units, 256)
    tiles = units // tile
    tokens = pick.shape[2]

    def kernel(*refs):
        ids_ref, refs = refs[0], refs[1:]
        part_refs = refs[:count]
        out_ref, pick_ref, slope_ref, act_ref, own_ref, other_ref = refs[count : count + 6]
        d_gate_ref, d_up_ref, token_ref, packed, held, sems = refs[count + 6 :]
        copies = {}
        for e, mat in enumerate((own_ref, other_ref)):
            for n in range(tiles):
                copies[e, n] = pltpu.make_async_copy(
                    mat.at[n * tile : (n + 1) * tile, :], held.at[e, n], sems.at[e, n]
                )
                copies[e, n].start()
        pack_rows(part_refs, packed)
        for e in range(2):
            for n in range(tiles):
                span = slice(n * tile, (n + 1) * tile)
                copies[e, n].wait()
                d_hidden = lax.dot_general(
                    packed[e], held[e, n], LAST, preferred_element_type=jnp.float32
                )
                d_gate_ref[e, :, span] = (d_hidden * slope_ref[e, :, span]).astype(jnp.bfloat16)
                d_up_ref[e, :, span] = (d_hidden * act_ref[e, :, span]).astype(jnp.bfloat16)
        for s in range(count):
            inner = jnp.sum(
                part_refs[s][...].astype(jnp.float32) * out_ref[s].astype(jnp.float32),
                axis=1,
                keepdims=True,
            )
            spread = pick_ref[s].astype(jnp.float32) * inner
            sums = [
                jnp.sum(spread[e * half : (e + 1) * half], axis=0, keepdims=True)
                for e in range(2)
            ]
            token_ref[source_at(s, ids_ref[1], count)] = jnp.concatenate(sums, axis=0)

    return call_kernel(
        kernel,
        [ids, *parts, outputs, pick, slope, activated, *down_mats],
        ["smem"] + ["vmem"] * (count + 4) + ["any"] * 2,
        [
            jax.ShapeDtypeStruct((2, total, units), jnp.bfloat16),
            jax.ShapeDtypeStruct((2, total, units), jnp.bfloat16),
            jax.ShapeDtypeStruct((count, 2, tokens), jnp.float32),
        ],
        [
            pltpu.VMEM((2, total, width), jnp.bfloat16),
            pltpu.VMEM((2, tiles, tile, width), jnp.bfloat16),
            pltpu.SemaphoreType.DMA((2, tiles)),
        ],
        4 * total * width * units,
        behind,
    )


def run_d_copy(d_pre_gate, d_pre_up, gate_mats, up_mats, count, behind):
    _, total, units = d_pre_gate.shape
    width = gate_mats[0].shape[0]
    half = total // count
    tile = cut(width, 512)
    tiles = width // tile

    def kernel(d_gate_ref, d_up_ref, *refs):
        mats = refs[:4]
        out_ref, held, sems = refs[4:]
        copies = {}
        for e in range(2):
            for n in range(tiles):
                for m in range(2):
                    copies[e, n, m] = pltpu.make_async_copy(
                        mats[2 * m + e].at[n * tile : (n + 1) * tile, :],
                        held.at[e, n, m],
                        sems.at[e, n, m],
                    )
                    copies[e, n, m].start()
        for e in range(2):
            for n in range(tiles):
                copies[e, n, 0].wait()
                out = lax.dot_general(
                    d_gate_ref[e], held[e, n, 0], LAST, preferred_element_type=jnp.float32
                )
                copies[e, n, 1].wait()
                out = out + lax.dot_general(
                    d_up_ref[e], held[e, n, 1], LAST, preferred_element_type=jnp.float32
                )
                out_ref[:, e * half : (e + 1) * half, n * tile : (n + 1) * tile] = (
                    out.astype(jnp.bfloat16).reshape(count, half, tile)
                )

    return call_kernel(
        kernel,
        [d_pre_gate, d_pre_up, *gate_mats, *up_mats],
        ["vmem", "vmem"] + ["any"] * 4,
        [jax.ShapeDtypeStruct((count, 2 * half, width), jnp.bfloat16)],
        [
            pltpu.VMEM((2, tiles, 2, tile, units), jnp.bfloat16),
            pltpu.SemaphoreType.DMA((2, tiles, 2)),
        ],
        8 * total * width * units,
        behind,
    )[0]


def swap_cores(array):
    return lax.ppermute(array, "grp", [(0, 1), (1, 0)])


def body_ring(tokens, cotangent, routes, gates, w_gate, w_up, w_down):
    token_count = tokens.shape[0]
    width = tokens.shape[1]
    top_count = routes.shape[1]
    chips = lax.axis_size("ep")
    expert_count = lax.axis_size(("grp", "ep"))
    capacity = max(2, 3 * token_count * top_count // (2 * expert_count))
    f32, bf16 = jnp.float32, jnp.bfloat16

    core = lax.axis_index("grp")
    chip = lax.axis_index("ep")
    ids = jnp.stack([core, chip]).astype(jnp.int32)
    table = jnp.concatenate([routes.astype(f32), gates.astype(f32)], axis=1).T
    copies = jnp.broadcast_to(table[None], (chips,) + table.shape)
    tables = lax.all_to_all(copies, "ep", split_axis=0, concat_axis=0, tiled=True)
    pick, spread = run_routing(ids, tables, top_count, capacity)

    gate_mats = (w_gate[0], swap_cores(w_gate[0]))
    up_mats = (w_up[0], swap_cores(w_up[0]))
    down_mats = (w_down[0], swap_cores(w_down[0]))
    behind = {(step, 2): (tables, gate_mats[1], up_mats[1]) for step in (1, -1)}
    behind.update({(step, 3): (down_mats[1],) for step in (1, -1)})
    in_shards, in_hops = ring_gather(tokens, chips, 1, behind)
    grad_later = copied(
        cotangent, [in_hops[1][0], in_hops[-1][0], tables, gate_mats[1], up_mats[1]]
    )
    behind = {
        (step, hop): (in_hops[step][hop - 1],)
        for step in (1, -1)
        for hop in range(2, len(in_hops[step]) + 1)
    }
    grad_shards, _ = ring_gather(grad_later, chips, -1, behind)

    def gather_rows(shards):
        return [
            jnp.dot(pick[s], shards[s], preferred_element_type=f32).astype(bf16)
            for s in range(chips)
        ]

    def scatter_rows(blocks):
        def share_of(s, partial, waits=(), add_waits=False):
            total = lax.dot_general(
                spread[s], blocks[s], (((0,), (0,)), ((), ())), preferred_element_type=f32
            )
            if partial is not None:
                total = total + partial.astype(f32)
            if add_waits:
                return (total + waits[0].astype(f32)).astype(bf16)
            total = total.astype(bf16)
            return held_back(total, waits) if waits else total

        return share_of

    rows_in = gather_rows(in_shards)
    hidden, slope, activated = run_hidden(rows_in, gate_mats, up_mats)
    outputs = run_down(hidden, down_mats, chips)
    rows_grad = gather_rows(grad_shards)
    d_pre_gate, d_pre_up, per_token = run_d_hidden(
        ids, rows_grad, outputs, pick, slope, activated, down_mats, ()
    )
    behind = {(step, 1): (per_token,) for step in (1, -1)}
    mixed, mixed_hops = ring_reduce(scatter_rows(outputs), chips, 1, behind)
    d_copies = run_d_copy(
        d_pre_gate, d_pre_up, gate_mats, up_mats, chips, [mixed_hops[step][0] for step in (1, -1)]
    )

    returned = lax.all_to_all(per_token, "ep", split_axis=0, concat_axis=0, tiled=True)
    behind = {
        (step, hop): (mixed_hops[step][hop + 1],)
        for step in (1, -1)
        for hop in range(len(mixed_hops[step]) - 1)
    }
    d_tokens, _ = ring_reduce(scatter_rows(d_copies), chips, -1, behind)
    chip_ids = jnp.arange(chips, dtype=jnp.int32)
    served = jnp.stack([core * chips + chip_ids, (1 - core) * chips + chip_ids], axis=1)
    chosen = routes.T[None, None] == served[:, :, None, None]
    d_gates = jnp.sum(jnp.where(chosen, returned[:, :, None, :], 0.0), axis=(0, 1)).T
    return (mixed, d_tokens, d_gates)


def solution(mesh):
    plan = body_ring if mesh.shape["ep"] <= 8 and mesh.shape["grp"] == 2 else body_exchange
    return jax.shard_map(
        plan,
        mesh=mesh,
        in_specs=(
            P(("rep", "grp", "ep"), None),
            P(("rep", "grp", "ep"), None),
            P(("rep", "grp", "ep"), None),
            P(("rep", "grp", "ep"), None),
            P(("grp", "ep"), None, None),
            P(("grp", "ep"), None, None),
            P(("grp", "ep"), None, None),
        ),
        out_specs=(
            P(("rep", "grp", "ep"), None),
            P(("rep", "grp", "ep"), None),
            P(("rep", "grp", "ep"), None),
        ),
        check_vma=False,
    )
```

```python
import jax
import jax.numpy as jnp
from jax import lax
from jax.experimental import pallas as pl
from jax.experimental.pallas import tpu as pltpu
from jax.sharding import PartitionSpec as P


def expert_pass(rows_in, rows_grad, gate_mat, up_mat, down_mat):
    pre_gate = jnp.dot(rows_in, gate_mat, preferred_element_type=jnp.float32)
    pre_up = jnp.dot(rows_in, up_mat, preferred_element_type=jnp.float32)
    activated = jax.nn.silu(pre_gate)
    hidden = (activated * pre_up).astype(jnp.bfloat16)
    outputs = jnp.dot(hidden, down_mat, preferred_element_type=jnp.float32).astype(jnp.bfloat16)
    d_hidden = lax.dot_general(
        rows_grad, down_mat, (((1,), (1,)), ((), ())), preferred_element_type=jnp.float32
    )
    sigma = jax.nn.sigmoid(pre_gate)
    d_pre_gate = (d_hidden * pre_up * sigma * (1.0 + pre_gate * (1.0 - sigma))).astype(jnp.bfloat16)
    d_pre_up = (d_hidden * activated).astype(jnp.bfloat16)
    both_pre = jnp.concatenate([d_pre_gate, d_pre_up], axis=1)
    both_mats = jnp.concatenate([gate_mat, up_mat], axis=1)
    d_copy = lax.dot_general(
        both_pre, both_mats, (((1,), (1,)), ((), ())), preferred_element_type=jnp.float32
    )
    return (outputs, d_copy.astype(jnp.bfloat16))


def run_items(pieces, gate_mat, up_mat, down_mat):
    rows_in, rows_grad = pieces
    lead_shape = rows_in.shape[:2]
    width = rows_in.shape[2]
    outputs, d_copy = expert_pass(
        rows_in.reshape(-1, width), rows_grad.reshape(-1, width), gate_mat, up_mat, down_mat
    )
    return (outputs.reshape(lead_shape + (width,)), d_copy.reshape(lead_shape + (width,)))


def ranks_of(chosen_hot):
    running = jnp.cumsum(chosen_hot, axis=-2)
    return jnp.sum(chosen_hot * running, axis=-1) - 1


def body_exchange(tokens, cotangent, routes, gates, w_gate, w_up, w_down):
    token_count = tokens.shape[0]
    width = tokens.shape[1]
    top_count = routes.shape[1]
    copy_count = token_count * top_count
    gate_mat = w_gate[0]
    up_mat = w_up[0]
    down_mat = w_down[0]
    expert_count = lax.axis_size(("grp", "ep"))
    capacity = max(2, 3 * token_count * top_count // (2 * expert_count))
    flat_experts = routes.reshape(-1)
    chosen_hot = (
        flat_experts[:, None] == jnp.arange(expert_count, dtype=jnp.int32)[None, :]
    ).astype(jnp.int32)
    slot_of = flat_experts * capacity + ranks_of(chosen_hot)
    token_of = jnp.arange(copy_count, dtype=jnp.int32) // top_count
    slot_token = jnp.zeros((expert_count * capacity,), jnp.int32).at[slot_of].set(token_of)
    slot_live = jnp.zeros((expert_count * capacity,), jnp.bool_).at[slot_of].set(True)
    send_in = jnp.where(
        slot_live[:, None], tokens[slot_token], jnp.zeros((), tokens.dtype)
    ).reshape(expert_count, capacity, width)
    send_grad = jnp.where(
        slot_live[:, None], cotangent[slot_token], jnp.zeros((), cotangent.dtype)
    ).reshape(expert_count, capacity, width)
    outputs, d_copy = run_items(
        (
            lax.all_to_all(send_in, ("grp", "ep"), split_axis=0, concat_axis=0, tiled=True),
            lax.all_to_all(send_grad, ("grp", "ep"), split_axis=0, concat_axis=0, tiled=True),
        ),
        gate_mat,
        up_mat,
        down_mat,
    )
    back_out = lax.all_to_all(outputs, ("grp", "ep"), split_axis=0, concat_axis=0, tiled=True)
    back_grad = lax.all_to_all(d_copy, ("grp", "ep"), split_axis=0, concat_axis=0, tiled=True)
    copy_out = back_out.reshape(-1, width)[slot_of].reshape(token_count, top_count, width)
    copy_grad = back_grad.reshape(-1, width)[slot_of].reshape(token_count, top_count, width)
    weight = gates.astype(jnp.float32)
    mixed = jnp.sum(weight[:, :, None] * copy_out.astype(jnp.float32), axis=1)
    d_tokens = jnp.sum(weight[:, :, None] * copy_grad.astype(jnp.float32), axis=1)
    d_gates = jnp.einsum("tkd,td->tk", copy_out, cotangent, preferred_element_type=jnp.float32)
    return (mixed.astype(jnp.bfloat16), d_tokens.astype(jnp.bfloat16), d_gates)


def ring_order(count):
    return list(range(0, count, 2)) + list(range(count - 1, 0, -2))


def ring_shift(array, count, step):
    order = ring_order(count)
    pairs = [(order[i], order[(i + step) % count]) for i in range(count)]
    return lax.ppermute(array, "ep", pairs)


def hops_of(count, step, far_step):
    return count // 2 if step == far_step else (count - 1) // 2


def ring_gather(first, second, count, behind):
    rows = first.shape[0]
    held = [{0: (first, 0)}, {0: (second, 0)}]
    for step in (1, -1):
        hops = hops_of(count, step, 1), hops_of(count, step, -1)
        low, high = (first, 0), None
        for stage in range(1, max(hops[0], hops[1] + 1) + 1):
            if stage == 2:
                high = (second, 0)
            one = low if stage <= hops[0] else None
            two = high if 1 < stage <= hops[1] + 1 else None
            last = stage >= hops[0]
            if one and two and not last:
                if one[0] is two[0]:
                    both = one[0]
                else:
                    both = run_join(one[0], two[0], behind)
                both = ring_shift(both, count, step)
                low, high = (both, 0), (both, rows)
            else:
                cuts = [None if v is None else v[0][v[1] : v[1] + rows] for v in (one, two)]
                if one:
                    low = (ring_shift(cuts[0], count, step), 0)
                if two:
                    high = (ring_shift(cuts[1], count, step), 0)
            if one:
                held[0][(-step * stage) % count] = low
            if two:
                held[1][(-step * (stage - 1)) % count] = high
    return [[h[place] for place in range(count)] for h in held]


VMEM_LIMIT = 48 * 1024 * 1024
LAST = (((1,), (1,)), ((), ()))


def cut(size, most):
    return max(w for w in range(128, most + 1, 128) if size % w == 0)


def call_kernel(kernel, operands, kinds, outs, scratch, flops, behind=()):
    spaces = {"any": pltpu.HBM, "vmem": pltpu.VMEM, "smem": pltpu.SMEM}
    count = len(operands)
    operands = [*operands, *behind]
    kinds = [*kinds, *["any" for _ in behind]]

    def body(*refs):
        kernel(*refs[:count], *refs[len(operands) :])

    return pl.pallas_call(
        body,
        out_shape=outs,
        in_specs=[pl.BlockSpec(memory_space=spaces[k]) for k in kinds],
        out_specs=[pl.BlockSpec(memory_space=pltpu.VMEM) for _ in outs],
        scratch_shapes=scratch,
        compiler_params=pltpu.CompilerParams(vmem_limit_bytes=VMEM_LIMIT),
        cost_estimate=pl.CostEstimate(flops=flops, bytes_accessed=1 << 20, transcendentals=0),
    )(*operands)


def pack_rows(parts, packed):
    half = parts[0].shape[0] // 2
    for e in range(2):
        for s, part in enumerate(parts):
            packed[e, s * half : (s + 1) * half, :] = part[e * half : (e + 1) * half, :]


def source_at(distance, chip, count):
    place = jnp.where(chip % 2 == 0, chip // 2, count - (chip + 1) // 2)
    place = (place + distance) % count
    return jnp.where(place < count // 2, 2 * place, 2 * (count - place) - 1)


def run_routing(ids, tables, top_count, capacity):
    count, _, tokens = tables.shape
    f32, bf16 = jnp.float32, jnp.bfloat16

    def kernel(ids_ref, table_ref, pick_ref, spread_ref):
        core, chip = ids_ref[0], ids_ref[1]
        first = lax.broadcasted_iota(jnp.int32, (tokens, tokens), 0)
        second = lax.broadcasted_iota(jnp.int32, (tokens, tokens), 1)
        before = (first <= second).astype(f32).astype(bf16)
        slot = lax.broadcasted_iota(jnp.int32, (capacity, tokens), 0).astype(f32)
        hits, weights = [], []
        for s in range(count):
            table = table_ref[source_at(s, chip, count)]
            for e in range(2):
                expert = jnp.where(core == e, chip, count + chip).astype(f32)
                hit = (table[:top_count] == expert).astype(f32)
                hits.append(jnp.sum(hit, axis=0, keepdims=True))
                weights.append(
                    jnp.sum(hit * table[top_count : 2 * top_count], axis=0, keepdims=True)
                )
        rank = jnp.dot(
            jnp.concatenate(hits, axis=0).astype(bf16), before, preferred_element_type=f32
        )
        for s in range(count):
            for e in range(2):
                i = 2 * s + e
                chosen = jnp.where(slot == rank[i : i + 1] - 1.0, hits[i], 0.0)
                span = slice(e * capacity, (e + 1) * capacity)
                pick_ref[s, span, :] = chosen.astype(bf16)
                spread_ref[s, span, :] = (chosen * weights[i]).astype(bf16)

    shape = jax.ShapeDtypeStruct((count, 2 * capacity, tokens), bf16)
    return call_kernel(kernel, [ids, tables], ["smem", "vmem"], [shape, shape], [], 1 << 20)


def run_join(upper, lower, behind):
    rows, width = upper.shape
    tile = cut(width, 512)

    def kernel(*refs):
        refs[-1][:rows, :] = refs[0][...]
        refs[-1][rows:, :] = refs[1][...]

    return pl.pallas_call(
        kernel,
        grid=(width // tile,),
        out_shape=jax.ShapeDtypeStruct((2 * rows, width), upper.dtype),
        in_specs=[pl.BlockSpec((rows, tile), lambda i: (0, i)) for _ in range(2)]
        + [pl.BlockSpec(memory_space=pltpu.HBM) for _ in behind],
        out_specs=pl.BlockSpec((2 * rows, tile), lambda i: (0, i)),
    )(upper, lower, *behind)


def run_pick(pick, wanted):
    _, slots, tokens = pick.shape
    width = wanted[0][0].shape[1]
    tile = cut(width, 512)
    count = len(wanted)

    def kernel(*refs):
        for i in range(count):
            refs[2 * count + i][...] = jnp.dot(
                refs[i][0], refs[count + i][...], preferred_element_type=jnp.float32
            ).astype(jnp.bfloat16)

    return pl.pallas_call(
        kernel,
        grid=(width // tile,),
        out_shape=[jax.ShapeDtypeStruct((slots, width), jnp.bfloat16) for _ in wanted],
        in_specs=[
            pl.BlockSpec((1, slots, tokens), lambda i, s=s: (s, 0, 0)) for _, _, s in wanted
        ]
        + [pl.BlockSpec((tokens, tile), lambda i, r=r: (r // tokens, i)) for _, r, _ in wanted],
        out_specs=[pl.BlockSpec((slots, tile), lambda i: (0, i)) for _ in wanted],
    )(*[pick for _ in wanted], *[buffer for buffer, _, _ in wanted])


def run_shares(spread, wanted, behind=()):
    _, slots, tokens = spread.shape
    width = wanted[0][0].shape[2]
    tile = cut(width, 512)
    count = len(wanted)
    extra = [partial for _, _, partials in wanted for partial in partials]

    def kernel(*refs):
        rest = list(refs[2 * count : 2 * count + len(extra)])
        for i, (_, _, partials) in enumerate(wanted):
            total = lax.dot_general(
                refs[i][0],
                refs[count + i][0],
                (((0,), (0,)), ((), ())),
                preferred_element_type=jnp.float32,
            )
            for _ in partials:
                total = total + rest.pop(0)[...].astype(jnp.float32)
            refs[-1][i * tokens : (i + 1) * tokens, :] = total.astype(jnp.bfloat16)

    return pl.pallas_call(
        kernel,
        grid=(width // tile,),
        out_shape=jax.ShapeDtypeStruct((count * tokens, width), jnp.bfloat16),
        in_specs=[
            pl.BlockSpec((1, slots, tokens), lambda i, s=s: (s, 0, 0)) for _, s, _ in wanted
        ]
        + [pl.BlockSpec((1, slots, tile), lambda i, s=s: (s, 0, i)) for _, s, _ in wanted]
        + [pl.BlockSpec((tokens, tile), lambda i, r=r: (r // tokens, i)) for _, r in extra]
        + [pl.BlockSpec(memory_space=pltpu.HBM) for _ in behind],
        out_specs=pl.BlockSpec((count * tokens, tile), lambda i: (0, i)),
    )(
        *[spread for _ in wanted],
        *[outputs for outputs, _, _ in wanted],
        *[buffer for buffer, _ in extra],
        *behind,
    )


def run_hidden(parts, gate_mats, up_mats):
    count, rows, width = len(parts), parts[0].shape[0], parts[0].shape[1]
    units = gate_mats[0].shape[1]
    total = count * rows // 2
    tile = cut(units, 256)
    tiles = units // tile

    def kernel(*refs):
        part_refs, mats = refs[:count], refs[count : count + 4]
        hidden_ref, slope_ref, act_ref, packed, held, sems = refs[count + 4 :]
        copies = {}
        for e in range(2):
            for m in range(2):
                copies[e, m] = pltpu.make_async_copy(
                    mats[2 * m + e], held.at[e, m], sems.at[e, m]
                )
                copies[e, m].start()
        pack_rows(part_refs, packed)
        for e in range(2):
            for m in range(2):
                copies[e, m].wait()
            for n in range(tiles):
                span = slice(n * tile, (n + 1) * tile)
                gate = jnp.dot(packed[e], held[e, 0, :, span], preferred_element_type=jnp.float32)
                up = jnp.dot(packed[e], held[e, 1, :, span], preferred_element_type=jnp.float32)
                sigma = 1.0 / (1.0 + jnp.exp(-gate))
                act = gate * sigma
                hidden_ref[e, :, span] = (act * up).astype(jnp.bfloat16)
                slope_ref[e, :, span] = up * sigma * (1.0 + gate * (1.0 - sigma))
                act_ref[e, :, span] = act

    return call_kernel(
        kernel,
        [*parts, *gate_mats, *up_mats],
        ["vmem"] * count + ["any"] * 4,
        [
            jax.ShapeDtypeStruct((2, total, units), jnp.bfloat16),
            jax.ShapeDtypeStruct((2, total, units), jnp.float32),
            jax.ShapeDtypeStruct((2, total, units), jnp.float32),
        ],
        [
            pltpu.VMEM((2, total, width), jnp.bfloat16),
            pltpu.VMEM((2, 2, width, units), jnp.bfloat16),
            pltpu.SemaphoreType.DMA((2, 2)),
        ],
        8 * total * width * units,
    )


def run_down(hidden, down_mats, count):
    _, total, units = hidden.shape
    width = down_mats[0].shape[1]
    half = total // count
    tile = cut(width, 512)
    tiles = width // tile

    def kernel(hidden_ref, own_ref, other_ref, out_ref, held, sems):
        copies = {}
        for e, mat in enumerate((own_ref, other_ref)):
            copies[e] = pltpu.make_async_copy(mat, held.at[e], sems.at[e])
            copies[e].start()
        for e in range(2):
            copies[e].wait()
            for n in range(tiles):
                columns = held[e, :, n * tile : (n + 1) * tile]
                out = jnp.dot(hidden_ref[e], columns, preferred_element_type=jnp.float32)
                out_ref[:, e * half : (e + 1) * half, n * tile : (n + 1) * tile] = (
                    out.astype(jnp.bfloat16).reshape(count, half, tile)
                )

    return call_kernel(
        kernel,
        [hidden, *down_mats],
        ["vmem", "any", "any"],
        [jax.ShapeDtypeStruct((count, 2 * half, width), jnp.bfloat16)],
        [
            pltpu.VMEM((2, units, width), jnp.bfloat16),
            pltpu.SemaphoreType.DMA((2,)),
        ],
        4 * total * width * units,
    )[0]


def run_d_hidden(ids, parts, outputs, pick, slope, activated, down_mats, behind):
    count, rows, width = len(parts), parts[0].shape[0], parts[0].shape[1]
    half = rows // 2
    _, total, units = slope.shape
    tile = cut(units, 256)
    tiles = units // tile
    tokens = pick.shape[2]

    def kernel(*refs):
        ids_ref, refs = refs[0], refs[1:]
        part_refs = refs[:count]
        out_ref, pick_ref, slope_ref, act_ref, own_ref, other_ref = refs[count : count + 6]
        d_gate_ref, d_up_ref, token_ref, packed, held, sems = refs[count + 6 :]
        copies = {}
        for e, mat in enumerate((own_ref, other_ref)):
            for n in range(tiles):
                copies[e, n] = pltpu.make_async_copy(
                    mat.at[n * tile : (n + 1) * tile, :], held.at[e, n], sems.at[e, n]
                )
                copies[e, n].start()
        pack_rows(part_refs, packed)
        for e in range(2):
            for n in range(tiles):
                span = slice(n * tile, (n + 1) * tile)
                copies[e, n].wait()
                d_hidden = lax.dot_general(
                    packed[e], held[e, n], LAST, preferred_element_type=jnp.float32
                )
                d_gate_ref[e, :, span] = (d_hidden * slope_ref[e, :, span]).astype(jnp.bfloat16)
                d_up_ref[e, :, span] = (d_hidden * act_ref[e, :, span]).astype(jnp.bfloat16)
        for s in range(count):
            inner = jnp.sum(
                part_refs[s][...].astype(jnp.float32) * out_ref[s].astype(jnp.float32),
                axis=1,
                keepdims=True,
            )
            spread = pick_ref[s].astype(jnp.float32) * inner
            sums = [
                jnp.sum(spread[e * half : (e + 1) * half], axis=0, keepdims=True)
                for e in range(2)
            ]
            token_ref[source_at(s, ids_ref[1], count)] = jnp.concatenate(sums, axis=0)

    return call_kernel(
        kernel,
        [ids, *parts, outputs, pick, slope, activated, *down_mats],
        ["smem"] + ["vmem"] * (count + 4) + ["any"] * 2,
        [
            jax.ShapeDtypeStruct((2, total, units), jnp.bfloat16),
            jax.ShapeDtypeStruct((2, total, units), jnp.bfloat16),
            jax.ShapeDtypeStruct((count, 2, tokens), jnp.float32),
        ],
        [
            pltpu.VMEM((2, total, width), jnp.bfloat16),
            pltpu.VMEM((2, tiles, tile, width), jnp.bfloat16),
            pltpu.SemaphoreType.DMA((2, tiles)),
        ],
        4 * total * width * units,
        behind,
    )


def run_d_copy(d_pre_gate, d_pre_up, gate_mats, up_mats, count, behind):
    _, total, units = d_pre_gate.shape
    width = gate_mats[0].shape[0]
    half = total // count
    tile = cut(width, 512)
    tiles = width // tile

    def kernel(d_gate_ref, d_up_ref, *refs):
        mats = refs[:4]
        out_ref, held, sems = refs[4:]
        copies = {}
        for e in range(2):
            for n in range(tiles):
                for m in range(2):
                    copies[e, n, m] = pltpu.make_async_copy(
                        mats[2 * m + e].at[n * tile : (n + 1) * tile, :],
                        held.at[e, n, m],
                        sems.at[e, n, m],
                    )
                    copies[e, n, m].start()
        for e in range(2):
            for n in range(tiles):
                copies[e, n, 0].wait()
                out = lax.dot_general(
                    d_gate_ref[e], held[e, n, 0], LAST, preferred_element_type=jnp.float32
                )
                copies[e, n, 1].wait()
                out = out + lax.dot_general(
                    d_up_ref[e], held[e, n, 1], LAST, preferred_element_type=jnp.float32
                )
                out_ref[:, e * half : (e + 1) * half, n * tile : (n + 1) * tile] = (
                    out.astype(jnp.bfloat16).reshape(count, half, tile)
                )

    return call_kernel(
        kernel,
        [d_pre_gate, d_pre_up, *gate_mats, *up_mats],
        ["vmem", "vmem"] + ["any"] * 4,
        [jax.ShapeDtypeStruct((count, 2 * half, width), jnp.bfloat16)],
        [
            pltpu.VMEM((2, tiles, 2, tile, units), jnp.bfloat16),
            pltpu.SemaphoreType.DMA((2, tiles, 2)),
        ],
        8 * total * width * units,
        behind,
    )[0]


def swap_cores(array):
    return lax.ppermute(array, "grp", [(0, 1), (1, 0)])


def body_ring(tokens, cotangent, routes, gates, w_gate, w_up, w_down):
    token_count = tokens.shape[0]
    width = tokens.shape[1]
    top_count = routes.shape[1]
    chips = lax.axis_size("ep")
    expert_count = lax.axis_size(("grp", "ep"))
    capacity = max(2, 3 * token_count * top_count // (2 * expert_count))
    f32, bf16 = jnp.float32, jnp.bfloat16

    core = lax.axis_index("grp")
    chip = lax.axis_index("ep")
    ids = jnp.stack([core, chip]).astype(jnp.int32)
    table = jnp.concatenate([routes.astype(f32), gates.astype(f32)], axis=1).T
    copies = jnp.broadcast_to(table[None], (chips,) + table.shape)
    tables = lax.all_to_all(copies, "ep", split_axis=0, concat_axis=0, tiled=True)
    pick, spread = run_routing(ids, tables, top_count, capacity)

    gate_mats = (w_gate[0], swap_cores(w_gate[0]))
    up_mats = (w_up[0], swap_cores(w_up[0]))
    down_mats = (w_down[0], swap_cores(w_down[0]))

    in_held, grad_held = ring_gather(
        tokens, cotangent, chips, (tables, gate_mats[1], up_mats[1])
    )
    rows_in, rows_grad = [None] * chips, [None] * chips
    grouped = {}
    for rows, held in ((rows_in, in_held), (rows_grad, grad_held)):
        for s, (buffer, offset) in enumerate(held):
            grouped.setdefault(id(buffer), []).append((rows, (buffer, offset, s)))
    for group in grouped.values():
        for (rows, (_, _, s)), picked in zip(group, run_pick(pick, [w for _, w in group])):
            rows[s] = picked

    hidden, slope, activated = run_hidden(rows_in, gate_mats, up_mats)
    outputs = run_down(hidden, down_mats, chips)
    d_pre_gate, d_pre_up, per_token = run_d_hidden(
        ids, rows_grad, outputs, pick, slope, activated, down_mats, ()
    )

    lag = 2
    arrived = {}
    for step in (1, -1):
        now = ring_shift(
            run_shares(spread, [(outputs, (step * hops_of(chips, step, 1)) % chips, [])]), chips, step
        )
        arrived[step] = [(now, 0)]
    d_copies = run_d_copy(
        d_pre_gate, d_pre_up, gate_mats, up_mats, chips, [arrived[step][0][0] for step in (1, -1)]
    )
    mixed_last, grad_last = {}, {}
    for step in (1, -1):
        ahead, later = hops_of(chips, step, 1), hops_of(chips, step, -1)
        partial, grad_partial = arrived[step][0], None
        for stage in range(2, max(ahead, later + lag) + 1):
            wanted = []
            if stage <= ahead:
                wanted.append((outputs, (step * (ahead - stage + 1)) % chips, [partial]))
            if stage > lag:
                place = (step * (later - stage + lag + 1)) % chips
                wanted.append((d_copies, place, [grad_partial] if grad_partial else []))
            behind = (per_token,) if stage == 2 else ()
            now = ring_shift(run_shares(spread, wanted, behind), chips, step)
            if stage <= ahead:
                partial = (now, 0)
            if stage > lag:
                grad_partial = (now, (len(wanted) - 1) * token_count)
        mixed_last[step], grad_last[step] = partial, grad_partial
    mixed = run_shares(spread, [(outputs, 0, [mixed_last[1], mixed_last[-1]])])
    d_tokens = run_shares(spread, [(d_copies, 0, [grad_last[1], grad_last[-1]])])

    returned = lax.all_to_all(per_token, "ep", split_axis=0, concat_axis=0, tiled=True)
    chip_ids = jnp.arange(chips, dtype=jnp.int32)
    served = jnp.stack([core * chips + chip_ids, (1 - core) * chips + chip_ids], axis=1)
    chosen = routes.T[None, None] == served[:, :, None, None]
    d_gates = jnp.sum(jnp.where(chosen, returned[:, :, None, :], 0.0), axis=(0, 1)).T
    return (mixed, d_tokens, d_gates)


def solution(mesh):
    plan = body_ring if 4 <= mesh.shape["ep"] <= 8 and mesh.shape["grp"] == 2 else body_exchange
    return jax.shard_map(
        plan,
        mesh=mesh,
        in_specs=(
            P(("rep", "grp", "ep"), None),
            P(("rep", "grp", "ep"), None),
            P(("rep", "grp", "ep"), None),
            P(("rep", "grp", "ep"), None),
            P(("grp", "ep"), None, None),
            P(("grp", "ep"), None, None),
            P(("grp", "ep"), None, None),
        ),
        out_specs=(
            P(("rep", "grp", "ep"), None),
            P(("rep", "grp", "ep"), None),
            P(("rep", "grp", "ep"), None),
        ),
        check_vma=False,
    )
```

```python
import jax
import jax.numpy as jnp
from jax import lax
from jax.experimental import pallas as pl
from jax.experimental.pallas import tpu as pltpu
from jax.sharding import PartitionSpec as P


def expert_pass(rows_in, rows_grad, gate_mat, up_mat, down_mat):
    pre_gate = jnp.dot(rows_in, gate_mat, preferred_element_type=jnp.float32)
    pre_up = jnp.dot(rows_in, up_mat, preferred_element_type=jnp.float32)
    activated = jax.nn.silu(pre_gate)
    hidden = (activated * pre_up).astype(jnp.bfloat16)
    outputs = jnp.dot(hidden, down_mat, preferred_element_type=jnp.float32).astype(jnp.bfloat16)
    d_hidden = lax.dot_general(
        rows_grad, down_mat, (((1,), (1,)), ((), ())), preferred_element_type=jnp.float32
    )
    sigma = jax.nn.sigmoid(pre_gate)
    d_pre_gate = (d_hidden * pre_up * sigma * (1.0 + pre_gate * (1.0 - sigma))).astype(jnp.bfloat16)
    d_pre_up = (d_hidden * activated).astype(jnp.bfloat16)
    both_pre = jnp.concatenate([d_pre_gate, d_pre_up], axis=1)
    both_mats = jnp.concatenate([gate_mat, up_mat], axis=1)
    d_copy = lax.dot_general(
        both_pre, both_mats, (((1,), (1,)), ((), ())), preferred_element_type=jnp.float32
    )
    return (outputs, d_copy.astype(jnp.bfloat16))


def run_items(pieces, gate_mat, up_mat, down_mat):
    rows_in, rows_grad = pieces
    lead_shape = rows_in.shape[:2]
    width = rows_in.shape[2]
    outputs, d_copy = expert_pass(
        rows_in.reshape(-1, width), rows_grad.reshape(-1, width), gate_mat, up_mat, down_mat
    )
    return (outputs.reshape(lead_shape + (width,)), d_copy.reshape(lead_shape + (width,)))


def ranks_of(chosen_hot):
    running = jnp.cumsum(chosen_hot, axis=-2)
    return jnp.sum(chosen_hot * running, axis=-1) - 1


def body_exchange(tokens, cotangent, routes, gates, w_gate, w_up, w_down):
    token_count = tokens.shape[0]
    width = tokens.shape[1]
    top_count = routes.shape[1]
    copy_count = token_count * top_count
    gate_mat = w_gate[0]
    up_mat = w_up[0]
    down_mat = w_down[0]
    expert_count = lax.axis_size(("grp", "ep"))
    capacity = max(2, 3 * token_count * top_count // (2 * expert_count))
    flat_experts = routes.reshape(-1)
    chosen_hot = (
        flat_experts[:, None] == jnp.arange(expert_count, dtype=jnp.int32)[None, :]
    ).astype(jnp.int32)
    slot_of = flat_experts * capacity + ranks_of(chosen_hot)
    token_of = jnp.arange(copy_count, dtype=jnp.int32) // top_count
    slot_token = jnp.zeros((expert_count * capacity,), jnp.int32).at[slot_of].set(token_of)
    slot_live = jnp.zeros((expert_count * capacity,), jnp.bool_).at[slot_of].set(True)
    send_in = jnp.where(
        slot_live[:, None], tokens[slot_token], jnp.zeros((), tokens.dtype)
    ).reshape(expert_count, capacity, width)
    send_grad = jnp.where(
        slot_live[:, None], cotangent[slot_token], jnp.zeros((), cotangent.dtype)
    ).reshape(expert_count, capacity, width)
    outputs, d_copy = run_items(
        (
            lax.all_to_all(send_in, ("grp", "ep"), split_axis=0, concat_axis=0, tiled=True),
            lax.all_to_all(send_grad, ("grp", "ep"), split_axis=0, concat_axis=0, tiled=True),
        ),
        gate_mat,
        up_mat,
        down_mat,
    )
    back_out = lax.all_to_all(outputs, ("grp", "ep"), split_axis=0, concat_axis=0, tiled=True)
    back_grad = lax.all_to_all(d_copy, ("grp", "ep"), split_axis=0, concat_axis=0, tiled=True)
    copy_out = back_out.reshape(-1, width)[slot_of].reshape(token_count, top_count, width)
    copy_grad = back_grad.reshape(-1, width)[slot_of].reshape(token_count, top_count, width)
    weight = gates.astype(jnp.float32)
    mixed = jnp.sum(weight[:, :, None] * copy_out.astype(jnp.float32), axis=1)
    d_tokens = jnp.sum(weight[:, :, None] * copy_grad.astype(jnp.float32), axis=1)
    d_gates = jnp.einsum("tkd,td->tk", copy_out, cotangent, preferred_element_type=jnp.float32)
    return (mixed.astype(jnp.bfloat16), d_tokens.astype(jnp.bfloat16), d_gates)


def ring_order(count):
    return list(range(0, count, 2)) + list(range(count - 1, 0, -2))


def ring_shift(array, count, step):
    order = ring_order(count)
    pairs = [(order[i], order[(i + step) % count]) for i in range(count)]
    return lax.ppermute(array, "ep", pairs)


def hops_of(count, step, far_step):
    return count // 2 if step == far_step else (count - 1) // 2


def ring_gather(first, second, count, behind, rows_of):
    rows = first.shape[0]
    held = [{0: (first, 0)}, {0: (second, 0)}]
    opening = {step: ring_shift(first, count, step) for step in (1, -1)}
    joined = dict(zip((1, -1), run_join([opening[1], opening[-1]], second, behind)))
    for step in (1, -1):
        hops = hops_of(count, step, 1), hops_of(count, step, -1)
        low, high = (first, 0), None
        for stage in range(1, max(hops[0], hops[1] + 1) + 1):
            if stage == 2:
                high = (second, 0)
            one = low if stage <= hops[0] else None
            two = high if 1 < stage <= hops[1] + 1 else None
            last = stage >= hops[0]
            if one and two and not last:
                both = ring_shift(joined[step] if stage == 2 else one[0], count, step)
                low, high = (both, 0), (both, rows)
            else:
                cuts = [None if v is None else v[0][v[1] : v[1] + rows] for v in (one, two)]
                if one and two:
                    cuts[1] = after(cuts[1], rows_of((-step * (stage - 1)) % count, low))
                if one:
                    sent = opening[step] if stage == 1 else ring_shift(cuts[0], count, step)
                    low = (sent, 0)
                if two:
                    high = (ring_shift(cuts[1], count, step), 0)
            if one:
                held[0][(-step * stage) % count] = low
            if two:
                held[1][(-step * (stage - 1)) % count] = high
    return [[h[place] for place in range(count)] for h in held]


def after(array, *others):
    for other in others:
        array = array + other[(slice(0, 1),) * other.ndim].reshape((1,) * array.ndim).astype(array.dtype) * 0
    return array


def ring_reduce(share_of, count, far_step, behind={}):
    arrived = {}
    for step in (far_step, -far_step):
        hops = count // 2 if step == far_step else (count - 1) // 2
        moving = None
        steps = []
        for hop in range(hops, 0, -1):
            waits = behind.get((step, hops - hop), ())
            share = share_of((step * hop) % count, moving, waits)
            moving = ring_shift(share, count, step)
            steps.append(moving)
        arrived[step] = steps
    total = share_of(0, arrived[far_step][-1], (arrived[-far_step][-1],), True)
    return total, arrived


VMEM_LIMIT = 48 * 1024 * 1024
LAST = (((1,), (1,)), ((), ()))


def cut(size, most):
    return max(w for w in range(128, most + 1, 128) if size % w == 0)


def call_kernel(kernel, operands, kinds, outs, scratch, flops, behind=()):
    spaces = {"any": pltpu.HBM, "vmem": pltpu.VMEM, "smem": pltpu.SMEM}
    count = len(operands)
    operands = [*operands, *behind]
    kinds = [*kinds, *["any" for _ in behind]]

    def body(*refs):
        kernel(*refs[:count], *refs[len(operands) :])

    return pl.pallas_call(
        body,
        out_shape=outs,
        in_specs=[pl.BlockSpec(memory_space=spaces[k]) for k in kinds],
        out_specs=[pl.BlockSpec(memory_space=pltpu.VMEM) for _ in outs],
        scratch_shapes=scratch,
        compiler_params=pltpu.CompilerParams(vmem_limit_bytes=VMEM_LIMIT),
        cost_estimate=pl.CostEstimate(flops=flops, bytes_accessed=1 << 20, transcendentals=0),
    )(*operands)


def pack_rows(parts, packed):
    half = parts[0].shape[0] // 2
    for e in range(2):
        for s, part in enumerate(parts):
            packed[e, s * half : (s + 1) * half, :] = part[e * half : (e + 1) * half, :]


def source_at(distance, chip, count):
    place = jnp.where(chip % 2 == 0, chip // 2, count - (chip + 1) // 2)
    place = (place + distance) % count
    return jnp.where(place < count // 2, 2 * place, 2 * (count - place) - 1)


def run_routing(ids, tables, top_count, capacity):
    count, _, tokens = tables.shape
    f32, bf16 = jnp.float32, jnp.bfloat16

    def kernel(ids_ref, table_ref, pick_ref, spread_ref):
        core, chip = ids_ref[0], ids_ref[1]
        first = lax.broadcasted_iota(jnp.int32, (tokens, tokens), 0)
        second = lax.broadcasted_iota(jnp.int32, (tokens, tokens), 1)
        before = (first <= second).astype(f32).astype(bf16)
        slot = lax.broadcasted_iota(jnp.int32, (capacity, tokens), 0).astype(f32)
        hits, weights = [], []
        for s in range(count):
            table = table_ref[source_at(s, chip, count)]
            for e in range(2):
                expert = jnp.where(core == e, chip, count + chip).astype(f32)
                hit = (table[:top_count] == expert).astype(f32)
                hits.append(jnp.sum(hit, axis=0, keepdims=True))
                weights.append(
                    jnp.sum(hit * table[top_count : 2 * top_count], axis=0, keepdims=True)
                )
        rank = jnp.dot(
            jnp.concatenate(hits, axis=0).astype(bf16), before, preferred_element_type=f32
        )
        for s in range(count):
            for e in range(2):
                i = 2 * s + e
                chosen = jnp.where(slot == rank[i : i + 1] - 1.0, hits[i], 0.0)
                span = slice(e * capacity, (e + 1) * capacity)
                pick_ref[s, span, :] = chosen.astype(bf16)
                spread_ref[s, span, :] = (chosen * weights[i]).astype(bf16)

    shape = jax.ShapeDtypeStruct((count, 2 * capacity, tokens), bf16)
    return call_kernel(kernel, [ids, tables], ["smem", "vmem"], [shape, shape], [], 1 << 20)


def run_join(uppers, lower, behind):
    rows, width = lower.shape
    count = len(uppers)

    def kernel(*refs):
        for upper_ref, out_ref in zip(refs[:count], refs[count + 1 :]):
            out_ref[:rows, :] = upper_ref[...]
            out_ref[rows:, :] = refs[count][...]

    shape = jax.ShapeDtypeStruct((2 * rows, width), lower.dtype)
    return call_kernel(
        kernel, [*uppers, lower], ["vmem"] * (count + 1), [shape] * count, [], 1, behind
    )


def run_hidden(parts, gate_mats, up_mats):
    count, rows, width = len(parts), parts[0].shape[0], parts[0].shape[1]
    units = gate_mats[0].shape[1]
    total = count * rows // 2
    tile = cut(units, 256)
    tiles = units // tile

    def kernel(*refs):
        part_refs, mats = refs[:count], refs[count : count + 4]
        hidden_ref, slope_ref, act_ref, packed, held, sems = refs[count + 4 :]
        copies = {}
        for e in range(2):
            for m in range(2):
                copies[e, m] = pltpu.make_async_copy(
                    mats[2 * m + e], held.at[e, m], sems.at[e, m]
                )
                copies[e, m].start()
        pack_rows(part_refs, packed)
        for e in range(2):
            for m in range(2):
                copies[e, m].wait()
            for n in range(tiles):
                span = slice(n * tile, (n + 1) * tile)
                gate = jnp.dot(packed[e], held[e, 0, :, span], preferred_element_type=jnp.float32)
                up = jnp.dot(packed[e], held[e, 1, :, span], preferred_element_type=jnp.float32)
                sigma = 1.0 / (1.0 + jnp.exp(-gate))
                act = gate * sigma
                hidden_ref[e, :, span] = (act * up).astype(jnp.bfloat16)
                slope_ref[e, :, span] = up * sigma * (1.0 + gate * (1.0 - sigma))
                act_ref[e, :, span] = act

    return call_kernel(
        kernel,
        [*parts, *gate_mats, *up_mats],
        ["vmem"] * count + ["any"] * 4,
        [
            jax.ShapeDtypeStruct((2, total, units), jnp.bfloat16),
            jax.ShapeDtypeStruct((2, total, units), jnp.float32),
            jax.ShapeDtypeStruct((2, total, units), jnp.float32),
        ],
        [
            pltpu.VMEM((2, total, width), jnp.bfloat16),
            pltpu.VMEM((2, 2, width, units), jnp.bfloat16),
            pltpu.SemaphoreType.DMA((2, 2)),
        ],
        8 * total * width * units,
    )


def run_down(hidden, down_mats, count):
    _, total, units = hidden.shape
    width = down_mats[0].shape[1]
    half = total // count
    tile = cut(width, 512)
    tiles = width // tile

    def kernel(hidden_ref, own_ref, other_ref, out_ref, held, sems):
        copies = {}
        for e, mat in enumerate((own_ref, other_ref)):
            copies[e] = pltpu.make_async_copy(mat, held.at[e], sems.at[e])
            copies[e].start()
        for e in range(2):
            copies[e].wait()
            for n in range(tiles):
                columns = held[e, :, n * tile : (n + 1) * tile]
                out = jnp.dot(hidden_ref[e], columns, preferred_element_type=jnp.float32)
                out_ref[:, e * half : (e + 1) * half, n * tile : (n + 1) * tile] = (
                    out.astype(jnp.bfloat16).reshape(count, half, tile)
                )

    return call_kernel(
        kernel,
        [hidden, *down_mats],
        ["vmem", "any", "any"],
        [jax.ShapeDtypeStruct((count, 2 * half, width), jnp.bfloat16)],
        [
            pltpu.VMEM((2, units, width), jnp.bfloat16),
            pltpu.SemaphoreType.DMA((2,)),
        ],
        4 * total * width * units,
    )[0]


def run_d_hidden(ids, parts, outputs, pick, slope, activated, down_mats, behind):
    count, rows, width = len(parts), parts[0].shape[0], parts[0].shape[1]
    half = rows // 2
    _, total, units = slope.shape
    tile = cut(units, 256)
    tiles = units // tile
    tokens = pick.shape[2]

    def kernel(*refs):
        ids_ref, refs = refs[0], refs[1:]
        part_refs = refs[:count]
        out_ref, pick_ref, slope_ref, act_ref, own_ref, other_ref = refs[count : count + 6]
        d_gate_ref, d_up_ref, token_ref, packed, held, sems = refs[count + 6 :]
        copies = {}
        for e, mat in enumerate((own_ref, other_ref)):
            for n in range(tiles):
                copies[e, n] = pltpu.make_async_copy(
                    mat.at[n * tile : (n + 1) * tile, :], held.at[e, n], sems.at[e, n]
                )
                copies[e, n].start()
        pack_rows(part_refs, packed)
        for e in range(2):
            for n in range(tiles):
                span = slice(n * tile, (n + 1) * tile)
                copies[e, n].wait()
                d_hidden = lax.dot_general(
                    packed[e], held[e, n], LAST, preferred_element_type=jnp.float32
                )
                d_gate_ref[e, :, span] = (d_hidden * slope_ref[e, :, span]).astype(jnp.bfloat16)
                d_up_ref[e, :, span] = (d_hidden * act_ref[e, :, span]).astype(jnp.bfloat16)
        for s in range(count):
            inner = jnp.sum(
                part_refs[s][...].astype(jnp.float32) * out_ref[s].astype(jnp.float32),
                axis=1,
                keepdims=True,
            )
            spread = pick_ref[s].astype(jnp.float32) * inner
            sums = [
                jnp.sum(spread[e * half : (e + 1) * half], axis=0, keepdims=True)
                for e in range(2)
            ]
            token_ref[source_at(s, ids_ref[1], count)] = jnp.concatenate(sums, axis=0)

    return call_kernel(
        kernel,
        [ids, *parts, outputs, pick, slope, activated, *down_mats],
        ["smem"] + ["vmem"] * (count + 4) + ["any"] * 2,
        [
            jax.ShapeDtypeStruct((2, total, units), jnp.bfloat16),
            jax.ShapeDtypeStruct((2, total, units), jnp.bfloat16),
            jax.ShapeDtypeStruct((count, 2, tokens), jnp.float32),
        ],
        [
            pltpu.VMEM((2, total, width), jnp.bfloat16),
            pltpu.VMEM((2, tiles, tile, width), jnp.bfloat16),
            pltpu.SemaphoreType.DMA((2, tiles)),
        ],
        4 * total * width * units,
        behind,
    )


def run_d_copy(d_pre_gate, d_pre_up, gate_mats, up_mats, count, behind):
    _, total, units = d_pre_gate.shape
    width = gate_mats[0].shape[0]
    half = total // count
    tile = cut(width, 512)
    tiles = width // tile

    def kernel(d_gate_ref, d_up_ref, *refs):
        mats = refs[:4]
        out_ref, held, sems = refs[4:]
        copies = {}
        for e in range(2):
            for n in range(tiles):
                for m in range(2):
                    copies[e, n, m] = pltpu.make_async_copy(
                        mats[2 * m + e].at[n * tile : (n + 1) * tile, :],
                        held.at[e, n, m],
                        sems.at[e, n, m],
                    )
                    copies[e, n, m].start()
        for e in range(2):
            for n in range(tiles):
                copies[e, n, 0].wait()
                out = lax.dot_general(
                    d_gate_ref[e], held[e, n, 0], LAST, preferred_element_type=jnp.float32
                )
                copies[e, n, 1].wait()
                out = out + lax.dot_general(
                    d_up_ref[e], held[e, n, 1], LAST, preferred_element_type=jnp.float32
                )
                out_ref[:, e * half : (e + 1) * half, n * tile : (n + 1) * tile] = (
                    out.astype(jnp.bfloat16).reshape(count, half, tile)
                )

    return call_kernel(
        kernel,
        [d_pre_gate, d_pre_up, *gate_mats, *up_mats],
        ["vmem", "vmem"] + ["any"] * 4,
        [jax.ShapeDtypeStruct((count, 2 * half, width), jnp.bfloat16)],
        [
            pltpu.VMEM((2, tiles, 2, tile, units), jnp.bfloat16),
            pltpu.SemaphoreType.DMA((2, tiles, 2)),
        ],
        8 * total * width * units,
        behind,
    )[0]


def swap_cores(array):
    return lax.ppermute(array, "grp", [(0, 1), (1, 0)])


def body_ring(tokens, cotangent, routes, gates, w_gate, w_up, w_down):
    token_count = tokens.shape[0]
    width = tokens.shape[1]
    top_count = routes.shape[1]
    chips = lax.axis_size("ep")
    expert_count = lax.axis_size(("grp", "ep"))
    capacity = max(2, 3 * token_count * top_count // (2 * expert_count))
    f32, bf16 = jnp.float32, jnp.bfloat16

    core = lax.axis_index("grp")
    chip = lax.axis_index("ep")
    ids = jnp.stack([core, chip]).astype(jnp.int32)
    table = jnp.concatenate([routes.astype(f32), gates.astype(f32)], axis=1).T
    copies = jnp.broadcast_to(table[None], (chips,) + table.shape)
    tables = lax.all_to_all(copies, "ep", split_axis=0, concat_axis=0, tiled=True)
    pick, spread = run_routing(ids, tables, top_count, capacity)

    gate_mats = (w_gate[0], swap_cores(w_gate[0]))
    up_mats = (w_up[0], swap_cores(w_up[0]))
    down_mats = (w_down[0], swap_cores(w_down[0]))

    def rows_of(s, held):
        buffer, row = held
        return jnp.dot(
            pick[s], buffer[row : row + token_count], preferred_element_type=f32
        ).astype(bf16)

    def gather_rows(held):
        return [rows_of(s, at) for s, at in enumerate(held)]

    in_held, grad_held = ring_gather(
        tokens, cotangent, chips, (tables, gate_mats[1], up_mats[1]), rows_of
    )

    def scatter_rows(blocks):
        def share_of(s, partial, waits=(), add_waits=False):
            total = lax.dot_general(
                spread[s], blocks[s], (((0,), (0,)), ((), ())), preferred_element_type=f32
            )
            if partial is not None:
                total = total + partial.astype(f32)
            if add_waits:
                return (total + waits[0].astype(f32)).astype(bf16)
            return after(total.astype(bf16), *waits)

        return share_of

    rows_in = gather_rows(in_held)
    hidden, slope, activated = run_hidden(rows_in, gate_mats, up_mats)
    outputs = run_down(hidden, down_mats, chips)
    rows_grad = gather_rows(grad_held)
    d_pre_gate, d_pre_up, per_token = run_d_hidden(
        ids, rows_grad, outputs, pick, slope, activated, down_mats, ()
    )
    behind = {(step, 1): (per_token,) for step in (1, -1)}
    mixed, mixed_hops = ring_reduce(scatter_rows(outputs), chips, 1, behind)
    d_copies = run_d_copy(
        d_pre_gate, d_pre_up, gate_mats, up_mats, chips, [mixed_hops[step][0] for step in (1, -1)]
    )

    returned = lax.all_to_all(per_token, "ep", split_axis=0, concat_axis=0, tiled=True)
    behind = {
        (step, hop): (mixed_hops[step][hop + 1],)
        for step in (1, -1)
        for hop in range(len(mixed_hops[step]) - 1)
    }
    d_tokens, _ = ring_reduce(scatter_rows(d_copies), chips, -1, behind)
    chip_ids = jnp.arange(chips, dtype=jnp.int32)
    served = jnp.stack([core * chips + chip_ids, (1 - core) * chips + chip_ids], axis=1)
    chosen = routes.T[None, None] == served[:, :, None, None]
    d_gates = jnp.sum(jnp.where(chosen, returned[:, :, None, :], 0.0), axis=(0, 1)).T
    return (mixed, d_tokens, d_gates)


def solution(mesh):
    plan = body_ring if 4 <= mesh.shape["ep"] <= 8 and mesh.shape["grp"] == 2 else body_exchange
    return jax.shard_map(
        plan,
        mesh=mesh,
        in_specs=(
            P(("rep", "grp", "ep"), None),
            P(("rep", "grp", "ep"), None),
            P(("rep", "grp", "ep"), None),
            P(("rep", "grp", "ep"), None),
            P(("grp", "ep"), None, None),
            P(("grp", "ep"), None, None),
            P(("grp", "ep"), None, None),
        ),
        out_specs=(
            P(("rep", "grp", "ep"), None),
            P(("rep", "grp", "ep"), None),
            P(("rep", "grp", "ep"), None),
        ),
        check_vma=False,
    )
```

```python
import jax
import jax.numpy as jnp
from jax import lax
from jax.experimental import pallas as pl
from jax.experimental.pallas import tpu as pltpu
from jax.sharding import PartitionSpec as P


def expert_pass(rows_in, rows_grad, gate_mat, up_mat, down_mat):
    pre_gate = jnp.dot(rows_in, gate_mat, preferred_element_type=jnp.float32)
    pre_up = jnp.dot(rows_in, up_mat, preferred_element_type=jnp.float32)
    activated = jax.nn.silu(pre_gate)
    hidden = (activated * pre_up).astype(jnp.bfloat16)
    outputs = jnp.dot(hidden, down_mat, preferred_element_type=jnp.float32).astype(jnp.bfloat16)
    d_hidden = lax.dot_general(
        rows_grad, down_mat, (((1,), (1,)), ((), ())), preferred_element_type=jnp.float32
    )
    sigma = jax.nn.sigmoid(pre_gate)
    d_pre_gate = (d_hidden * pre_up * sigma * (1.0 + pre_gate * (1.0 - sigma))).astype(jnp.bfloat16)
    d_pre_up = (d_hidden * activated).astype(jnp.bfloat16)
    both_pre = jnp.concatenate([d_pre_gate, d_pre_up], axis=1)
    both_mats = jnp.concatenate([gate_mat, up_mat], axis=1)
    d_copy = lax.dot_general(
        both_pre, both_mats, (((1,), (1,)), ((), ())), preferred_element_type=jnp.float32
    )
    return (outputs, d_copy.astype(jnp.bfloat16))


def run_items(pieces, gate_mat, up_mat, down_mat):
    rows_in, rows_grad = pieces
    lead_shape = rows_in.shape[:2]
    width = rows_in.shape[2]
    outputs, d_copy = expert_pass(
        rows_in.reshape(-1, width), rows_grad.reshape(-1, width), gate_mat, up_mat, down_mat
    )
    return (outputs.reshape(lead_shape + (width,)), d_copy.reshape(lead_shape + (width,)))


def ranks_of(chosen_hot):
    running = jnp.cumsum(chosen_hot, axis=-2)
    return jnp.sum(chosen_hot * running, axis=-1) - 1


def body_exchange(tokens, cotangent, routes, gates, w_gate, w_up, w_down):
    token_count = tokens.shape[0]
    width = tokens.shape[1]
    top_count = routes.shape[1]
    copy_count = token_count * top_count
    gate_mat = w_gate[0]
    up_mat = w_up[0]
    down_mat = w_down[0]
    expert_count = lax.axis_size(("grp", "ep"))
    capacity = max(2, 3 * token_count * top_count // (2 * expert_count))
    flat_experts = routes.reshape(-1)
    chosen_hot = (
        flat_experts[:, None] == jnp.arange(expert_count, dtype=jnp.int32)[None, :]
    ).astype(jnp.int32)
    slot_of = flat_experts * capacity + ranks_of(chosen_hot)
    token_of = jnp.arange(copy_count, dtype=jnp.int32) // top_count
    slot_token = jnp.zeros((expert_count * capacity,), jnp.int32).at[slot_of].set(token_of)
    slot_live = jnp.zeros((expert_count * capacity,), jnp.bool_).at[slot_of].set(True)
    send_in = jnp.where(
        slot_live[:, None], tokens[slot_token], jnp.zeros((), tokens.dtype)
    ).reshape(expert_count, capacity, width)
    send_grad = jnp.where(
        slot_live[:, None], cotangent[slot_token], jnp.zeros((), cotangent.dtype)
    ).reshape(expert_count, capacity, width)
    outputs, d_copy = run_items(
        (
            lax.all_to_all(send_in, ("grp", "ep"), split_axis=0, concat_axis=0, tiled=True),
            lax.all_to_all(send_grad, ("grp", "ep"), split_axis=0, concat_axis=0, tiled=True),
        ),
        gate_mat,
        up_mat,
        down_mat,
    )
    back_out = lax.all_to_all(outputs, ("grp", "ep"), split_axis=0, concat_axis=0, tiled=True)
    back_grad = lax.all_to_all(d_copy, ("grp", "ep"), split_axis=0, concat_axis=0, tiled=True)
    copy_out = back_out.reshape(-1, width)[slot_of].reshape(token_count, top_count, width)
    copy_grad = back_grad.reshape(-1, width)[slot_of].reshape(token_count, top_count, width)
    weight = gates.astype(jnp.float32)
    mixed = jnp.sum(weight[:, :, None] * copy_out.astype(jnp.float32), axis=1)
    d_tokens = jnp.sum(weight[:, :, None] * copy_grad.astype(jnp.float32), axis=1)
    d_gates = jnp.einsum("tkd,td->tk", copy_out, cotangent, preferred_element_type=jnp.float32)
    return (mixed.astype(jnp.bfloat16), d_tokens.astype(jnp.bfloat16), d_gates)


def ring_order(count):
    return list(range(0, count, 2)) + list(range(count - 1, 0, -2))


def ring_shift(array, count, step):
    order = ring_order(count)
    pairs = [(order[i], order[(i + step) % count]) for i in range(count)]
    return lax.ppermute(array, "ep", pairs)


def ring_gather(shard, count, far_step, behind={}):
    held = {0: shard}
    arrivals = {}
    for step in (far_step, -far_step):
        hops = count // 2 if step == far_step else (count - 1) // 2
        moving = shard
        arrivals[step] = []
        for hop in range(1, hops + 1):
            if (step, hop) in behind:
                moving = held_back(moving, behind[step, hop])
                if hop > 1:
                    held[(-step * (hop - 1)) % count] = moving
            moving = ring_shift(moving, count, step)
            held[(-step * hop) % count] = moving
            arrivals[step].append(moving)
    return [held[place] for place in range(count)], arrivals


def after(array, *others):
    for other in others:
        array = array + other[(slice(0, 1),) * other.ndim].reshape((1,) * array.ndim).astype(array.dtype) * 0
    return array


def held_back(array, others):
    def kernel(*refs):
        pass

    return pl.pallas_call(
        kernel,
        out_shape=jax.ShapeDtypeStruct(array.shape, array.dtype),
        in_specs=[pl.BlockSpec(memory_space=pltpu.HBM) for _ in range(1 + len(others))],
        out_specs=pl.BlockSpec(memory_space=pltpu.HBM),
        input_output_aliases={0: 0},
    )(array, *others)


def ring_reduce(share_of, count, far_step, behind={}):
    arrived = {}
    for step in (far_step, -far_step):
        hops = count // 2 if step == far_step else (count - 1) // 2
        moving = None
        steps = []
        for hop in range(hops, 0, -1):
            waits = behind.get((step, hops - hop), ())
            share = share_of((step * hop) % count, moving, waits)
            moving = ring_shift(share, count, step)
            steps.append(moving)
        arrived[step] = steps
    total = share_of(0, arrived[far_step][-1], (arrived[-far_step][-1],), True)
    return total, arrived


VMEM_LIMIT = 48 * 1024 * 1024
LAST = (((1,), (1,)), ((), ()))


def cut(size, most):
    return max(w for w in range(128, most + 1, 128) if size % w == 0)


def call_kernel(kernel, operands, kinds, outs, scratch, flops, behind=()):
    spaces = {"any": pltpu.HBM, "vmem": pltpu.VMEM, "smem": pltpu.SMEM}
    count = len(operands)
    operands = [*operands, *behind]
    kinds = [*kinds, *["any" for _ in behind]]

    def body(*refs):
        kernel(*refs[:count], *refs[len(operands) :])

    return pl.pallas_call(
        body,
        out_shape=outs,
        in_specs=[pl.BlockSpec(memory_space=spaces[k]) for k in kinds],
        out_specs=[pl.BlockSpec(memory_space=pltpu.VMEM) for _ in outs],
        scratch_shapes=scratch,
        compiler_params=pltpu.CompilerParams(vmem_limit_bytes=VMEM_LIMIT),
        cost_estimate=pl.CostEstimate(flops=flops, bytes_accessed=1 << 20, transcendentals=0),
    )(*operands)


def pack_rows(parts, packed):
    half = parts[0].shape[0] // 2
    for e in range(2):
        for s, part in enumerate(parts):
            packed[e, s * half : (s + 1) * half, :] = part[e * half : (e + 1) * half, :]


def source_at(distance, chip, count):
    place = jnp.where(chip % 2 == 0, chip // 2, count - (chip + 1) // 2)
    place = (place + distance) % count
    return jnp.where(place < count // 2, 2 * place, 2 * (count - place) - 1)


def run_hold(array, behind):
    def kernel(in_ref, out_ref):
        out_ref[...] = in_ref[...]

    shape = jax.ShapeDtypeStruct(array.shape, array.dtype)
    return call_kernel(kernel, [array], ["vmem"], [shape], [], 1, behind)[0]


def run_routing(ids, tables, top_count, capacity):
    count, _, tokens = tables.shape
    f32, bf16 = jnp.float32, jnp.bfloat16

    def kernel(ids_ref, table_ref, pick_ref, spread_ref):
        core, chip = ids_ref[0], ids_ref[1]
        first = lax.broadcasted_iota(jnp.int32, (tokens, tokens), 0)
        second = lax.broadcasted_iota(jnp.int32, (tokens, tokens), 1)
        before = (first <= second).astype(f32).astype(bf16)
        slot = lax.broadcasted_iota(jnp.int32, (capacity, tokens), 0).astype(f32)
        hits, weights = [], []
        for s in range(count):
            table = table_ref[source_at(s, chip, count)]
            for e in range(2):
                expert = jnp.where(core == e, chip, count + chip).astype(f32)
                hit = (table[:top_count] == expert).astype(f32)
                hits.append(jnp.sum(hit, axis=0, keepdims=True))
                weights.append(
                    jnp.sum(hit * table[top_count : 2 * top_count], axis=0, keepdims=True)
                )
        rank = jnp.dot(
            jnp.concatenate(hits, axis=0).astype(bf16), before, preferred_element_type=f32
        )
        for s in range(count):
            for e in range(2):
                i = 2 * s + e
                chosen = jnp.where(slot == rank[i : i + 1] - 1.0, hits[i], 0.0)
                span = slice(e * capacity, (e + 1) * capacity)
                pick_ref[s, span, :] = chosen.astype(bf16)
                spread_ref[s, span, :] = (chosen * weights[i]).astype(bf16)

    shape = jax.ShapeDtypeStruct((count, 2 * capacity, tokens), bf16)
    return call_kernel(kernel, [ids, tables], ["smem", "vmem"], [shape, shape], [], 1 << 20)


def run_hidden(parts, gate_mats, up_mats):
    count, rows, width = len(parts), parts[0].shape[0], parts[0].shape[1]
    units = gate_mats[0].shape[1]
    total = count * rows // 2
    tile = cut(units, 256)
    tiles = units // tile

    def kernel(*refs):
        part_refs, mats = refs[:count], refs[count : count + 4]
        hidden_ref, slope_ref, act_ref, packed, held, sems = refs[count + 4 :]
        copies = {}
        for e in range(2):
            for m in range(2):
                copies[e, m] = pltpu.make_async_copy(
                    mats[2 * m + e], held.at[e, m], sems.at[e, m]
                )
                copies[e, m].start()
        pack_rows(part_refs, packed)
        for e in range(2):
            for m in range(2):
                copies[e, m].wait()
            for n in range(tiles):
                span = slice(n * tile, (n + 1) * tile)
                gate = jnp.dot(packed[e], held[e, 0, :, span], preferred_element_type=jnp.float32)
                up = jnp.dot(packed[e], held[e, 1, :, span], preferred_element_type=jnp.float32)
                sigma = 1.0 / (1.0 + jnp.exp(-gate))
                act = gate * sigma
                hidden_ref[e, :, span] = (act * up).astype(jnp.bfloat16)
                slope_ref[e, :, span] = up * sigma * (1.0 + gate * (1.0 - sigma))
                act_ref[e, :, span] = act

    return call_kernel(
        kernel,
        [*parts, *gate_mats, *up_mats],
        ["vmem"] * count + ["any"] * 4,
        [
            jax.ShapeDtypeStruct((2, total, units), jnp.bfloat16),
            jax.ShapeDtypeStruct((2, total, units), jnp.float32),
            jax.ShapeDtypeStruct((2, total, units), jnp.float32),
        ],
        [
            pltpu.VMEM((2, total, width), jnp.bfloat16),
            pltpu.VMEM((2, 2, width, units), jnp.bfloat16),
            pltpu.SemaphoreType.DMA((2, 2)),
        ],
        8 * total * width * units,
    )


def run_down(hidden, down_mats, count):
    _, total, units = hidden.shape
    width = down_mats[0].shape[1]
    half = total // count
    tile = cut(width, 512)
    tiles = width // tile

    def kernel(hidden_ref, own_ref, other_ref, out_ref, held, sems):
        copies = {}
        for e, mat in enumerate((own_ref, other_ref)):
            copies[e] = pltpu.make_async_copy(mat, held.at[e], sems.at[e])
            copies[e].start()
        for e in range(2):
            copies[e].wait()
            for n in range(tiles):
                columns = held[e, :, n * tile : (n + 1) * tile]
                out = jnp.dot(hidden_ref[e], columns, preferred_element_type=jnp.float32)
                out_ref[:, e * half : (e + 1) * half, n * tile : (n + 1) * tile] = (
                    out.astype(jnp.bfloat16).reshape(count, half, tile)
                )

    return call_kernel(
        kernel,
        [hidden, *down_mats],
        ["vmem", "any", "any"],
        [jax.ShapeDtypeStruct((count, 2 * half, width), jnp.bfloat16)],
        [
            pltpu.VMEM((2, units, width), jnp.bfloat16),
            pltpu.SemaphoreType.DMA((2,)),
        ],
        4 * total * width * units,
    )[0]


def run_d_hidden(ids, parts, outputs, pick, slope, activated, down_mats, behind):
    count, rows, width = len(parts), parts[0].shape[0], parts[0].shape[1]
    half = rows // 2
    _, total, units = slope.shape
    tile = cut(units, 256)
    tiles = units // tile
    tokens = pick.shape[2]

    def kernel(*refs):
        ids_ref, refs = refs[0], refs[1:]
        part_refs = refs[:count]
        out_ref, pick_ref, slope_ref, act_ref, own_ref, other_ref = refs[count : count + 6]
        d_gate_ref, d_up_ref, token_ref, packed, held, sems = refs[count + 6 :]
        copies = {}
        for e, mat in enumerate((own_ref, other_ref)):
            for n in range(tiles):
                copies[e, n] = pltpu.make_async_copy(
                    mat.at[n * tile : (n + 1) * tile, :], held.at[e, n], sems.at[e, n]
                )
                copies[e, n].start()
        pack_rows(part_refs, packed)
        for e in range(2):
            for n in range(tiles):
                span = slice(n * tile, (n + 1) * tile)
                copies[e, n].wait()
                d_hidden = lax.dot_general(
                    packed[e], held[e, n], LAST, preferred_element_type=jnp.float32
                )
                d_gate_ref[e, :, span] = (d_hidden * slope_ref[e, :, span]).astype(jnp.bfloat16)
                d_up_ref[e, :, span] = (d_hidden * act_ref[e, :, span]).astype(jnp.bfloat16)
        for s in range(count):
            inner = jnp.sum(
                part_refs[s][...].astype(jnp.float32) * out_ref[s].astype(jnp.float32),
                axis=1,
                keepdims=True,
            )
            spread = pick_ref[s].astype(jnp.float32) * inner
            sums = [
                jnp.sum(spread[e * half : (e + 1) * half], axis=0, keepdims=True)
                for e in range(2)
            ]
            token_ref[source_at(s, ids_ref[1], count)] = jnp.concatenate(sums, axis=0)

    return call_kernel(
        kernel,
        [ids, *parts, outputs, pick, slope, activated, *down_mats],
        ["smem"] + ["vmem"] * (count + 4) + ["any"] * 2,
        [
            jax.ShapeDtypeStruct((2, total, units), jnp.bfloat16),
            jax.ShapeDtypeStruct((2, total, units), jnp.bfloat16),
            jax.ShapeDtypeStruct((count, 2, tokens), jnp.float32),
        ],
        [
            pltpu.VMEM((2, total, width), jnp.bfloat16),
            pltpu.VMEM((2, tiles, tile, width), jnp.bfloat16),
            pltpu.SemaphoreType.DMA((2, tiles)),
        ],
        4 * total * width * units,
        behind,
    )


def run_d_copy(d_pre_gate, d_pre_up, gate_mats, up_mats, count, behind):
    _, total, units = d_pre_gate.shape
    width = gate_mats[0].shape[0]
    half = total // count
    tile = cut(width, 512)
    tiles = width // tile

    def kernel(d_gate_ref, d_up_ref, *refs):
        mats = refs[:4]
        out_ref, held, sems = refs[4:]
        copies = {}
        for e in range(2):
            for n in range(tiles):
                for m in range(2):
                    copies[e, n, m] = pltpu.make_async_copy(
                        mats[2 * m + e].at[n * tile : (n + 1) * tile, :],
                        held.at[e, n, m],
                        sems.at[e, n, m],
                    )
                    copies[e, n, m].start()
        for e in range(2):
            for n in range(tiles):
                copies[e, n, 0].wait()
                out = lax.dot_general(
                    d_gate_ref[e], held[e, n, 0], LAST, preferred_element_type=jnp.float32
                )
                copies[e, n, 1].wait()
                out = out + lax.dot_general(
                    d_up_ref[e], held[e, n, 1], LAST, preferred_element_type=jnp.float32
                )
                out_ref[:, e * half : (e + 1) * half, n * tile : (n + 1) * tile] = (
                    out.astype(jnp.bfloat16).reshape(count, half, tile)
                )

    return call_kernel(
        kernel,
        [d_pre_gate, d_pre_up, *gate_mats, *up_mats],
        ["vmem", "vmem"] + ["any"] * 4,
        [jax.ShapeDtypeStruct((count, 2 * half, width), jnp.bfloat16)],
        [
            pltpu.VMEM((2, tiles, 2, tile, units), jnp.bfloat16),
            pltpu.SemaphoreType.DMA((2, tiles, 2)),
        ],
        8 * total * width * units,
        behind,
    )[0]


def swap_cores(array):
    return lax.ppermute(array, "grp", [(0, 1), (1, 0)])


def body_ring(tokens, cotangent, routes, gates, w_gate, w_up, w_down):
    token_count = tokens.shape[0]
    width = tokens.shape[1]
    top_count = routes.shape[1]
    chips = lax.axis_size("ep")
    expert_count = lax.axis_size(("grp", "ep"))
    capacity = max(2, 3 * token_count * top_count // (2 * expert_count))
    f32, bf16 = jnp.float32, jnp.bfloat16

    core = lax.axis_index("grp")
    chip = lax.axis_index("ep")
    ids = jnp.stack([core, chip]).astype(jnp.int32)
    table = jnp.concatenate([routes.astype(f32), gates.astype(f32)], axis=1).T
    copies = jnp.broadcast_to(table[None], (chips,) + table.shape)
    tables = lax.all_to_all(copies, "ep", split_axis=0, concat_axis=0, tiled=True)
    pick, spread = run_routing(ids, tables, top_count, capacity)

    gate_mats = (w_gate[0], swap_cores(w_gate[0]))
    up_mats = (w_up[0], swap_cores(w_up[0]))
    down_mats = (w_down[0], swap_cores(w_down[0]))
    swapped = (gate_mats[1], up_mats[1], down_mats[1])

    behind = {(step, 2): (tables,) for step in (1, -1)}
    behind.update({(step, 3): swapped for step in (1, -1)})
    in_shards, in_hops = ring_gather(tokens, chips, 1, behind)
    grad_later = run_hold(cotangent, (in_hops[1][1], in_hops[-1][1], *swapped))
    grad_shards, _ = ring_gather(grad_later, chips, -1)

    def gather_rows(shards):
        return [
            jnp.dot(pick[s], shards[s], preferred_element_type=f32).astype(bf16)
            for s in range(chips)
        ]

    def scatter_rows(blocks):
        def share_of(s, partial, waits=(), add_waits=False):
            total = lax.dot_general(
                spread[s], blocks[s], (((0,), (0,)), ((), ())), preferred_element_type=f32
            )
            if partial is not None:
                total = total + partial.astype(f32)
            if add_waits:
                return (total + waits[0].astype(f32)).astype(bf16)
            return after(total.astype(bf16), *waits)

        return share_of

    rows_in = gather_rows(in_shards)
    hidden, slope, activated = run_hidden(rows_in, gate_mats, up_mats)
    outputs = run_down(hidden, down_mats, chips)
    rows_grad = gather_rows(grad_shards)
    d_pre_gate, d_pre_up, per_token = run_d_hidden(
        ids, rows_grad, outputs, pick, slope, activated, down_mats, ()
    )
    mixed, mixed_hops = ring_reduce(scatter_rows(outputs), chips, 1)
    d_copies = run_d_copy(
        d_pre_gate, d_pre_up, gate_mats, up_mats, chips, [mixed_hops[step][1] for step in (1, -1)]
    )

    returned = lax.all_to_all(per_token, "ep", split_axis=0, concat_axis=0, tiled=True)
    behind = {
        (step, hop): (mixed_hops[step][hop + 1],)
        for step in (1, -1)
        for hop in range(len(mixed_hops[step]) - 1)
    }
    d_tokens, _ = ring_reduce(scatter_rows(d_copies), chips, -1, behind)
    chip_ids = jnp.arange(chips, dtype=jnp.int32)
    served = jnp.stack([core * chips + chip_ids, (1 - core) * chips + chip_ids], axis=1)
    chosen = routes.T[None, None] == served[:, :, None, None]
    d_gates = jnp.sum(jnp.where(chosen, returned[:, :, None, :], 0.0), axis=(0, 1)).T
    return (mixed, d_tokens, d_gates)


def solution(mesh):
    plan = body_ring if mesh.shape["ep"] <= 8 and mesh.shape["grp"] == 2 else body_exchange
    return jax.shard_map(
        plan,
        mesh=mesh,
        in_specs=(
            P(("rep", "grp", "ep"), None),
            P(("rep", "grp", "ep"), None),
            P(("rep", "grp", "ep"), None),
            P(("rep", "grp", "ep"), None),
            P(("grp", "ep"), None, None),
            P(("grp", "ep"), None, None),
            P(("grp", "ep"), None, None),
        ),
        out_specs=(
            P(("rep", "grp", "ep"), None),
            P(("rep", "grp", "ep"), None),
            P(("rep", "grp", "ep"), None),
        ),
        check_vma=False,
    )
```

```python
import jax
import jax.numpy as jnp
from jax import lax
from jax.experimental import pallas as pl
from jax.experimental.pallas import tpu as pltpu
from jax.sharding import PartitionSpec as P


def expert_pass(rows_in, rows_grad, gate_mat, up_mat, down_mat):
    pre_gate = jnp.dot(rows_in, gate_mat, preferred_element_type=jnp.float32)
    pre_up = jnp.dot(rows_in, up_mat, preferred_element_type=jnp.float32)
    activated = jax.nn.silu(pre_gate)
    hidden = (activated * pre_up).astype(jnp.bfloat16)
    outputs = jnp.dot(hidden, down_mat, preferred_element_type=jnp.float32).astype(jnp.bfloat16)
    d_hidden = lax.dot_general(
        rows_grad, down_mat, (((1,), (1,)), ((), ())), preferred_element_type=jnp.float32
    )
    sigma = jax.nn.sigmoid(pre_gate)
    d_pre_gate = (d_hidden * pre_up * sigma * (1.0 + pre_gate * (1.0 - sigma))).astype(jnp.bfloat16)
    d_pre_up = (d_hidden * activated).astype(jnp.bfloat16)
    both_pre = jnp.concatenate([d_pre_gate, d_pre_up], axis=1)
    both_mats = jnp.concatenate([gate_mat, up_mat], axis=1)
    d_copy = lax.dot_general(
        both_pre, both_mats, (((1,), (1,)), ((), ())), preferred_element_type=jnp.float32
    )
    return (outputs, d_copy.astype(jnp.bfloat16))


def run_items(pieces, gate_mat, up_mat, down_mat):
    rows_in, rows_grad = pieces
    lead_shape = rows_in.shape[:2]
    width = rows_in.shape[2]
    outputs, d_copy = expert_pass(
        rows_in.reshape(-1, width), rows_grad.reshape(-1, width), gate_mat, up_mat, down_mat
    )
    return (outputs.reshape(lead_shape + (width,)), d_copy.reshape(lead_shape + (width,)))


def ranks_of(chosen_hot):
    running = jnp.cumsum(chosen_hot, axis=-2)
    return jnp.sum(chosen_hot * running, axis=-1) - 1


def body_exchange(tokens, cotangent, routes, gates, w_gate, w_up, w_down):
    token_count = tokens.shape[0]
    width = tokens.shape[1]
    top_count = routes.shape[1]
    copy_count = token_count * top_count
    gate_mat = w_gate[0]
    up_mat = w_up[0]
    down_mat = w_down[0]
    expert_count = lax.axis_size(("grp", "ep"))
    capacity = max(2, 3 * token_count * top_count // (2 * expert_count))
    flat_experts = routes.reshape(-1)
    chosen_hot = (
        flat_experts[:, None] == jnp.arange(expert_count, dtype=jnp.int32)[None, :]
    ).astype(jnp.int32)
    slot_of = flat_experts * capacity + ranks_of(chosen_hot)
    token_of = jnp.arange(copy_count, dtype=jnp.int32) // top_count
    slot_token = jnp.zeros((expert_count * capacity,), jnp.int32).at[slot_of].set(token_of)
    slot_live = jnp.zeros((expert_count * capacity,), jnp.bool_).at[slot_of].set(True)
    send_in = jnp.where(
        slot_live[:, None], tokens[slot_token], jnp.zeros((), tokens.dtype)
    ).reshape(expert_count, capacity, width)
    send_grad = jnp.where(
        slot_live[:, None], cotangent[slot_token], jnp.zeros((), cotangent.dtype)
    ).reshape(expert_count, capacity, width)
    outputs, d_copy = run_items(
        (
            lax.all_to_all(send_in, ("grp", "ep"), split_axis=0, concat_axis=0, tiled=True),
            lax.all_to_all(send_grad, ("grp", "ep"), split_axis=0, concat_axis=0, tiled=True),
        ),
        gate_mat,
        up_mat,
        down_mat,
    )
    back_out = lax.all_to_all(outputs, ("grp", "ep"), split_axis=0, concat_axis=0, tiled=True)
    back_grad = lax.all_to_all(d_copy, ("grp", "ep"), split_axis=0, concat_axis=0, tiled=True)
    copy_out = back_out.reshape(-1, width)[slot_of].reshape(token_count, top_count, width)
    copy_grad = back_grad.reshape(-1, width)[slot_of].reshape(token_count, top_count, width)
    weight = gates.astype(jnp.float32)
    mixed = jnp.sum(weight[:, :, None] * copy_out.astype(jnp.float32), axis=1)
    d_tokens = jnp.sum(weight[:, :, None] * copy_grad.astype(jnp.float32), axis=1)
    d_gates = jnp.einsum("tkd,td->tk", copy_out, cotangent, preferred_element_type=jnp.float32)
    return (mixed.astype(jnp.bfloat16), d_tokens.astype(jnp.bfloat16), d_gates)


def ring_order(count):
    return list(range(0, count, 2)) + list(range(count - 1, 0, -2))


def ring_shift(array, count, step):
    order = ring_order(count)
    pairs = [(order[i], order[(i + step) % count]) for i in range(count)]
    return lax.ppermute(array, "ep", pairs)


def ring_gather(shard, count, far_step, behind={}):
    held = {0: shard}
    arrivals = {}
    for step in (far_step, -far_step):
        hops = count // 2 if step == far_step else (count - 1) // 2
        moving = shard
        arrivals[step] = []
        for hop in range(1, hops + 1):
            if (step, hop) in behind:
                moving = held_back(moving, behind[step, hop])
                if hop > 1:
                    held[(-step * (hop - 1)) % count] = moving
            moving = ring_shift(moving, count, step)
            held[(-step * hop) % count] = moving
            arrivals[step].append(moving)
    return [held[place] for place in range(count)], arrivals


def after(array, *others):
    for other in others:
        array = array + other[(slice(0, 1),) * other.ndim].reshape((1,) * array.ndim).astype(array.dtype) * 0
    return array


def held_back(array, others):
    def kernel(*refs):
        pass

    return pl.pallas_call(
        kernel,
        out_shape=jax.ShapeDtypeStruct(array.shape, array.dtype),
        in_specs=[pl.BlockSpec(memory_space=pl.ANY) for _ in range(1 + len(others))],
        out_specs=pl.BlockSpec(memory_space=pl.ANY),
        input_output_aliases={0: 0},
    )(array, *others)


def ring_reduce(share_of, count, far_step, behind={}):
    arrived = {}
    for step in (far_step, -far_step):
        hops = count // 2 if step == far_step else (count - 1) // 2
        moving = None
        steps = []
        for hop in range(hops, 0, -1):
            waits = behind.get((step, hops - hop), ())
            share = share_of((step * hop) % count, moving, waits)
            moving = ring_shift(share, count, step)
            steps.append(moving)
        arrived[step] = steps
    total = share_of(0, arrived[far_step][-1], (arrived[-far_step][-1],), True)
    return total, arrived


VMEM_LIMIT = 48 * 1024 * 1024
LAST = (((1,), (1,)), ((), ()))


def cut(size, most):
    return max(w for w in range(128, most + 1, 128) if size % w == 0)


def call_kernel(kernel, operands, kinds, outs, scratch, flops, behind=()):
    spaces = {"any": pltpu.HBM, "vmem": pltpu.VMEM, "smem": pltpu.SMEM}
    count = len(operands)
    operands = [*operands, *behind]
    kinds = [*kinds, *["any" for _ in behind]]

    def body(*refs):
        kernel(*refs[:count], *refs[len(operands) :])

    return pl.pallas_call(
        body,
        out_shape=outs,
        in_specs=[pl.BlockSpec(memory_space=spaces[k]) for k in kinds],
        out_specs=[pl.BlockSpec(memory_space=pltpu.VMEM) for _ in outs],
        scratch_shapes=scratch,
        compiler_params=pltpu.CompilerParams(vmem_limit_bytes=VMEM_LIMIT),
        cost_estimate=pl.CostEstimate(flops=flops, bytes_accessed=1 << 20, transcendentals=0),
    )(*operands)


def pack_rows(parts, packed):
    half = parts[0].shape[0] // 2
    for e in range(2):
        for s, part in enumerate(parts):
            packed[e, s * half : (s + 1) * half, :] = part[e * half : (e + 1) * half, :]


def source_at(distance, chip, count):
    place = jnp.where(chip % 2 == 0, chip // 2, count - (chip + 1) // 2)
    place = (place + distance) % count
    return jnp.where(place < count // 2, 2 * place, 2 * (count - place) - 1)


def run_hold(array, behind):
    def kernel(in_ref, out_ref):
        out_ref[...] = in_ref[...]

    shape = jax.ShapeDtypeStruct(array.shape, array.dtype)
    return call_kernel(kernel, [array], ["vmem"], [shape], [], 1, behind)[0]


def run_routing(ids, tables, top_count, capacity):
    count, _, tokens = tables.shape
    f32, bf16 = jnp.float32, jnp.bfloat16

    def kernel(ids_ref, table_ref, pick_ref, spread_ref):
        core, chip = ids_ref[0], ids_ref[1]
        first = lax.broadcasted_iota(jnp.int32, (tokens, tokens), 0)
        second = lax.broadcasted_iota(jnp.int32, (tokens, tokens), 1)
        before = (first <= second).astype(f32).astype(bf16)
        slot = lax.broadcasted_iota(jnp.int32, (capacity, tokens), 0).astype(f32)
        hits, weights = [], []
        for s in range(count):
            table = table_ref[source_at(s, chip, count)]
            for e in range(2):
                expert = jnp.where(core == e, chip, count + chip).astype(f32)
                hit = (table[:top_count] == expert).astype(f32)
                hits.append(jnp.sum(hit, axis=0, keepdims=True))
                weights.append(
                    jnp.sum(hit * table[top_count : 2 * top_count], axis=0, keepdims=True)
                )
        rank = jnp.dot(
            jnp.concatenate(hits, axis=0).astype(bf16), before, preferred_element_type=f32
        )
        for s in range(count):
            for e in range(2):
                i = 2 * s + e
                chosen = jnp.where(slot == rank[i : i + 1] - 1.0, hits[i], 0.0)
                span = slice(e * capacity, (e + 1) * capacity)
                pick_ref[s, span, :] = chosen.astype(bf16)
                spread_ref[s, span, :] = (chosen * weights[i]).astype(bf16)

    shape = jax.ShapeDtypeStruct((count, 2 * capacity, tokens), bf16)
    return call_kernel(kernel, [ids, tables], ["smem", "vmem"], [shape, shape], [], 1 << 20)


def run_hidden(parts, gate_mats, up_mats, behind):
    count, rows, width = len(parts), parts[0].shape[0], parts[0].shape[1]
    units = gate_mats[0].shape[1]
    total = count * rows // 2
    tile = cut(units, 256)
    tiles = units // tile

    def kernel(*refs):
        part_refs, mats = refs[:count], refs[count : count + 4]
        hidden_ref, slope_ref, act_ref, packed, held, sems = refs[count + 4 :]
        copies = {}
        for e in range(2):
            for m in range(2):
                copies[e, m] = pltpu.make_async_copy(
                    mats[2 * m + e], held.at[e, m], sems.at[e, m]
                )
                copies[e, m].start()
        pack_rows(part_refs, packed)
        for e in range(2):
            for m in range(2):
                copies[e, m].wait()
            for n in range(tiles):
                span = slice(n * tile, (n + 1) * tile)
                gate = jnp.dot(packed[e], held[e, 0, :, span], preferred_element_type=jnp.float32)
                up = jnp.dot(packed[e], held[e, 1, :, span], preferred_element_type=jnp.float32)
                sigma = 1.0 / (1.0 + jnp.exp(-gate))
                act = gate * sigma
                hidden_ref[e, :, span] = (act * up).astype(jnp.bfloat16)
                slope_ref[e, :, span] = up * sigma * (1.0 + gate * (1.0 - sigma))
                act_ref[e, :, span] = act

    return call_kernel(
        kernel,
        [*parts, *gate_mats, *up_mats],
        ["vmem"] * count + ["any"] * 4,
        [
            jax.ShapeDtypeStruct((2, total, units), jnp.bfloat16),
            jax.ShapeDtypeStruct((2, total, units), jnp.float32),
            jax.ShapeDtypeStruct((2, total, units), jnp.float32),
        ],
        [
            pltpu.VMEM((2, total, width), jnp.bfloat16),
            pltpu.VMEM((2, 2, width, units), jnp.bfloat16),
            pltpu.SemaphoreType.DMA((2, 2)),
        ],
        8 * total * width * units,
        behind,
    )


def run_down(hidden, down_mats, count, behind):
    _, total, units = hidden.shape
    width = down_mats[0].shape[1]
    half = total // count
    tile = cut(width, 512)
    tiles = width // tile

    def kernel(hidden_ref, own_ref, other_ref, out_ref, held, sems):
        copies = {}
        for e, mat in enumerate((own_ref, other_ref)):
            copies[e] = pltpu.make_async_copy(mat, held.at[e], sems.at[e])
            copies[e].start()
        for e in range(2):
            copies[e].wait()
            for n in range(tiles):
                columns = held[e, :, n * tile : (n + 1) * tile]
                out = jnp.dot(hidden_ref[e], columns, preferred_element_type=jnp.float32)
                out_ref[:, e * half : (e + 1) * half, n * tile : (n + 1) * tile] = (
                    out.astype(jnp.bfloat16).reshape(count, half, tile)
                )

    return call_kernel(
        kernel,
        [hidden, *down_mats],
        ["vmem", "any", "any"],
        [jax.ShapeDtypeStruct((count, 2 * half, width), jnp.bfloat16)],
        [
            pltpu.VMEM((2, units, width), jnp.bfloat16),
            pltpu.SemaphoreType.DMA((2,)),
        ],
        4 * total * width * units,
        behind,
    )[0]


def run_d_hidden(parts, slope, activated, down_mats):
    count, rows, width = len(parts), parts[0].shape[0], parts[0].shape[1]
    _, total, units = slope.shape
    tile = cut(units, 256)
    tiles = units // tile

    def kernel(*refs):
        part_refs = refs[:count]
        slope_ref, act_ref, own_ref, other_ref = refs[count : count + 4]
        d_gate_ref, d_up_ref, packed, held, sems = refs[count + 4 :]
        copies = {}
        for e, mat in enumerate((own_ref, other_ref)):
            for n in range(tiles):
                copies[e, n] = pltpu.make_async_copy(
                    mat.at[n * tile : (n + 1) * tile, :], held.at[e, n], sems.at[e, n]
                )
                copies[e, n].start()
        pack_rows(part_refs, packed)
        for e in range(2):
            for n in range(tiles):
                span = slice(n * tile, (n + 1) * tile)
                copies[e, n].wait()
                d_hidden = lax.dot_general(
                    packed[e], held[e, n], LAST, preferred_element_type=jnp.float32
                )
                d_gate_ref[e, :, span] = (d_hidden * slope_ref[e, :, span]).astype(jnp.bfloat16)
                d_up_ref[e, :, span] = (d_hidden * act_ref[e, :, span]).astype(jnp.bfloat16)

    return call_kernel(
        kernel,
        [*parts, slope, activated, *down_mats],
        ["vmem"] * (count + 2) + ["any"] * 2,
        [jax.ShapeDtypeStruct((2, total, units), jnp.bfloat16)] * 2,
        [
            pltpu.VMEM((2, total, width), jnp.bfloat16),
            pltpu.VMEM((2, tiles, tile, width), jnp.bfloat16),
            pltpu.SemaphoreType.DMA((2, tiles)),
        ],
        4 * total * width * units,
    )


def run_d_gates(ids, parts, outputs, pick, behind):
    count, rows = len(parts), parts[0].shape[0]
    half = rows // 2
    tokens = pick.shape[2]

    def kernel(*refs):
        ids_ref, part_refs = refs[0], refs[1 : 1 + count]
        out_ref, pick_ref, token_ref = refs[1 + count :]
        for s in range(count):
            inner = jnp.sum(
                part_refs[s][...].astype(jnp.float32) * out_ref[s].astype(jnp.float32),
                axis=1,
                keepdims=True,
            )
            spread = pick_ref[s].astype(jnp.float32) * inner
            sums = [
                jnp.sum(spread[e * half : (e + 1) * half], axis=0, keepdims=True)
                for e in range(2)
            ]
            token_ref[source_at(s, ids_ref[1], count)] = jnp.concatenate(sums, axis=0)

    return call_kernel(
        kernel,
        [ids, *parts, outputs, pick],
        ["smem"] + ["vmem"] * (count + 2),
        [jax.ShapeDtypeStruct((count, 2, tokens), jnp.float32)],
        [],
        1 << 20,
        behind,
    )[0]


def run_d_copy(d_pre_gate, d_pre_up, gate_mats, up_mats, count, behind):
    _, total, units = d_pre_gate.shape
    width = gate_mats[0].shape[0]
    half = total // count
    tile = cut(width, 512)
    tiles = width // tile

    def kernel(d_gate_ref, d_up_ref, *refs):
        mats = refs[:4]
        out_ref, held, sems = refs[4:]
        copies = {}
        for e in range(2):
            for n in range(tiles):
                for m in range(2):
                    copies[e, n, m] = pltpu.make_async_copy(
                        mats[2 * m + e].at[n * tile : (n + 1) * tile, :],
                        held.at[e, n, m],
                        sems.at[e, n, m],
                    )
                    copies[e, n, m].start()
        for e in range(2):
            for n in range(tiles):
                copies[e, n, 0].wait()
                out = lax.dot_general(
                    d_gate_ref[e], held[e, n, 0], LAST, preferred_element_type=jnp.float32
                )
                copies[e, n, 1].wait()
                out = out + lax.dot_general(
                    d_up_ref[e], held[e, n, 1], LAST, preferred_element_type=jnp.float32
                )
                out_ref[:, e * half : (e + 1) * half, n * tile : (n + 1) * tile] = (
                    out.astype(jnp.bfloat16).reshape(count, half, tile)
                )

    return call_kernel(
        kernel,
        [d_pre_gate, d_pre_up, *gate_mats, *up_mats],
        ["vmem", "vmem"] + ["any"] * 4,
        [jax.ShapeDtypeStruct((count, 2 * half, width), jnp.bfloat16)],
        [
            pltpu.VMEM((2, tiles, 2, tile, units), jnp.bfloat16),
            pltpu.SemaphoreType.DMA((2, tiles, 2)),
        ],
        8 * total * width * units,
        behind,
    )[0]


def swap_cores(array):
    return lax.ppermute(array, "grp", [(0, 1), (1, 0)])


def body_ring(tokens, cotangent, routes, gates, w_gate, w_up, w_down):
    token_count = tokens.shape[0]
    width = tokens.shape[1]
    top_count = routes.shape[1]
    chips = lax.axis_size("ep")
    expert_count = lax.axis_size(("grp", "ep"))
    capacity = max(2, 3 * token_count * top_count // (2 * expert_count))
    f32, bf16 = jnp.float32, jnp.bfloat16

    core = lax.axis_index("grp")
    chip = lax.axis_index("ep")
    ids = jnp.stack([core, chip]).astype(jnp.int32)
    table = jnp.concatenate([routes.astype(f32), gates.astype(f32)], axis=1).T
    copies = jnp.broadcast_to(table[None], (chips,) + table.shape)
    tables = lax.all_to_all(copies, "ep", split_axis=0, concat_axis=0, tiled=True)
    pick, spread = run_routing(ids, tables, top_count, capacity)

    gate_mats = (w_gate[0], swap_cores(w_gate[0]))
    up_mats = (w_up[0], swap_cores(w_up[0]))
    down_mats = (w_down[0], swap_cores(w_down[0]))
    swapped = (gate_mats[1], up_mats[1], down_mats[1])

    behind = {(step, 2): (tables,) for step in (1, -1)}
    behind.update({(step, 3): swapped for step in (1, -1)})
    in_shards, in_hops = ring_gather(tokens, chips, 1, behind)
    grad_later = run_hold(cotangent, (in_hops[1][1], in_hops[-1][1], *swapped))
    grad_shards, grad_hops = ring_gather(grad_later, chips, -1)

    def gather_rows(shards):
        return [
            jnp.dot(pick[s], shards[s], preferred_element_type=f32).astype(bf16)
            for s in range(chips)
        ]

    def scatter_rows(blocks):
        def share_of(s, partial, waits=(), add_waits=False):
            total = lax.dot_general(
                spread[s], blocks[s], (((0,), (0,)), ((), ())), preferred_element_type=f32
            )
            if partial is not None:
                total = total + partial.astype(f32)
            if add_waits:
                return (total + waits[0].astype(f32)).astype(bf16)
            return after(total.astype(bf16), *waits)

        return share_of

    rows_in = gather_rows(in_shards)
    hidden, slope, activated = run_hidden(
        rows_in, gate_mats, up_mats, [grad_hops[step][1] for step in (1, -1)]
    )
    outputs = run_down(hidden, down_mats, chips, [grad_hops[step][2] for step in (1, -1)])
    rows_grad = gather_rows(grad_shards)
    d_pre_gate, d_pre_up = run_d_hidden(rows_grad, slope, activated, down_mats)
    behind = {(step, 1): (d_pre_gate,) for step in (1, -1)}
    mixed, mixed_hops = ring_reduce(scatter_rows(outputs), chips, 1, behind)
    d_copies = run_d_copy(
        d_pre_gate, d_pre_up, gate_mats, up_mats, chips, [mixed_hops[step][0] for step in (1, -1)]
    )

    per_token = run_d_gates(ids, rows_grad, outputs, pick, (d_pre_gate,))
    returned = lax.all_to_all(per_token, "ep", split_axis=0, concat_axis=0, tiled=True)
    behind = {
        (step, hop): (mixed_hops[step][hop + 1],)
        for step in (1, -1)
        for hop in range(len(mixed_hops[step]) - 1)
    }
    behind[-1, 1] += (per_token,)
    d_tokens, _ = ring_reduce(scatter_rows(d_copies), chips, -1, behind)
    chip_ids = jnp.arange(chips, dtype=jnp.int32)
    served = jnp.stack([core * chips + chip_ids, (1 - core) * chips + chip_ids], axis=1)
    chosen = routes.T[None, None] == served[:, :, None, None]
    d_gates = jnp.sum(jnp.where(chosen, returned[:, :, None, :], 0.0), axis=(0, 1)).T
    return (mixed, d_tokens, d_gates)


def solution(mesh):
    plan = body_ring if mesh.shape["ep"] <= 8 and mesh.shape["grp"] == 2 else body_exchange
    return jax.shard_map(
        plan,
        mesh=mesh,
        in_specs=(
            P(("rep", "grp", "ep"), None),
            P(("rep", "grp", "ep"), None),
            P(("rep", "grp", "ep"), None),
            P(("rep", "grp", "ep"), None),
            P(("grp", "ep"), None, None),
            P(("grp", "ep"), None, None),
            P(("grp", "ep"), None, None),
        ),
        out_specs=(
            P(("rep", "grp", "ep"), None),
            P(("rep", "grp", "ep"), None),
            P(("rep", "grp", "ep"), None),
        ),
        check_vma=False,
    )
```

```python
import jax
import jax.numpy as jnp
from jax import lax
from jax.experimental import pallas as pl
from jax.experimental.pallas import tpu as pltpu
from jax.sharding import PartitionSpec as P


def expert_pass(rows_in, rows_grad, gate_mat, up_mat, down_mat):
    pre_gate = jnp.dot(rows_in, gate_mat, preferred_element_type=jnp.float32)
    pre_up = jnp.dot(rows_in, up_mat, preferred_element_type=jnp.float32)
    activated = jax.nn.silu(pre_gate)
    hidden = (activated * pre_up).astype(jnp.bfloat16)
    outputs = jnp.dot(hidden, down_mat, preferred_element_type=jnp.float32).astype(jnp.bfloat16)
    d_hidden = lax.dot_general(
        rows_grad, down_mat, (((1,), (1,)), ((), ())), preferred_element_type=jnp.float32
    )
    sigma = jax.nn.sigmoid(pre_gate)
    d_pre_gate = (d_hidden * pre_up * sigma * (1.0 + pre_gate * (1.0 - sigma))).astype(jnp.bfloat16)
    d_pre_up = (d_hidden * activated).astype(jnp.bfloat16)
    both_pre = jnp.concatenate([d_pre_gate, d_pre_up], axis=1)
    both_mats = jnp.concatenate([gate_mat, up_mat], axis=1)
    d_copy = lax.dot_general(
        both_pre, both_mats, (((1,), (1,)), ((), ())), preferred_element_type=jnp.float32
    )
    return (outputs, d_copy.astype(jnp.bfloat16))


def run_items(pieces, gate_mat, up_mat, down_mat):
    rows_in, rows_grad = pieces
    lead_shape = rows_in.shape[:2]
    width = rows_in.shape[2]
    outputs, d_copy = expert_pass(
        rows_in.reshape(-1, width), rows_grad.reshape(-1, width), gate_mat, up_mat, down_mat
    )
    return (outputs.reshape(lead_shape + (width,)), d_copy.reshape(lead_shape + (width,)))


def ranks_of(chosen_hot):
    running = jnp.cumsum(chosen_hot, axis=-2)
    return jnp.sum(chosen_hot * running, axis=-1) - 1


def body_exchange(tokens, cotangent, routes, gates, w_gate, w_up, w_down):
    token_count = tokens.shape[0]
    width = tokens.shape[1]
    top_count = routes.shape[1]
    copy_count = token_count * top_count
    gate_mat = w_gate[0]
    up_mat = w_up[0]
    down_mat = w_down[0]
    expert_count = lax.axis_size(("grp", "ep"))
    capacity = max(2, 3 * token_count * top_count // (2 * expert_count))
    flat_experts = routes.reshape(-1)
    chosen_hot = (
        flat_experts[:, None] == jnp.arange(expert_count, dtype=jnp.int32)[None, :]
    ).astype(jnp.int32)
    slot_of = flat_experts * capacity + ranks_of(chosen_hot)
    token_of = jnp.arange(copy_count, dtype=jnp.int32) // top_count
    slot_token = jnp.zeros((expert_count * capacity,), jnp.int32).at[slot_of].set(token_of)
    slot_live = jnp.zeros((expert_count * capacity,), jnp.bool_).at[slot_of].set(True)
    send_in = jnp.where(
        slot_live[:, None], tokens[slot_token], jnp.zeros((), tokens.dtype)
    ).reshape(expert_count, capacity, width)
    send_grad = jnp.where(
        slot_live[:, None], cotangent[slot_token], jnp.zeros((), cotangent.dtype)
    ).reshape(expert_count, capacity, width)
    outputs, d_copy = run_items(
        (
            lax.all_to_all(send_in, ("grp", "ep"), split_axis=0, concat_axis=0, tiled=True),
            lax.all_to_all(send_grad, ("grp", "ep"), split_axis=0, concat_axis=0, tiled=True),
        ),
        gate_mat,
        up_mat,
        down_mat,
    )
    back_out = lax.all_to_all(outputs, ("grp", "ep"), split_axis=0, concat_axis=0, tiled=True)
    back_grad = lax.all_to_all(d_copy, ("grp", "ep"), split_axis=0, concat_axis=0, tiled=True)
    copy_out = back_out.reshape(-1, width)[slot_of].reshape(token_count, top_count, width)
    copy_grad = back_grad.reshape(-1, width)[slot_of].reshape(token_count, top_count, width)
    weight = gates.astype(jnp.float32)
    mixed = jnp.sum(weight[:, :, None] * copy_out.astype(jnp.float32), axis=1)
    d_tokens = jnp.sum(weight[:, :, None] * copy_grad.astype(jnp.float32), axis=1)
    d_gates = jnp.einsum("tkd,td->tk", copy_out, cotangent, preferred_element_type=jnp.float32)
    return (mixed.astype(jnp.bfloat16), d_tokens.astype(jnp.bfloat16), d_gates)


def ring_order(count):
    return list(range(0, count, 2)) + list(range(count - 1, 0, -2))


def ring_shift(array, count, step):
    order = ring_order(count)
    pairs = [(order[i], order[(i + step) % count]) for i in range(count)]
    return lax.ppermute(array, "ep", pairs)


def ring_gather(shard, count, far_step, behind={}):
    held = {0: shard}
    arrivals = {}
    for step in (far_step, -far_step):
        hops = count // 2 if step == far_step else (count - 1) // 2
        moving = shard
        arrivals[step] = []
        for hop in range(1, hops + 1):
            if (step, hop) in behind:
                moving = held_back(moving, behind[step, hop])
                if hop > 1:
                    held[(-step * (hop - 1)) % count] = moving
            moving = ring_shift(moving, count, step)
            held[(-step * hop) % count] = moving
            arrivals[step].append(moving)
    return [held[place] for place in range(count)], arrivals


def after(array, *others):
    for other in others:
        array = array + other[(slice(0, 1),) * other.ndim].reshape((1,) * array.ndim).astype(array.dtype) * 0
    return array


def held_back(array, others):
    def kernel(*refs):
        pass

    return pl.pallas_call(
        kernel,
        out_shape=jax.ShapeDtypeStruct(array.shape, array.dtype),
        in_specs=[pl.BlockSpec(memory_space=pl.ANY) for _ in range(1 + len(others))],
        out_specs=pl.BlockSpec(memory_space=pl.ANY),
        input_output_aliases={0: 0},
    )(array, *others)


def ring_reduce(share_of, count, far_step, behind={}):
    arrived = {}
    for step in (far_step, -far_step):
        hops = count // 2 if step == far_step else (count - 1) // 2
        moving = None
        steps = []
        for hop in range(hops, 0, -1):
            waits = behind.get((step, hops - hop), ())
            share = share_of((step * hop) % count, moving, waits)
            moving = ring_shift(share, count, step)
            steps.append(moving)
        arrived[step] = steps
    total = share_of(0, arrived[far_step][-1], (arrived[-far_step][-1],), True)
    return total, arrived


VMEM_LIMIT = 48 * 1024 * 1024
LAST = (((1,), (1,)), ((), ()))


def cut(size, most):
    return max(w for w in range(128, most + 1, 128) if size % w == 0)


def call_kernel(kernel, operands, kinds, outs, scratch, flops, behind=()):
    spaces = {"any": pl.ANY, "vmem": pltpu.VMEM, "smem": pltpu.SMEM}
    count = len(operands)
    operands = [*operands, *behind]
    kinds = [*kinds, *["any" for _ in behind]]

    def body(*refs):
        kernel(*refs[:count], *refs[len(operands) :])

    return pl.pallas_call(
        body,
        out_shape=outs,
        in_specs=[pl.BlockSpec(memory_space=spaces[k]) for k in kinds],
        out_specs=[pl.BlockSpec(memory_space=pltpu.VMEM) for _ in outs],
        scratch_shapes=scratch,
        compiler_params=pltpu.CompilerParams(vmem_limit_bytes=VMEM_LIMIT),
        cost_estimate=pl.CostEstimate(flops=flops, bytes_accessed=1 << 20, transcendentals=0),
    )(*operands)


def pack_rows(parts, packed):
    half = parts[0].shape[0] // 2
    for e in range(2):
        for s, part in enumerate(parts):
            packed[e, s * half : (s + 1) * half, :] = part[e * half : (e + 1) * half, :]


def source_at(distance, chip, count):
    place = jnp.where(chip % 2 == 0, chip // 2, count - (chip + 1) // 2)
    place = (place + distance) % count
    return jnp.where(place < count // 2, 2 * place, 2 * (count - place) - 1)


def run_hold(array, behind):
    def kernel(in_ref, out_ref):
        out_ref[...] = in_ref[...]

    shape = jax.ShapeDtypeStruct(array.shape, array.dtype)
    return call_kernel(kernel, [array], ["vmem"], [shape], [], 1, behind)[0]


def run_routing(ids, tables, top_count, capacity):
    count, _, tokens = tables.shape
    f32, bf16 = jnp.float32, jnp.bfloat16

    def kernel(ids_ref, table_ref, pick_ref, spread_ref):
        core, chip = ids_ref[0], ids_ref[1]
        first = lax.broadcasted_iota(jnp.int32, (tokens, tokens), 0)
        second = lax.broadcasted_iota(jnp.int32, (tokens, tokens), 1)
        before = (first <= second).astype(f32).astype(bf16)
        slot = lax.broadcasted_iota(jnp.int32, (capacity, tokens), 0).astype(f32)
        hits, weights = [], []
        for s in range(count):
            table = table_ref[source_at(s, chip, count)]
            for e in range(2):
                expert = jnp.where(core == e, chip, count + chip).astype(f32)
                hit = (table[:top_count] == expert).astype(f32)
                hits.append(jnp.sum(hit, axis=0, keepdims=True))
                weights.append(
                    jnp.sum(hit * table[top_count : 2 * top_count], axis=0, keepdims=True)
                )
        rank = jnp.dot(
            jnp.concatenate(hits, axis=0).astype(bf16), before, preferred_element_type=f32
        )
        for s in range(count):
            for e in range(2):
                i = 2 * s + e
                chosen = jnp.where(slot == rank[i : i + 1] - 1.0, hits[i], 0.0)
                span = slice(e * capacity, (e + 1) * capacity)
                pick_ref[s, span, :] = chosen.astype(bf16)
                spread_ref[s, span, :] = (chosen * weights[i]).astype(bf16)

    shape = jax.ShapeDtypeStruct((count, 2 * capacity, tokens), bf16)
    return call_kernel(kernel, [ids, tables], ["smem", "vmem"], [shape, shape], [], 1 << 20)


def run_hidden(parts, gate_mats, up_mats, behind):
    count, rows, width = len(parts), parts[0].shape[0], parts[0].shape[1]
    units = gate_mats[0].shape[1]
    total = count * rows // 2
    tile = cut(units, 256)
    tiles = units // tile

    def kernel(*refs):
        part_refs, mats = refs[:count], refs[count : count + 4]
        hidden_ref, slope_ref, act_ref, packed, held, sems = refs[count + 4 :]
        copies = {}
        for e in range(2):
            for m in range(2):
                copies[e, m] = pltpu.make_async_copy(
                    mats[2 * m + e], held.at[e, m], sems.at[e, m]
                )
                copies[e, m].start()
        pack_rows(part_refs, packed)
        for e in range(2):
            for m in range(2):
                copies[e, m].wait()
            for n in range(tiles):
                span = slice(n * tile, (n + 1) * tile)
                gate = jnp.dot(packed[e], held[e, 0, :, span], preferred_element_type=jnp.float32)
                up = jnp.dot(packed[e], held[e, 1, :, span], preferred_element_type=jnp.float32)
                sigma = 1.0 / (1.0 + jnp.exp(-gate))
                act = gate * sigma
                hidden_ref[e, :, span] = (act * up).astype(jnp.bfloat16)
                slope_ref[e, :, span] = up * sigma * (1.0 + gate * (1.0 - sigma))
                act_ref[e, :, span] = act

    return call_kernel(
        kernel,
        [*parts, *gate_mats, *up_mats],
        ["vmem"] * count + ["any"] * 4,
        [
            jax.ShapeDtypeStruct((2, total, units), jnp.bfloat16),
            jax.ShapeDtypeStruct((2, total, units), jnp.float32),
            jax.ShapeDtypeStruct((2, total, units), jnp.float32),
        ],
        [
            pltpu.VMEM((2, total, width), jnp.bfloat16),
            pltpu.VMEM((2, 2, width, units), jnp.bfloat16),
            pltpu.SemaphoreType.DMA((2, 2)),
        ],
        8 * total * width * units,
        behind,
    )


def run_down(hidden, down_mats, count, behind):
    _, total, units = hidden.shape
    width = down_mats[0].shape[1]
    half = total // count
    tile = cut(width, 512)
    tiles = width // tile

    def kernel(hidden_ref, own_ref, other_ref, out_ref, held, sems):
        copies = {}
        for e, mat in enumerate((own_ref, other_ref)):
            copies[e] = pltpu.make_async_copy(mat, held.at[e], sems.at[e])
            copies[e].start()
        for e in range(2):
            copies[e].wait()
            for n in range(tiles):
                columns = held[e, :, n * tile : (n + 1) * tile]
                out = jnp.dot(hidden_ref[e], columns, preferred_element_type=jnp.float32)
                out_ref[:, e * half : (e + 1) * half, n * tile : (n + 1) * tile] = (
                    out.astype(jnp.bfloat16).reshape(count, half, tile)
                )

    return call_kernel(
        kernel,
        [hidden, *down_mats],
        ["vmem", "any", "any"],
        [jax.ShapeDtypeStruct((count, 2 * half, width), jnp.bfloat16)],
        [
            pltpu.VMEM((2, units, width), jnp.bfloat16),
            pltpu.SemaphoreType.DMA((2,)),
        ],
        4 * total * width * units,
        behind,
    )[0]


def run_d_hidden(parts, slope, activated, down_mats):
    count, rows, width = len(parts), parts[0].shape[0], parts[0].shape[1]
    _, total, units = slope.shape
    tile = cut(units, 256)
    tiles = units // tile

    def kernel(*refs):
        part_refs = refs[:count]
        slope_ref, act_ref, own_ref, other_ref = refs[count : count + 4]
        d_gate_ref, d_up_ref, packed, held, sems = refs[count + 4 :]
        copies = {}
        for e, mat in enumerate((own_ref, other_ref)):
            for n in range(tiles):
                copies[e, n] = pltpu.make_async_copy(
                    mat.at[n * tile : (n + 1) * tile, :], held.at[e, n], sems.at[e, n]
                )
                copies[e, n].start()
        pack_rows(part_refs, packed)
        for e in range(2):
            for n in range(tiles):
                span = slice(n * tile, (n + 1) * tile)
                copies[e, n].wait()
                d_hidden = lax.dot_general(
                    packed[e], held[e, n], LAST, preferred_element_type=jnp.float32
                )
                d_gate_ref[e, :, span] = (d_hidden * slope_ref[e, :, span]).astype(jnp.bfloat16)
                d_up_ref[e, :, span] = (d_hidden * act_ref[e, :, span]).astype(jnp.bfloat16)

    return call_kernel(
        kernel,
        [*parts, slope, activated, *down_mats],
        ["vmem"] * (count + 2) + ["any"] * 2,
        [jax.ShapeDtypeStruct((2, total, units), jnp.bfloat16)] * 2,
        [
            pltpu.VMEM((2, total, width), jnp.bfloat16),
            pltpu.VMEM((2, tiles, tile, width), jnp.bfloat16),
            pltpu.SemaphoreType.DMA((2, tiles)),
        ],
        4 * total * width * units,
    )


def run_d_gates(ids, parts, outputs, pick, behind):
    count, rows = len(parts), parts[0].shape[0]
    half = rows // 2
    tokens = pick.shape[2]

    def kernel(*refs):
        ids_ref, part_refs = refs[0], refs[1 : 1 + count]
        out_ref, pick_ref, token_ref = refs[1 + count :]
        for s in range(count):
            inner = jnp.sum(
                part_refs[s][...].astype(jnp.float32) * out_ref[s].astype(jnp.float32),
                axis=1,
                keepdims=True,
            )
            spread = pick_ref[s].astype(jnp.float32) * inner
            sums = [
                jnp.sum(spread[e * half : (e + 1) * half], axis=0, keepdims=True)
                for e in range(2)
            ]
            token_ref[source_at(s, ids_ref[1], count)] = jnp.concatenate(sums, axis=0)

    return call_kernel(
        kernel,
        [ids, *parts, outputs, pick],
        ["smem"] + ["vmem"] * (count + 2),
        [jax.ShapeDtypeStruct((count, 2, tokens), jnp.float32)],
        [],
        1 << 20,
        behind,
    )[0]


def run_d_copy(d_pre_gate, d_pre_up, gate_mats, up_mats, count, behind):
    _, total, units = d_pre_gate.shape
    width = gate_mats[0].shape[0]
    half = total // count
    tile = cut(width, 512)
    tiles = width // tile

    def kernel(d_gate_ref, d_up_ref, *refs):
        mats = refs[:4]
        out_ref, held, sems = refs[4:]
        copies = {}
        for e in range(2):
            for n in range(tiles):
                for m in range(2):
                    copies[e, n, m] = pltpu.make_async_copy(
                        mats[2 * m + e].at[n * tile : (n + 1) * tile, :],
                        held.at[e, n, m],
                        sems.at[e, n, m],
                    )
                    copies[e, n, m].start()
        for e in range(2):
            for n in range(tiles):
                copies[e, n, 0].wait()
                out = lax.dot_general(
                    d_gate_ref[e], held[e, n, 0], LAST, preferred_element_type=jnp.float32
                )
                copies[e, n, 1].wait()
                out = out + lax.dot_general(
                    d_up_ref[e], held[e, n, 1], LAST, preferred_element_type=jnp.float32
                )
                out_ref[:, e * half : (e + 1) * half, n * tile : (n + 1) * tile] = (
                    out.astype(jnp.bfloat16).reshape(count, half, tile)
                )

    return call_kernel(
        kernel,
        [d_pre_gate, d_pre_up, *gate_mats, *up_mats],
        ["vmem", "vmem"] + ["any"] * 4,
        [jax.ShapeDtypeStruct((count, 2 * half, width), jnp.bfloat16)],
        [
            pltpu.VMEM((2, tiles, 2, tile, units), jnp.bfloat16),
            pltpu.SemaphoreType.DMA((2, tiles, 2)),
        ],
        8 * total * width * units,
        behind,
    )[0]


def swap_cores(array):
    return lax.ppermute(array, "grp", [(0, 1), (1, 0)])


def body_ring(tokens, cotangent, routes, gates, w_gate, w_up, w_down):
    token_count = tokens.shape[0]
    width = tokens.shape[1]
    top_count = routes.shape[1]
    chips = lax.axis_size("ep")
    expert_count = lax.axis_size(("grp", "ep"))
    capacity = max(2, 3 * token_count * top_count // (2 * expert_count))
    f32, bf16 = jnp.float32, jnp.bfloat16

    core = lax.axis_index("grp")
    chip = lax.axis_index("ep")
    ids = jnp.stack([core, chip]).astype(jnp.int32)
    table = jnp.concatenate([routes.astype(f32), gates.astype(f32)], axis=1).T
    copies = jnp.broadcast_to(table[None], (chips,) + table.shape)
    tables = lax.all_to_all(copies, "ep", split_axis=0, concat_axis=0, tiled=True)
    pick, spread = run_routing(ids, tables, top_count, capacity)

    gate_mats = (w_gate[0], swap_cores(w_gate[0]))
    up_mats = (w_up[0], swap_cores(w_up[0]))
    down_mats = (w_down[0], swap_cores(w_down[0]))
    swapped = (gate_mats[1], up_mats[1], down_mats[1])

    behind = {(step, 2): (tables,) for step in (1, -1)}
    behind.update({(step, 3): swapped for step in (1, -1)})
    in_shards, in_hops = ring_gather(tokens, chips, 1, behind)
    grad_later = run_hold(cotangent, (in_hops[1][1], in_hops[-1][1], *swapped))
    grad_shards, grad_hops = ring_gather(grad_later, chips, -1)

    def gather_rows(shards):
        return [
            jnp.dot(pick[s], shards[s], preferred_element_type=f32).astype(bf16)
            for s in range(chips)
        ]

    def scatter_rows(blocks):
        def share_of(s, partial, waits=(), add_waits=False):
            total = lax.dot_general(
                spread[s], blocks[s], (((0,), (0,)), ((), ())), preferred_element_type=f32
            )
            if partial is not None:
                total = total + partial.astype(f32)
            if add_waits:
                return (total + waits[0].astype(f32)).astype(bf16)
            return after(total.astype(bf16), *waits)

        return share_of

    rows_in = gather_rows(in_shards)
    hidden, slope, activated = run_hidden(
        rows_in, gate_mats, up_mats, [grad_hops[step][1] for step in (1, -1)]
    )
    outputs = run_down(hidden, down_mats, chips, [grad_hops[step][2] for step in (1, -1)])
    rows_grad = gather_rows(grad_shards)
    d_pre_gate, d_pre_up = run_d_hidden(rows_grad, slope, activated, down_mats)
    behind = {(-1, 0): (grad_hops[-1][-1],), (-1, 1): (d_pre_gate,)}
    mixed, mixed_hops = ring_reduce(scatter_rows(outputs), chips, 1, behind)
    d_copies = run_d_copy(
        d_pre_gate, d_pre_up, gate_mats, up_mats, chips, [mixed_hops[step][0] for step in (1, -1)]
    )

    per_token = run_d_gates(ids, rows_grad, outputs, pick, (d_pre_gate,))
    returned = lax.all_to_all(per_token, "ep", split_axis=0, concat_axis=0, tiled=True)
    behind = {
        (step, hop): (mixed_hops[step][hop + 1],)
        for step in (1, -1)
        for hop in range(len(mixed_hops[step]) - 1)
    }
    behind[-1, 1] += (per_token,)
    d_tokens, _ = ring_reduce(scatter_rows(d_copies), chips, -1, behind)
    chip_ids = jnp.arange(chips, dtype=jnp.int32)
    served = jnp.stack([core * chips + chip_ids, (1 - core) * chips + chip_ids], axis=1)
    chosen = routes.T[None, None] == served[:, :, None, None]
    d_gates = jnp.sum(jnp.where(chosen, returned[:, :, None, :], 0.0), axis=(0, 1)).T
    return (mixed, d_tokens, d_gates)


def solution(mesh):
    plan = body_ring if mesh.shape["ep"] <= 8 and mesh.shape["grp"] == 2 else body_exchange
    return jax.shard_map(
        plan,
        mesh=mesh,
        in_specs=(
            P(("rep", "grp", "ep"), None),
            P(("rep", "grp", "ep"), None),
            P(("rep", "grp", "ep"), None),
            P(("rep", "grp", "ep"), None),
            P(("grp", "ep"), None, None),
            P(("grp", "ep"), None, None),
            P(("grp", "ep"), None, None),
        ),
        out_specs=(
            P(("rep", "grp", "ep"), None),
            P(("rep", "grp", "ep"), None),
            P(("rep", "grp", "ep"), None),
        ),
        check_vma=False,
    )
```

```python
import jax
import jax.numpy as jnp
from jax import lax
from jax.experimental import pallas as pl
from jax.experimental.pallas import tpu as pltpu
from jax.sharding import PartitionSpec as P


def expert_pass(rows_in, rows_grad, gate_mat, up_mat, down_mat):
    pre_gate = jnp.dot(rows_in, gate_mat, preferred_element_type=jnp.float32)
    pre_up = jnp.dot(rows_in, up_mat, preferred_element_type=jnp.float32)
    activated = jax.nn.silu(pre_gate)
    hidden = (activated * pre_up).astype(jnp.bfloat16)
    outputs = jnp.dot(hidden, down_mat, preferred_element_type=jnp.float32).astype(jnp.bfloat16)
    d_hidden = lax.dot_general(
        rows_grad, down_mat, (((1,), (1,)), ((), ())), preferred_element_type=jnp.float32
    )
    sigma = jax.nn.sigmoid(pre_gate)
    d_pre_gate = (d_hidden * pre_up * sigma * (1.0 + pre_gate * (1.0 - sigma))).astype(jnp.bfloat16)
    d_pre_up = (d_hidden * activated).astype(jnp.bfloat16)
    both_pre = jnp.concatenate([d_pre_gate, d_pre_up], axis=1)
    both_mats = jnp.concatenate([gate_mat, up_mat], axis=1)
    d_copy = lax.dot_general(
        both_pre, both_mats, (((1,), (1,)), ((), ())), preferred_element_type=jnp.float32
    )
    return (outputs, d_copy.astype(jnp.bfloat16))


def run_items(pieces, gate_mat, up_mat, down_mat):
    rows_in, rows_grad = pieces
    lead_shape = rows_in.shape[:2]
    width = rows_in.shape[2]
    outputs, d_copy = expert_pass(
        rows_in.reshape(-1, width), rows_grad.reshape(-1, width), gate_mat, up_mat, down_mat
    )
    return (outputs.reshape(lead_shape + (width,)), d_copy.reshape(lead_shape + (width,)))


def ranks_of(chosen_hot):
    running = jnp.cumsum(chosen_hot, axis=-2)
    return jnp.sum(chosen_hot * running, axis=-1) - 1


def body_exchange(tokens, cotangent, routes, gates, w_gate, w_up, w_down):
    token_count = tokens.shape[0]
    width = tokens.shape[1]
    top_count = routes.shape[1]
    copy_count = token_count * top_count
    gate_mat = w_gate[0]
    up_mat = w_up[0]
    down_mat = w_down[0]
    expert_count = lax.axis_size(("grp", "ep"))
    capacity = max(2, 3 * token_count * top_count // (2 * expert_count))
    flat_experts = routes.reshape(-1)
    chosen_hot = (
        flat_experts[:, None] == jnp.arange(expert_count, dtype=jnp.int32)[None, :]
    ).astype(jnp.int32)
    slot_of = flat_experts * capacity + ranks_of(chosen_hot)
    token_of = jnp.arange(copy_count, dtype=jnp.int32) // top_count
    slot_token = jnp.zeros((expert_count * capacity,), jnp.int32).at[slot_of].set(token_of)
    slot_live = jnp.zeros((expert_count * capacity,), jnp.bool_).at[slot_of].set(True)
    send_in = jnp.where(
        slot_live[:, None], tokens[slot_token], jnp.zeros((), tokens.dtype)
    ).reshape(expert_count, capacity, width)
    send_grad = jnp.where(
        slot_live[:, None], cotangent[slot_token], jnp.zeros((), cotangent.dtype)
    ).reshape(expert_count, capacity, width)
    outputs, d_copy = run_items(
        (
            lax.all_to_all(send_in, ("grp", "ep"), split_axis=0, concat_axis=0, tiled=True),
            lax.all_to_all(send_grad, ("grp", "ep"), split_axis=0, concat_axis=0, tiled=True),
        ),
        gate_mat,
        up_mat,
        down_mat,
    )
    back_out = lax.all_to_all(outputs, ("grp", "ep"), split_axis=0, concat_axis=0, tiled=True)
    back_grad = lax.all_to_all(d_copy, ("grp", "ep"), split_axis=0, concat_axis=0, tiled=True)
    copy_out = back_out.reshape(-1, width)[slot_of].reshape(token_count, top_count, width)
    copy_grad = back_grad.reshape(-1, width)[slot_of].reshape(token_count, top_count, width)
    weight = gates.astype(jnp.float32)
    mixed = jnp.sum(weight[:, :, None] * copy_out.astype(jnp.float32), axis=1)
    d_tokens = jnp.sum(weight[:, :, None] * copy_grad.astype(jnp.float32), axis=1)
    d_gates = jnp.einsum("tkd,td->tk", copy_out, cotangent, preferred_element_type=jnp.float32)
    return (mixed.astype(jnp.bfloat16), d_tokens.astype(jnp.bfloat16), d_gates)


def ring_order(count):
    return list(range(0, count, 2)) + list(range(count - 1, 0, -2))


def ring_shift(array, count, step):
    order = ring_order(count)
    pairs = [(order[i], order[(i + step) % count]) for i in range(count)]
    return lax.ppermute(array, "ep", pairs)


def ring_gather(shard, count, far_step, behind={}):
    held = {0: shard}
    arrivals = {}
    for step in (far_step, -far_step):
        hops = count // 2 if step == far_step else (count - 1) // 2
        moving = shard
        arrivals[step] = []
        for hop in range(1, hops + 1):
            if (step, hop) in behind:
                moving = held_back(moving, behind[step, hop])
                if hop > 1:
                    held[(-step * (hop - 1)) % count] = moving
            moving = ring_shift(moving, count, step)
            held[(-step * hop) % count] = moving
            arrivals[step].append(moving)
    return [held[place] for place in range(count)], arrivals


def after(array, *others):
    for other in others:
        array = array + other[(slice(0, 1),) * other.ndim].reshape((1,) * array.ndim).astype(array.dtype) * 0
    return array


def held_back(array, others):
    def kernel(*refs):
        pass

    return pl.pallas_call(
        kernel,
        out_shape=jax.ShapeDtypeStruct(array.shape, array.dtype),
        in_specs=[pl.BlockSpec(memory_space=pl.ANY) for _ in range(1 + len(others))],
        out_specs=pl.BlockSpec(memory_space=pl.ANY),
        input_output_aliases={0: 0},
    )(array, *others)


def ring_reduce(share_of, count, far_step, behind={}):
    arrived = {}
    for step in (far_step, -far_step):
        hops = count // 2 if step == far_step else (count - 1) // 2
        moving = None
        steps = []
        for hop in range(hops, 0, -1):
            waits = behind.get((step, hops - hop), ())
            share = share_of((step * hop) % count, moving, waits)
            moving = ring_shift(share, count, step)
            steps.append(moving)
        arrived[step] = steps
    total = share_of(0, arrived[far_step][-1], (arrived[-far_step][-1],), True)
    return total, arrived


VMEM_LIMIT = 48 * 1024 * 1024
LAST = (((1,), (1,)), ((), ()))


def cut(size, most):
    return max(w for w in range(128, most + 1, 128) if size % w == 0)


def call_kernel(kernel, operands, kinds, outs, scratch, flops, behind=()):
    spaces = {"any": pl.ANY, "vmem": pltpu.VMEM, "smem": pltpu.SMEM}
    count = len(operands)
    operands = [*operands, *behind]
    kinds = [*kinds, *["any" for _ in behind]]

    def body(*refs):
        kernel(*refs[:count], *refs[len(operands) :])

    return pl.pallas_call(
        body,
        out_shape=outs,
        in_specs=[pl.BlockSpec(memory_space=spaces[k]) for k in kinds],
        out_specs=[pl.BlockSpec(memory_space=pltpu.VMEM) for _ in outs],
        scratch_shapes=scratch,
        compiler_params=pltpu.CompilerParams(vmem_limit_bytes=VMEM_LIMIT),
        cost_estimate=pl.CostEstimate(flops=flops, bytes_accessed=1 << 20, transcendentals=0),
    )(*operands)


def pack_rows(parts, packed):
    half = parts[0].shape[0] // 2
    for e in range(2):
        for s, part in enumerate(parts):
            packed[e, s * half : (s + 1) * half, :] = part[e * half : (e + 1) * half, :]


def source_at(distance, chip, count):
    place = jnp.where(chip % 2 == 0, chip // 2, count - (chip + 1) // 2)
    place = (place + distance) % count
    return jnp.where(place < count // 2, 2 * place, 2 * (count - place) - 1)


def run_hold(array, behind):
    def kernel(in_ref, out_ref):
        out_ref[...] = in_ref[...]

    shape = jax.ShapeDtypeStruct(array.shape, array.dtype)
    return call_kernel(kernel, [array], ["vmem"], [shape], [], 1, behind)[0]


def run_routing(ids, tables, top_count, capacity, behind):
    count, _, tokens = tables.shape
    f32, bf16 = jnp.float32, jnp.bfloat16

    def kernel(ids_ref, table_ref, pick_ref, spread_ref):
        core, chip = ids_ref[0], ids_ref[1]
        first = lax.broadcasted_iota(jnp.int32, (tokens, tokens), 0)
        second = lax.broadcasted_iota(jnp.int32, (tokens, tokens), 1)
        before = (first <= second).astype(f32).astype(bf16)
        slot = lax.broadcasted_iota(jnp.int32, (capacity, tokens), 0).astype(f32)
        hits, weights = [], []
        for s in range(count):
            table = table_ref[source_at(s, chip, count)]
            for e in range(2):
                expert = jnp.where(core == e, chip, count + chip).astype(f32)
                hit = (table[:top_count] == expert).astype(f32)
                hits.append(jnp.sum(hit, axis=0, keepdims=True))
                weights.append(
                    jnp.sum(hit * table[top_count : 2 * top_count], axis=0, keepdims=True)
                )
        rank = jnp.dot(
            jnp.concatenate(hits, axis=0).astype(bf16), before, preferred_element_type=f32
        )
        for s in range(count):
            for e in range(2):
                i = 2 * s + e
                chosen = jnp.where(slot == rank[i : i + 1] - 1.0, hits[i], 0.0)
                span = slice(e * capacity, (e + 1) * capacity)
                pick_ref[s, span, :] = chosen.astype(bf16)
                spread_ref[s, span, :] = (chosen * weights[i]).astype(bf16)

    shape = jax.ShapeDtypeStruct((count, 2 * capacity, tokens), bf16)
    return call_kernel(kernel, [ids, tables], ["smem", "vmem"], [shape, shape], [], 1 << 20, behind)


def run_hidden(parts, gate_mats, up_mats, behind):
    count, rows, width = len(parts), parts[0].shape[0], parts[0].shape[1]
    units = gate_mats[0].shape[1]
    total = count * rows // 2
    tile = cut(units, 256)
    tiles = units // tile

    def kernel(*refs):
        part_refs, mats = refs[:count], refs[count : count + 4]
        hidden_ref, slope_ref, act_ref, packed, held, sems = refs[count + 4 :]
        copies = {}
        for e in range(2):
            for m in range(2):
                copies[e, m] = pltpu.make_async_copy(
                    mats[2 * m + e], held.at[e, m], sems.at[e, m]
                )
                copies[e, m].start()
        pack_rows(part_refs, packed)
        for e in range(2):
            for m in range(2):
                copies[e, m].wait()
            for n in range(tiles):
                span = slice(n * tile, (n + 1) * tile)
                gate = jnp.dot(packed[e], held[e, 0, :, span], preferred_element_type=jnp.float32)
                up = jnp.dot(packed[e], held[e, 1, :, span], preferred_element_type=jnp.float32)
                sigma = 1.0 / (1.0 + jnp.exp(-gate))
                act = gate * sigma
                hidden_ref[e, :, span] = (act * up).astype(jnp.bfloat16)
                slope_ref[e, :, span] = up * sigma * (1.0 + gate * (1.0 - sigma))
                act_ref[e, :, span] = act

    return call_kernel(
        kernel,
        [*parts, *gate_mats, *up_mats],
        ["vmem"] * count + ["any"] * 4,
        [
            jax.ShapeDtypeStruct((2, total, units), jnp.bfloat16),
            jax.ShapeDtypeStruct((2, total, units), jnp.float32),
            jax.ShapeDtypeStruct((2, total, units), jnp.float32),
        ],
        [
            pltpu.VMEM((2, total, width), jnp.bfloat16),
            pltpu.VMEM((2, 2, width, units), jnp.bfloat16),
            pltpu.SemaphoreType.DMA((2, 2)),
        ],
        8 * total * width * units,
        behind,
    )


def run_down(hidden, down_mats, count, behind):
    _, total, units = hidden.shape
    width = down_mats[0].shape[1]
    half = total // count
    tile = cut(width, 512)
    tiles = width // tile

    def kernel(hidden_ref, own_ref, other_ref, out_ref, held, sems):
        copies = {}
        for e, mat in enumerate((own_ref, other_ref)):
            copies[e] = pltpu.make_async_copy(mat, held.at[e], sems.at[e])
            copies[e].start()
        for e in range(2):
            copies[e].wait()
            for n in range(tiles):
                columns = held[e, :, n * tile : (n + 1) * tile]
                out = jnp.dot(hidden_ref[e], columns, preferred_element_type=jnp.float32)
                out_ref[:, e * half : (e + 1) * half, n * tile : (n + 1) * tile] = (
                    out.astype(jnp.bfloat16).reshape(count, half, tile)
                )

    return call_kernel(
        kernel,
        [hidden, *down_mats],
        ["vmem", "any", "any"],
        [jax.ShapeDtypeStruct((count, 2 * half, width), jnp.bfloat16)],
        [
            pltpu.VMEM((2, units, width), jnp.bfloat16),
            pltpu.SemaphoreType.DMA((2,)),
        ],
        4 * total * width * units,
        behind,
    )[0]


def run_d_hidden(parts, slope, activated, down_mats):
    count, rows, width = len(parts), parts[0].shape[0], parts[0].shape[1]
    _, total, units = slope.shape
    tile = cut(units, 256)
    tiles = units // tile

    def kernel(*refs):
        part_refs = refs[:count]
        slope_ref, act_ref, own_ref, other_ref = refs[count : count + 4]
        d_gate_ref, d_up_ref, packed, held, sems = refs[count + 4 :]
        copies = {}
        for e, mat in enumerate((own_ref, other_ref)):
            for n in range(tiles):
                copies[e, n] = pltpu.make_async_copy(
                    mat.at[n * tile : (n + 1) * tile, :], held.at[e, n], sems.at[e, n]
                )
                copies[e, n].start()
        pack_rows(part_refs, packed)
        for e in range(2):
            for n in range(tiles):
                span = slice(n * tile, (n + 1) * tile)
                copies[e, n].wait()
                d_hidden = lax.dot_general(
                    packed[e], held[e, n], LAST, preferred_element_type=jnp.float32
                )
                d_gate_ref[e, :, span] = (d_hidden * slope_ref[e, :, span]).astype(jnp.bfloat16)
                d_up_ref[e, :, span] = (d_hidden * act_ref[e, :, span]).astype(jnp.bfloat16)

    return call_kernel(
        kernel,
        [*parts, slope, activated, *down_mats],
        ["vmem"] * (count + 2) + ["any"] * 2,
        [jax.ShapeDtypeStruct((2, total, units), jnp.bfloat16)] * 2,
        [
            pltpu.VMEM((2, total, width), jnp.bfloat16),
            pltpu.VMEM((2, tiles, tile, width), jnp.bfloat16),
            pltpu.SemaphoreType.DMA((2, tiles)),
        ],
        4 * total * width * units,
    )


def run_d_gates(ids, parts, outputs, pick, behind):
    count, rows = len(parts), parts[0].shape[0]
    half = rows // 2
    tokens = pick.shape[2]

    def kernel(*refs):
        ids_ref, part_refs = refs[0], refs[1 : 1 + count]
        out_ref, pick_ref, token_ref = refs[1 + count :]
        for s in range(count):
            inner = jnp.sum(
                part_refs[s][...].astype(jnp.float32) * out_ref[s].astype(jnp.float32),
                axis=1,
                keepdims=True,
            )
            spread = pick_ref[s].astype(jnp.float32) * inner
            sums = [
                jnp.sum(spread[e * half : (e + 1) * half], axis=0, keepdims=True)
                for e in range(2)
            ]
            token_ref[source_at(s, ids_ref[1], count)] = jnp.concatenate(sums, axis=0)

    return call_kernel(
        kernel,
        [ids, *parts, outputs, pick],
        ["smem"] + ["vmem"] * (count + 2),
        [jax.ShapeDtypeStruct((count, 2, tokens), jnp.float32)],
        [],
        1 << 20,
        behind,
    )[0]


def run_d_copy(d_pre_gate, d_pre_up, gate_mats, up_mats, count, behind):
    _, total, units = d_pre_gate.shape
    width = gate_mats[0].shape[0]
    half = total // count
    tile = cut(width, 512)
    tiles = width // tile

    def kernel(d_gate_ref, d_up_ref, *refs):
        mats = refs[:4]
        out_ref, held, sems = refs[4:]
        copies = {}
        for e in range(2):
            for n in range(tiles):
                for m in range(2):
                    copies[e, n, m] = pltpu.make_async_copy(
                        mats[2 * m + e].at[n * tile : (n + 1) * tile, :],
                        held.at[e, n, m],
                        sems.at[e, n, m],
                    )
                    copies[e, n, m].start()
        for e in range(2):
            for n in range(tiles):
                copies[e, n, 0].wait()
                out = lax.dot_general(
                    d_gate_ref[e], held[e, n, 0], LAST, preferred_element_type=jnp.float32
                )
                copies[e, n, 1].wait()
                out = out + lax.dot_general(
                    d_up_ref[e], held[e, n, 1], LAST, preferred_element_type=jnp.float32
                )
                out_ref[:, e * half : (e + 1) * half, n * tile : (n + 1) * tile] = (
                    out.astype(jnp.bfloat16).reshape(count, half, tile)
                )

    return call_kernel(
        kernel,
        [d_pre_gate, d_pre_up, *gate_mats, *up_mats],
        ["vmem", "vmem"] + ["any"] * 4,
        [jax.ShapeDtypeStruct((count, 2 * half, width), jnp.bfloat16)],
        [
            pltpu.VMEM((2, tiles, 2, tile, units), jnp.bfloat16),
            pltpu.SemaphoreType.DMA((2, tiles, 2)),
        ],
        8 * total * width * units,
        behind,
    )[0]


def swap_cores(array):
    return lax.ppermute(array, "grp", [(0, 1), (1, 0)])


def body_ring(tokens, cotangent, routes, gates, w_gate, w_up, w_down):
    token_count = tokens.shape[0]
    width = tokens.shape[1]
    top_count = routes.shape[1]
    chips = lax.axis_size("ep")
    expert_count = lax.axis_size(("grp", "ep"))
    capacity = max(2, 3 * token_count * top_count // (2 * expert_count))
    f32, bf16 = jnp.float32, jnp.bfloat16

    core = lax.axis_index("grp")
    chip = lax.axis_index("ep")
    ids = jnp.stack([core, chip]).astype(jnp.int32)
    table = jnp.concatenate([routes.astype(f32), gates.astype(f32)], axis=1).T
    copies = jnp.broadcast_to(table[None], (chips,) + table.shape)
    tables = lax.all_to_all(copies, "ep", split_axis=0, concat_axis=0, tiled=True)
    gate_mats = (w_gate[0], swap_cores(w_gate[0]))
    up_mats = (w_up[0], swap_cores(w_up[0]))
    down_mats = (w_down[0], swap_cores(w_down[0]))
    pick, spread = run_routing(ids, tables, top_count, capacity, (gate_mats[1], up_mats[1]))

    swapped = (down_mats[1],)

    behind = {(step, 2): (tables,) for step in (1, -1)}
    behind.update({(step, 3): swapped for step in (1, -1)})
    in_shards, in_hops = ring_gather(tokens, chips, 1, behind)
    grad_later = run_hold(cotangent, (in_hops[1][1], in_hops[-1][1], *swapped))
    grad_shards, grad_hops = ring_gather(grad_later, chips, -1)

    def gather_rows(shards):
        return [
            jnp.dot(pick[s], shards[s], preferred_element_type=f32).astype(bf16)
            for s in range(chips)
        ]

    def scatter_rows(blocks):
        def share_of(s, partial, waits=(), add_waits=False):
            total = lax.dot_general(
                spread[s], blocks[s], (((0,), (0,)), ((), ())), preferred_element_type=f32
            )
            if partial is not None:
                total = total + partial.astype(f32)
            if add_waits:
                return (total + waits[0].astype(f32)).astype(bf16)
            return after(total.astype(bf16), *waits)

        return share_of

    rows_in = gather_rows(in_shards)
    hidden, slope, activated = run_hidden(
        rows_in, gate_mats, up_mats, [grad_hops[-1][1]]
    )
    outputs = run_down(hidden, down_mats, chips, [grad_hops[-1][2]])
    rows_grad = gather_rows(grad_shards)
    d_pre_gate, d_pre_up = run_d_hidden(rows_grad, slope, activated, down_mats)
    behind = {(-1, 0): (grad_hops[-1][-1],), (-1, 1): (d_pre_gate,)}
    mixed, mixed_hops = ring_reduce(scatter_rows(outputs), chips, 1, behind)
    d_copies = run_d_copy(
        d_pre_gate, d_pre_up, gate_mats, up_mats, chips, [mixed_hops[step][0] for step in (1, -1)]
    )

    per_token = run_d_gates(ids, rows_grad, outputs, pick, (d_pre_gate,))
    returned = lax.all_to_all(per_token, "ep", split_axis=0, concat_axis=0, tiled=True)
    behind = {
        (step, hop): (mixed_hops[step][hop + 1],)
        for step in (1, -1)
        for hop in range(len(mixed_hops[step]) - 1)
    }
    behind[-1, 2] = (per_token,)
    d_tokens, _ = ring_reduce(scatter_rows(d_copies), chips, -1, behind)
    chip_ids = jnp.arange(chips, dtype=jnp.int32)
    served = jnp.stack([core * chips + chip_ids, (1 - core) * chips + chip_ids], axis=1)
    chosen = routes.T[None, None] == served[:, :, None, None]
    d_gates = jnp.sum(jnp.where(chosen, returned[:, :, None, :], 0.0), axis=(0, 1)).T
    return (mixed, d_tokens, d_gates)


def solution(mesh):
    plan = body_ring if mesh.shape["ep"] <= 8 and mesh.shape["grp"] == 2 else body_exchange
    return jax.shard_map(
        plan,
        mesh=mesh,
        in_specs=(
            P(("rep", "grp", "ep"), None),
            P(("rep", "grp", "ep"), None),
            P(("rep", "grp", "ep"), None),
            P(("rep", "grp", "ep"), None),
            P(("grp", "ep"), None, None),
            P(("grp", "ep"), None, None),
            P(("grp", "ep"), None, None),
        ),
        out_specs=(
            P(("rep", "grp", "ep"), None),
            P(("rep", "grp", "ep"), None),
            P(("rep", "grp", "ep"), None),
        ),
        check_vma=False,
    )
```

```python
import jax
import jax.numpy as jnp
from jax import lax
from jax.experimental import pallas as pl
from jax.experimental.pallas import tpu as pltpu
from jax.sharding import PartitionSpec as P


def expert_pass(rows_in, rows_grad, gate_mat, up_mat, down_mat):
    pre_gate = jnp.dot(rows_in, gate_mat, preferred_element_type=jnp.float32)
    pre_up = jnp.dot(rows_in, up_mat, preferred_element_type=jnp.float32)
    activated = jax.nn.silu(pre_gate)
    hidden = (activated * pre_up).astype(jnp.bfloat16)
    outputs = jnp.dot(hidden, down_mat, preferred_element_type=jnp.float32).astype(jnp.bfloat16)
    d_hidden = lax.dot_general(
        rows_grad, down_mat, (((1,), (1,)), ((), ())), preferred_element_type=jnp.float32
    )
    sigma = jax.nn.sigmoid(pre_gate)
    d_pre_gate = (d_hidden * pre_up * sigma * (1.0 + pre_gate * (1.0 - sigma))).astype(jnp.bfloat16)
    d_pre_up = (d_hidden * activated).astype(jnp.bfloat16)
    both_pre = jnp.concatenate([d_pre_gate, d_pre_up], axis=1)
    both_mats = jnp.concatenate([gate_mat, up_mat], axis=1)
    d_copy = lax.dot_general(
        both_pre, both_mats, (((1,), (1,)), ((), ())), preferred_element_type=jnp.float32
    )
    return (outputs, d_copy.astype(jnp.bfloat16))


def run_items(pieces, gate_mat, up_mat, down_mat):
    rows_in, rows_grad = pieces
    lead_shape = rows_in.shape[:2]
    width = rows_in.shape[2]
    outputs, d_copy = expert_pass(
        rows_in.reshape(-1, width), rows_grad.reshape(-1, width), gate_mat, up_mat, down_mat
    )
    return (outputs.reshape(lead_shape + (width,)), d_copy.reshape(lead_shape + (width,)))


def ranks_of(chosen_hot):
    running = jnp.cumsum(chosen_hot, axis=-2)
    return jnp.sum(chosen_hot * running, axis=-1) - 1


def body_exchange(tokens, cotangent, routes, gates, w_gate, w_up, w_down):
    token_count = tokens.shape[0]
    width = tokens.shape[1]
    top_count = routes.shape[1]
    copy_count = token_count * top_count
    gate_mat = w_gate[0]
    up_mat = w_up[0]
    down_mat = w_down[0]
    expert_count = lax.axis_size(("grp", "ep"))
    capacity = max(2, 3 * token_count * top_count // (2 * expert_count))
    flat_experts = routes.reshape(-1)
    chosen_hot = (
        flat_experts[:, None] == jnp.arange(expert_count, dtype=jnp.int32)[None, :]
    ).astype(jnp.int32)
    slot_of = flat_experts * capacity + ranks_of(chosen_hot)
    token_of = jnp.arange(copy_count, dtype=jnp.int32) // top_count
    slot_token = jnp.zeros((expert_count * capacity,), jnp.int32).at[slot_of].set(token_of)
    slot_live = jnp.zeros((expert_count * capacity,), jnp.bool_).at[slot_of].set(True)
    send_in = jnp.where(
        slot_live[:, None], tokens[slot_token], jnp.zeros((), tokens.dtype)
    ).reshape(expert_count, capacity, width)
    send_grad = jnp.where(
        slot_live[:, None], cotangent[slot_token], jnp.zeros((), cotangent.dtype)
    ).reshape(expert_count, capacity, width)
    outputs, d_copy = run_items(
        (
            lax.all_to_all(send_in, ("grp", "ep"), split_axis=0, concat_axis=0, tiled=True),
            lax.all_to_all(send_grad, ("grp", "ep"), split_axis=0, concat_axis=0, tiled=True),
        ),
        gate_mat,
        up_mat,
        down_mat,
    )
    back_out = lax.all_to_all(outputs, ("grp", "ep"), split_axis=0, concat_axis=0, tiled=True)
    back_grad = lax.all_to_all(d_copy, ("grp", "ep"), split_axis=0, concat_axis=0, tiled=True)
    copy_out = back_out.reshape(-1, width)[slot_of].reshape(token_count, top_count, width)
    copy_grad = back_grad.reshape(-1, width)[slot_of].reshape(token_count, top_count, width)
    weight = gates.astype(jnp.float32)
    mixed = jnp.sum(weight[:, :, None] * copy_out.astype(jnp.float32), axis=1)
    d_tokens = jnp.sum(weight[:, :, None] * copy_grad.astype(jnp.float32), axis=1)
    d_gates = jnp.einsum("tkd,td->tk", copy_out, cotangent, preferred_element_type=jnp.float32)
    return (mixed.astype(jnp.bfloat16), d_tokens.astype(jnp.bfloat16), d_gates)


def ring_order(count):
    return list(range(0, count, 2)) + list(range(count - 1, 0, -2))


def ring_shift(array, count, step):
    order = ring_order(count)
    pairs = [(order[i], order[(i + step) % count]) for i in range(count)]
    return lax.ppermute(array, "ep", pairs)


def ring_gather(shard, count, far_step, behind={}):
    held = {0: shard}
    arrivals = {}
    for step in (far_step, -far_step):
        hops = count // 2 if step == far_step else (count - 1) // 2
        moving = shard
        arrivals[step] = []
        for hop in range(1, hops + 1):
            if (step, hop) in behind:
                moving = held_back(moving, behind[step, hop])
                if hop > 1:
                    held[(-step * (hop - 1)) % count] = moving
            moving = ring_shift(moving, count, step)
            held[(-step * hop) % count] = moving
            arrivals[step].append(moving)
    return [held[place] for place in range(count)], arrivals


def after(array, *others):
    for other in others:
        array = array + other[(slice(0, 1),) * other.ndim].reshape((1,) * array.ndim).astype(array.dtype) * 0
    return array


def held_back(array, others):
    def kernel(*refs):
        pass

    return pl.pallas_call(
        kernel,
        out_shape=jax.ShapeDtypeStruct(array.shape, array.dtype),
        in_specs=[pl.BlockSpec(memory_space=pl.ANY) for _ in range(1 + len(others))],
        out_specs=pl.BlockSpec(memory_space=pl.ANY),
        input_output_aliases={0: 0},
    )(array, *others)


def ring_reduce(share_of, count, far_step, behind={}):
    arrived = {}
    for step in (far_step, -far_step):
        hops = count // 2 if step == far_step else (count - 1) // 2
        moving = None
        steps = []
        for hop in range(hops, 0, -1):
            waits = behind.get((step, hops - hop), ())
            share = share_of((step * hop) % count, moving, waits)
            moving = ring_shift(share, count, step)
            steps.append(moving)
        arrived[step] = steps
    total = share_of(0, arrived[far_step][-1], (arrived[-far_step][-1],), True)
    return total, arrived


VMEM_LIMIT = 48 * 1024 * 1024
LAST = (((1,), (1,)), ((), ()))


def cut(size, most):
    return max(w for w in range(128, most + 1, 128) if size % w == 0)


def call_kernel(kernel, operands, kinds, outs, scratch, flops, behind=()):
    spaces = {"any": pl.ANY, "vmem": pltpu.VMEM, "smem": pltpu.SMEM}
    count = len(operands)
    operands = [*operands, *behind]
    kinds = [*kinds, *["any" for _ in behind]]

    def body(*refs):
        kernel(*refs[:count], *refs[len(operands) :])

    return pl.pallas_call(
        body,
        out_shape=outs,
        in_specs=[pl.BlockSpec(memory_space=spaces[k]) for k in kinds],
        out_specs=[pl.BlockSpec(memory_space=pltpu.VMEM) for _ in outs],
        scratch_shapes=scratch,
        compiler_params=pltpu.CompilerParams(vmem_limit_bytes=VMEM_LIMIT),
        cost_estimate=pl.CostEstimate(flops=flops, bytes_accessed=1 << 20, transcendentals=0),
    )(*operands)


def pack_rows(parts, packed):
    half = parts[0].shape[0] // 2
    for e in range(2):
        for s, part in enumerate(parts):
            packed[e, s * half : (s + 1) * half, :] = part[e * half : (e + 1) * half, :]


def source_at(distance, chip, count):
    place = jnp.where(chip % 2 == 0, chip // 2, count - (chip + 1) // 2)
    place = (place + distance) % count
    return jnp.where(place < count // 2, 2 * place, 2 * (count - place) - 1)


def run_hold(array, behind):
    def kernel(in_ref, out_ref):
        out_ref[...] = in_ref[...]

    shape = jax.ShapeDtypeStruct(array.shape, array.dtype)
    return call_kernel(kernel, [array], ["vmem"], [shape], [], 1, behind)[0]


def run_routing(ids, tables, top_count, capacity, behind):
    count, _, tokens = tables.shape
    f32, bf16 = jnp.float32, jnp.bfloat16

    def kernel(ids_ref, table_ref, pick_ref, spread_ref):
        core, chip = ids_ref[0], ids_ref[1]
        first = lax.broadcasted_iota(jnp.int32, (tokens, tokens), 0)
        second = lax.broadcasted_iota(jnp.int32, (tokens, tokens), 1)
        before = (first <= second).astype(f32).astype(bf16)
        slot = lax.broadcasted_iota(jnp.int32, (capacity, tokens), 0).astype(f32)
        hits, weights = [], []
        for s in range(count):
            table = table_ref[source_at(s, chip, count)]
            for e in range(2):
                expert = jnp.where(core == e, chip, count + chip).astype(f32)
                hit = (table[:top_count] == expert).astype(f32)
                hits.append(jnp.sum(hit, axis=0, keepdims=True))
                weights.append(
                    jnp.sum(hit * table[top_count : 2 * top_count], axis=0, keepdims=True)
                )
        rank = jnp.dot(
            jnp.concatenate(hits, axis=0).astype(bf16), before, preferred_element_type=f32
        )
        for s in range(count):
            for e in range(2):
                i = 2 * s + e
                chosen = jnp.where(slot == rank[i : i + 1] - 1.0, hits[i], 0.0)
                span = slice(e * capacity, (e + 1) * capacity)
                pick_ref[s, span, :] = chosen.astype(bf16)
                spread_ref[s, span, :] = (chosen * weights[i]).astype(bf16)

    shape = jax.ShapeDtypeStruct((count, 2 * capacity, tokens), bf16)
    return call_kernel(kernel, [ids, tables], ["smem", "vmem"], [shape, shape], [], 1 << 20, behind)


def run_hidden(parts, gate_mats, up_mats, behind):
    count, rows, width = len(parts), parts[0].shape[0], parts[0].shape[1]
    units = gate_mats[0].shape[1]
    total = count * rows // 2
    tile = cut(units, 256)
    tiles = units // tile

    def kernel(*refs):
        part_refs, mats = refs[:count], refs[count : count + 4]
        hidden_ref, slope_ref, act_ref, packed, held, sems = refs[count + 4 :]
        copies = {}
        for e in range(2):
            for m in range(2):
                copies[e, m] = pltpu.make_async_copy(
                    mats[2 * m + e], held.at[e, m], sems.at[e, m]
                )
                copies[e, m].start()
        pack_rows(part_refs, packed)
        for e in range(2):
            for m in range(2):
                copies[e, m].wait()
            for n in range(tiles):
                span = slice(n * tile, (n + 1) * tile)
                gate = jnp.dot(packed[e], held[e, 0, :, span], preferred_element_type=jnp.float32)
                up = jnp.dot(packed[e], held[e, 1, :, span], preferred_element_type=jnp.float32)
                sigma = 1.0 / (1.0 + jnp.exp(-gate))
                act = gate * sigma
                hidden_ref[e, :, span] = (act * up).astype(jnp.bfloat16)
                slope_ref[e, :, span] = up * sigma * (1.0 + gate * (1.0 - sigma))
                act_ref[e, :, span] = act

    return call_kernel(
        kernel,
        [*parts, *gate_mats, *up_mats],
        ["vmem"] * count + ["any"] * 4,
        [
            jax.ShapeDtypeStruct((2, total, units), jnp.bfloat16),
            jax.ShapeDtypeStruct((2, total, units), jnp.float32),
            jax.ShapeDtypeStruct((2, total, units), jnp.float32),
        ],
        [
            pltpu.VMEM((2, total, width), jnp.bfloat16),
            pltpu.VMEM((2, 2, width, units), jnp.bfloat16),
            pltpu.SemaphoreType.DMA((2, 2)),
        ],
        8 * total * width * units,
        behind,
    )


def run_down(hidden, down_mats, count, behind):
    _, total, units = hidden.shape
    width = down_mats[0].shape[1]
    half = total // count
    tile = cut(width, 512)
    tiles = width // tile

    def kernel(hidden_ref, own_ref, other_ref, out_ref, held, sems):
        copies = {}
        for e, mat in enumerate((own_ref, other_ref)):
            copies[e] = pltpu.make_async_copy(mat, held.at[e], sems.at[e])
            copies[e].start()
        for e in range(2):
            copies[e].wait()
            for n in range(tiles):
                columns = held[e, :, n * tile : (n + 1) * tile]
                out = jnp.dot(hidden_ref[e], columns, preferred_element_type=jnp.float32)
                out_ref[:, e * half : (e + 1) * half, n * tile : (n + 1) * tile] = (
                    out.astype(jnp.bfloat16).reshape(count, half, tile)
                )

    return call_kernel(
        kernel,
        [hidden, *down_mats],
        ["vmem", "any", "any"],
        [jax.ShapeDtypeStruct((count, 2 * half, width), jnp.bfloat16)],
        [
            pltpu.VMEM((2, units, width), jnp.bfloat16),
            pltpu.SemaphoreType.DMA((2,)),
        ],
        4 * total * width * units,
        behind,
    )[0]


def run_d_hidden(parts, slope, activated, down_mats):
    count, rows, width = len(parts), parts[0].shape[0], parts[0].shape[1]
    _, total, units = slope.shape
    tile = cut(units, 256)
    tiles = units // tile

    def kernel(*refs):
        part_refs = refs[:count]
        slope_ref, act_ref, own_ref, other_ref = refs[count : count + 4]
        d_gate_ref, d_up_ref, packed, held, sems = refs[count + 4 :]
        copies = {}
        for e, mat in enumerate((own_ref, other_ref)):
            for n in range(tiles):
                copies[e, n] = pltpu.make_async_copy(
                    mat.at[n * tile : (n + 1) * tile, :], held.at[e, n], sems.at[e, n]
                )
                copies[e, n].start()
        pack_rows(part_refs, packed)
        for e in range(2):
            for n in range(tiles):
                span = slice(n * tile, (n + 1) * tile)
                copies[e, n].wait()
                d_hidden = lax.dot_general(
                    packed[e], held[e, n], LAST, preferred_element_type=jnp.float32
                )
                d_gate_ref[e, :, span] = (d_hidden * slope_ref[e, :, span]).astype(jnp.bfloat16)
                d_up_ref[e, :, span] = (d_hidden * act_ref[e, :, span]).astype(jnp.bfloat16)

    return call_kernel(
        kernel,
        [*parts, slope, activated, *down_mats],
        ["vmem"] * (count + 2) + ["any"] * 2,
        [jax.ShapeDtypeStruct((2, total, units), jnp.bfloat16)] * 2,
        [
            pltpu.VMEM((2, total, width), jnp.bfloat16),
            pltpu.VMEM((2, tiles, tile, width), jnp.bfloat16),
            pltpu.SemaphoreType.DMA((2, tiles)),
        ],
        4 * total * width * units,
    )


def run_d_gates(ids, parts, outputs, pick, behind):
    count, rows = len(parts), parts[0].shape[0]
    half = rows // 2
    tokens = pick.shape[2]

    def kernel(*refs):
        ids_ref, part_refs = refs[0], refs[1 : 1 + count]
        out_ref, pick_ref, token_ref = refs[1 + count :]
        for s in range(count):
            inner = jnp.sum(
                part_refs[s][...].astype(jnp.float32) * out_ref[s].astype(jnp.float32),
                axis=1,
                keepdims=True,
            )
            spread = pick_ref[s].astype(jnp.float32) * inner
            sums = [
                jnp.sum(spread[e * half : (e + 1) * half], axis=0, keepdims=True)
                for e in range(2)
            ]
            token_ref[source_at(s, ids_ref[1], count)] = jnp.concatenate(sums, axis=0)

    return call_kernel(
        kernel,
        [ids, *parts, outputs, pick],
        ["smem"] + ["vmem"] * (count + 2),
        [jax.ShapeDtypeStruct((count, 2, tokens), jnp.float32)],
        [],
        1 << 20,
        behind,
    )[0]


def run_d_copy(d_pre_gate, d_pre_up, gate_mats, up_mats, count, behind):
    _, total, units = d_pre_gate.shape
    width = gate_mats[0].shape[0]
    half = total // count
    tile = cut(width, 512)
    tiles = width // tile

    def kernel(d_gate_ref, d_up_ref, *refs):
        mats = refs[:4]
        out_ref, held, sems = refs[4:]
        copies = {}
        for e in range(2):
            for n in range(tiles):
                for m in range(2):
                    copies[e, n, m] = pltpu.make_async_copy(
                        mats[2 * m + e].at[n * tile : (n + 1) * tile, :],
                        held.at[e, n, m],
                        sems.at[e, n, m],
                    )
                    copies[e, n, m].start()
        for e in range(2):
            for n in range(tiles):
                copies[e, n, 0].wait()
                out = lax.dot_general(
                    d_gate_ref[e], held[e, n, 0], LAST, preferred_element_type=jnp.float32
                )
                copies[e, n, 1].wait()
                out = out + lax.dot_general(
                    d_up_ref[e], held[e, n, 1], LAST, preferred_element_type=jnp.float32
                )
                out_ref[:, e * half : (e + 1) * half, n * tile : (n + 1) * tile] = (
                    out.astype(jnp.bfloat16).reshape(count, half, tile)
                )

    return call_kernel(
        kernel,
        [d_pre_gate, d_pre_up, *gate_mats, *up_mats],
        ["vmem", "vmem"] + ["any"] * 4,
        [jax.ShapeDtypeStruct((count, 2 * half, width), jnp.bfloat16)],
        [
            pltpu.VMEM((2, tiles, 2, tile, units), jnp.bfloat16),
            pltpu.SemaphoreType.DMA((2, tiles, 2)),
        ],
        8 * total * width * units,
        behind,
    )[0]


def swap_cores(array):
    return lax.ppermute(array, "grp", [(0, 1), (1, 0)])


def body_ring(tokens, cotangent, routes, gates, w_gate, w_up, w_down):
    token_count = tokens.shape[0]
    width = tokens.shape[1]
    top_count = routes.shape[1]
    chips = lax.axis_size("ep")
    expert_count = lax.axis_size(("grp", "ep"))
    capacity = max(2, 3 * token_count * top_count // (2 * expert_count))
    f32, bf16 = jnp.float32, jnp.bfloat16

    core = lax.axis_index("grp")
    chip = lax.axis_index("ep")
    ids = jnp.stack([core, chip]).astype(jnp.int32)
    table = jnp.concatenate([routes.astype(f32), gates.astype(f32)], axis=1).T
    copies = jnp.broadcast_to(table[None], (chips,) + table.shape)
    tables = lax.all_to_all(copies, "ep", split_axis=0, concat_axis=0, tiled=True)
    gate_mats = (w_gate[0], swap_cores(w_gate[0]))
    up_mats = (w_up[0], swap_cores(w_up[0]))
    down_mats = (w_down[0], swap_cores(w_down[0]))
    pick, spread = run_routing(ids, tables, top_count, capacity, (gate_mats[1], up_mats[1]))

    swapped = (down_mats[1],)

    behind = {(step, 2): (tables,) for step in (1, -1)}
    behind.update({(step, 3): swapped for step in (1, -1)})
    in_shards, in_hops = ring_gather(tokens, chips, 1, behind)
    grad_later = run_hold(cotangent, (in_hops[1][1], in_hops[-1][1], *swapped))
    grad_shards, grad_hops = ring_gather(grad_later, chips, -1)

    def gather_rows(shards):
        return [
            jnp.dot(pick[s], shards[s], preferred_element_type=f32).astype(bf16)
            for s in range(chips)
        ]

    def scatter_rows(blocks):
        def share_of(s, partial, waits=(), add_waits=False):
            total = lax.dot_general(
                spread[s], blocks[s], (((0,), (0,)), ((), ())), preferred_element_type=f32
            )
            if partial is not None:
                total = total + partial.astype(f32)
            if add_waits:
                return (total + waits[0].astype(f32)).astype(bf16)
            return after(total.astype(bf16), *waits)

        return share_of

    rows_in = gather_rows(in_shards)
    hidden, slope, activated = run_hidden(
        rows_in, gate_mats, up_mats, [grad_hops[-1][1]]
    )
    outputs = run_down(hidden, down_mats, chips, [grad_hops[-1][2]])
    rows_grad = gather_rows(grad_shards)
    d_pre_gate, d_pre_up = run_d_hidden(rows_grad, slope, activated, down_mats)
    behind = {(-1, 0): (grad_hops[-1][-1],), (-1, 1): (d_pre_gate,)}
    mixed, mixed_hops = ring_reduce(scatter_rows(outputs), chips, 1, behind)
    d_copies = run_d_copy(
        d_pre_gate, d_pre_up, gate_mats, up_mats, chips, [mixed_hops[step][0] for step in (1, -1)]
    )

    per_token = run_d_gates(ids, rows_grad, outputs, pick, (d_pre_gate,))
    returned = lax.all_to_all(per_token, "ep", split_axis=0, concat_axis=0, tiled=True)
    behind = {
        (step, hop): (mixed_hops[step][hop + 1],)
        for step in (1, -1)
        for hop in range(len(mixed_hops[step]) - 1)
    }
    behind[-1, 1] += (per_token,)
    behind[-1, 3] = (returned,)
    d_tokens, _ = ring_reduce(scatter_rows(d_copies), chips, -1, behind)
    chip_ids = jnp.arange(chips, dtype=jnp.int32)
    served = jnp.stack([core * chips + chip_ids, (1 - core) * chips + chip_ids], axis=1)
    chosen = routes.T[None, None] == served[:, :, None, None]
    d_gates = jnp.sum(jnp.where(chosen, returned[:, :, None, :], 0.0), axis=(0, 1)).T
    return (mixed, d_tokens, d_gates)


def solution(mesh):
    plan = body_ring if mesh.shape["ep"] <= 8 and mesh.shape["grp"] == 2 else body_exchange
    return jax.shard_map(
        plan,
        mesh=mesh,
        in_specs=(
            P(("rep", "grp", "ep"), None),
            P(("rep", "grp", "ep"), None),
            P(("rep", "grp", "ep"), None),
            P(("rep", "grp", "ep"), None),
            P(("grp", "ep"), None, None),
            P(("grp", "ep"), None, None),
            P(("grp", "ep"), None, None),
        ),
        out_specs=(
            P(("rep", "grp", "ep"), None),
            P(("rep", "grp", "ep"), None),
            P(("rep", "grp", "ep"), None),
        ),
        check_vma=False,
    )
```

```python
import jax
import jax.numpy as jnp
from jax import lax
from jax.experimental import pallas as pl
from jax.experimental.pallas import tpu as pltpu
from jax.sharding import PartitionSpec as P


def expert_pass(rows_in, rows_grad, gate_mat, up_mat, down_mat):
    pre_gate = jnp.dot(rows_in, gate_mat, preferred_element_type=jnp.float32)
    pre_up = jnp.dot(rows_in, up_mat, preferred_element_type=jnp.float32)
    activated = jax.nn.silu(pre_gate)
    hidden = (activated * pre_up).astype(jnp.bfloat16)
    outputs = jnp.dot(hidden, down_mat, preferred_element_type=jnp.float32).astype(jnp.bfloat16)
    d_hidden = lax.dot_general(
        rows_grad, down_mat, (((1,), (1,)), ((), ())), preferred_element_type=jnp.float32
    )
    sigma = jax.nn.sigmoid(pre_gate)
    d_pre_gate = (d_hidden * pre_up * sigma * (1.0 + pre_gate * (1.0 - sigma))).astype(jnp.bfloat16)
    d_pre_up = (d_hidden * activated).astype(jnp.bfloat16)
    both_pre = jnp.concatenate([d_pre_gate, d_pre_up], axis=1)
    both_mats = jnp.concatenate([gate_mat, up_mat], axis=1)
    d_copy = lax.dot_general(
        both_pre, both_mats, (((1,), (1,)), ((), ())), preferred_element_type=jnp.float32
    )
    return (outputs, d_copy.astype(jnp.bfloat16))


def run_items(pieces, gate_mat, up_mat, down_mat):
    rows_in, rows_grad = pieces
    lead_shape = rows_in.shape[:2]
    width = rows_in.shape[2]
    outputs, d_copy = expert_pass(
        rows_in.reshape(-1, width), rows_grad.reshape(-1, width), gate_mat, up_mat, down_mat
    )
    return (outputs.reshape(lead_shape + (width,)), d_copy.reshape(lead_shape + (width,)))


def ranks_of(chosen_hot):
    running = jnp.cumsum(chosen_hot, axis=-2)
    return jnp.sum(chosen_hot * running, axis=-1) - 1


def body_exchange(tokens, cotangent, routes, gates, w_gate, w_up, w_down):
    token_count = tokens.shape[0]
    width = tokens.shape[1]
    top_count = routes.shape[1]
    copy_count = token_count * top_count
    gate_mat = w_gate[0]
    up_mat = w_up[0]
    down_mat = w_down[0]
    expert_count = lax.axis_size(("grp", "ep"))
    capacity = max(2, 3 * token_count * top_count // (2 * expert_count))
    flat_experts = routes.reshape(-1)
    chosen_hot = (
        flat_experts[:, None] == jnp.arange(expert_count, dtype=jnp.int32)[None, :]
    ).astype(jnp.int32)
    slot_of = flat_experts * capacity + ranks_of(chosen_hot)
    token_of = jnp.arange(copy_count, dtype=jnp.int32) // top_count
    slot_token = jnp.zeros((expert_count * capacity,), jnp.int32).at[slot_of].set(token_of)
    slot_live = jnp.zeros((expert_count * capacity,), jnp.bool_).at[slot_of].set(True)
    send_in = jnp.where(
        slot_live[:, None], tokens[slot_token], jnp.zeros((), tokens.dtype)
    ).reshape(expert_count, capacity, width)
    send_grad = jnp.where(
        slot_live[:, None], cotangent[slot_token], jnp.zeros((), cotangent.dtype)
    ).reshape(expert_count, capacity, width)
    outputs, d_copy = run_items(
        (
            lax.all_to_all(send_in, ("grp", "ep"), split_axis=0, concat_axis=0, tiled=True),
            lax.all_to_all(send_grad, ("grp", "ep"), split_axis=0, concat_axis=0, tiled=True),
        ),
        gate_mat,
        up_mat,
        down_mat,
    )
    back_out = lax.all_to_all(outputs, ("grp", "ep"), split_axis=0, concat_axis=0, tiled=True)
    back_grad = lax.all_to_all(d_copy, ("grp", "ep"), split_axis=0, concat_axis=0, tiled=True)
    copy_out = back_out.reshape(-1, width)[slot_of].reshape(token_count, top_count, width)
    copy_grad = back_grad.reshape(-1, width)[slot_of].reshape(token_count, top_count, width)
    weight = gates.astype(jnp.float32)
    mixed = jnp.sum(weight[:, :, None] * copy_out.astype(jnp.float32), axis=1)
    d_tokens = jnp.sum(weight[:, :, None] * copy_grad.astype(jnp.float32), axis=1)
    d_gates = jnp.einsum("tkd,td->tk", copy_out, cotangent, preferred_element_type=jnp.float32)
    return (mixed.astype(jnp.bfloat16), d_tokens.astype(jnp.bfloat16), d_gates)


def ring_order(count):
    return list(range(0, count, 2)) + list(range(count - 1, 0, -2))


def ring_shift(array, count, step):
    order = ring_order(count)
    pairs = [(order[i], order[(i + step) % count]) for i in range(count)]
    return lax.ppermute(array, "ep", pairs)


def ring_gather(shard, count, far_step, behind={}):
    held = {0: shard}
    arrivals = {}
    for step in (far_step, -far_step):
        hops = count // 2 if step == far_step else (count - 1) // 2
        moving = shard
        arrivals[step] = []
        for hop in range(1, hops + 1):
            if (step, hop) in behind:
                moving = held_back(moving, behind[step, hop])
                if hop > 1:
                    held[(-step * (hop - 1)) % count] = moving
            moving = ring_shift(moving, count, step)
            held[(-step * hop) % count] = moving
            arrivals[step].append(moving)
    return [held[place] for place in range(count)], arrivals


def after(array, *others):
    for other in others:
        array = array + other[(slice(0, 1),) * other.ndim].reshape((1,) * array.ndim).astype(array.dtype) * 0
    return array


def held_back(array, others):
    def kernel(*refs):
        pass

    return pl.pallas_call(
        kernel,
        out_shape=jax.ShapeDtypeStruct(array.shape, array.dtype),
        in_specs=[pl.BlockSpec(memory_space=pl.ANY) for _ in range(1 + len(others))],
        out_specs=pl.BlockSpec(memory_space=pl.ANY),
        input_output_aliases={0: 0},
    )(array, *others)


def ring_reduce(share_of, count, far_step, behind={}):
    arrived = {}
    for step in (far_step, -far_step):
        hops = count // 2 if step == far_step else (count - 1) // 2
        moving = None
        steps = []
        for hop in range(hops, 0, -1):
            waits = behind.get((step, hops - hop), ())
            share = share_of((step * hop) % count, moving, waits)
            moving = ring_shift(share, count, step)
            steps.append(moving)
        arrived[step] = steps
    total = share_of(0, arrived[far_step][-1], (arrived[-far_step][-1],), True)
    return total, arrived


VMEM_LIMIT = 48 * 1024 * 1024
LAST = (((1,), (1,)), ((), ()))


def cut(size, most):
    return max(w for w in range(128, most + 1, 128) if size % w == 0)


def call_kernel(kernel, operands, kinds, outs, scratch, flops, behind=()):
    spaces = {"any": pl.ANY, "vmem": pltpu.VMEM, "smem": pltpu.SMEM}
    count = len(operands)
    operands = [*operands, *behind]
    kinds = [*kinds, *["any" for _ in behind]]

    def body(*refs):
        kernel(*refs[:count], *refs[len(operands) :])

    return pl.pallas_call(
        body,
        out_shape=outs,
        in_specs=[pl.BlockSpec(memory_space=spaces[k]) for k in kinds],
        out_specs=[pl.BlockSpec(memory_space=pltpu.VMEM) for _ in outs],
        scratch_shapes=scratch,
        compiler_params=pltpu.CompilerParams(vmem_limit_bytes=VMEM_LIMIT),
        cost_estimate=pl.CostEstimate(flops=flops, bytes_accessed=1 << 20, transcendentals=0),
    )(*operands)


def pack_rows(parts, packed):
    half = parts[0].shape[0] // 2
    for e in range(2):
        for s, part in enumerate(parts):
            packed[e, s * half : (s + 1) * half, :] = part[e * half : (e + 1) * half, :]


def source_at(distance, chip, count):
    place = jnp.where(chip % 2 == 0, chip // 2, count - (chip + 1) // 2)
    place = (place + distance) % count
    return jnp.where(place < count // 2, 2 * place, 2 * (count - place) - 1)


def run_hold(array, behind):
    def kernel(in_ref, out_ref):
        out_ref[...] = in_ref[...]

    shape = jax.ShapeDtypeStruct(array.shape, array.dtype)
    return call_kernel(kernel, [array], ["vmem"], [shape], [], 1, behind)[0]


def run_routing(ids, tables, top_count, capacity, behind):
    count, _, tokens = tables.shape
    f32, bf16 = jnp.float32, jnp.bfloat16

    def kernel(ids_ref, table_ref, pick_ref, spread_ref):
        core, chip = ids_ref[0], ids_ref[1]
        first = lax.broadcasted_iota(jnp.int32, (tokens, tokens), 0)
        second = lax.broadcasted_iota(jnp.int32, (tokens, tokens), 1)
        before = (first <= second).astype(f32).astype(bf16)
        slot = lax.broadcasted_iota(jnp.int32, (capacity, tokens), 0).astype(f32)
        hits, weights = [], []
        for s in range(count):
            table = table_ref[source_at(s, chip, count)]
            for e in range(2):
                expert = jnp.where(core == e, chip, count + chip).astype(f32)
                hit = (table[:top_count] == expert).astype(f32)
                hits.append(jnp.sum(hit, axis=0, keepdims=True))
                weights.append(
                    jnp.sum(hit * table[top_count : 2 * top_count], axis=0, keepdims=True)
                )
        rank = jnp.dot(
            jnp.concatenate(hits, axis=0).astype(bf16), before, preferred_element_type=f32
        )
        for s in range(count):
            for e in range(2):
                i = 2 * s + e
                chosen = jnp.where(slot == rank[i : i + 1] - 1.0, hits[i], 0.0)
                span = slice(e * capacity, (e + 1) * capacity)
                pick_ref[s, span, :] = chosen.astype(bf16)
                spread_ref[s, span, :] = (chosen * weights[i]).astype(bf16)

    shape = jax.ShapeDtypeStruct((count, 2 * capacity, tokens), bf16)
    return call_kernel(kernel, [ids, tables], ["smem", "vmem"], [shape, shape], [], 1 << 20, behind)


def run_hidden(parts, gate_mats, up_mats, behind):
    count, rows, width = len(parts), parts[0].shape[0], parts[0].shape[1]
    units = gate_mats[0].shape[1]
    total = count * rows // 2
    tile = cut(units, 256)
    tiles = units // tile

    def kernel(*refs):
        part_refs, mats = refs[:count], refs[count : count + 4]
        hidden_ref, slope_ref, act_ref, packed, held, sems = refs[count + 4 :]
        copies = {}
        for e in range(2):
            for m in range(2):
                copies[e, m] = pltpu.make_async_copy(
                    mats[2 * m + e], held.at[e, m], sems.at[e, m]
                )
                copies[e, m].start()
        pack_rows(part_refs, packed)
        for e in range(2):
            for m in range(2):
                copies[e, m].wait()
            for n in range(tiles):
                span = slice(n * tile, (n + 1) * tile)
                gate = jnp.dot(packed[e], held[e, 0, :, span], preferred_element_type=jnp.float32)
                up = jnp.dot(packed[e], held[e, 1, :, span], preferred_element_type=jnp.float32)
                sigma = 1.0 / (1.0 + jnp.exp(-gate))
                act = gate * sigma
                hidden_ref[e, :, span] = (act * up).astype(jnp.bfloat16)
                slope_ref[e, :, span] = up * sigma * (1.0 + gate * (1.0 - sigma))
                act_ref[e, :, span] = act

    return call_kernel(
        kernel,
        [*parts, *gate_mats, *up_mats],
        ["vmem"] * count + ["any"] * 4,
        [
            jax.ShapeDtypeStruct((2, total, units), jnp.bfloat16),
            jax.ShapeDtypeStruct((2, total, units), jnp.float32),
            jax.ShapeDtypeStruct((2, total, units), jnp.float32),
        ],
        [
            pltpu.VMEM((2, total, width), jnp.bfloat16),
            pltpu.VMEM((2, 2, width, units), jnp.bfloat16),
            pltpu.SemaphoreType.DMA((2, 2)),
        ],
        8 * total * width * units,
        behind,
    )


def run_down(hidden, down_mats, count, behind):
    _, total, units = hidden.shape
    width = down_mats[0].shape[1]
    half = total // count
    tile = cut(width, 512)
    tiles = width // tile

    def kernel(hidden_ref, own_ref, other_ref, out_ref, held, sems):
        copies = {}
        for e, mat in enumerate((own_ref, other_ref)):
            copies[e] = pltpu.make_async_copy(mat, held.at[e], sems.at[e])
            copies[e].start()
        for e in range(2):
            copies[e].wait()
            for n in range(tiles):
                columns = held[e, :, n * tile : (n + 1) * tile]
                out = jnp.dot(hidden_ref[e], columns, preferred_element_type=jnp.float32)
                out_ref[:, e * half : (e + 1) * half, n * tile : (n + 1) * tile] = (
                    out.astype(jnp.bfloat16).reshape(count, half, tile)
                )

    return call_kernel(
        kernel,
        [hidden, *down_mats],
        ["vmem", "any", "any"],
        [jax.ShapeDtypeStruct((count, 2 * half, width), jnp.bfloat16)],
        [
            pltpu.VMEM((2, units, width), jnp.bfloat16),
            pltpu.SemaphoreType.DMA((2,)),
        ],
        4 * total * width * units,
        behind,
    )[0]


def run_d_hidden(parts, slope, activated, down_mats):
    count, rows, width = len(parts), parts[0].shape[0], parts[0].shape[1]
    _, total, units = slope.shape
    tile = cut(units, 256)
    tiles = units // tile

    def kernel(*refs):
        part_refs = refs[:count]
        slope_ref, act_ref, own_ref, other_ref = refs[count : count + 4]
        d_gate_ref, d_up_ref, packed, held, sems = refs[count + 4 :]
        copies = {}
        for e, mat in enumerate((own_ref, other_ref)):
            for n in range(tiles):
                copies[e, n] = pltpu.make_async_copy(
                    mat.at[n * tile : (n + 1) * tile, :], held.at[e, n], sems.at[e, n]
                )
                copies[e, n].start()
        pack_rows(part_refs, packed)
        for e in range(2):
            for n in range(tiles):
                span = slice(n * tile, (n + 1) * tile)
                copies[e, n].wait()
                d_hidden = lax.dot_general(
                    packed[e], held[e, n], LAST, preferred_element_type=jnp.float32
                )
                d_gate_ref[e, :, span] = (d_hidden * slope_ref[e, :, span]).astype(jnp.bfloat16)
                d_up_ref[e, :, span] = (d_hidden * act_ref[e, :, span]).astype(jnp.bfloat16)

    return call_kernel(
        kernel,
        [*parts, slope, activated, *down_mats],
        ["vmem"] * (count + 2) + ["any"] * 2,
        [jax.ShapeDtypeStruct((2, total, units), jnp.bfloat16)] * 2,
        [
            pltpu.VMEM((2, total, width), jnp.bfloat16),
            pltpu.VMEM((2, tiles, tile, width), jnp.bfloat16),
            pltpu.SemaphoreType.DMA((2, tiles)),
        ],
        4 * total * width * units,
    )


def run_d_gates(ids, parts, outputs, pick, behind):
    count, rows = len(parts), parts[0].shape[0]
    half = rows // 2
    tokens = pick.shape[2]

    def kernel(*refs):
        ids_ref, part_refs = refs[0], refs[1 : 1 + count]
        out_ref, pick_ref, token_ref = refs[1 + count :]
        for s in range(count):
            inner = jnp.sum(
                part_refs[s][...].astype(jnp.float32) * out_ref[s].astype(jnp.float32),
                axis=1,
                keepdims=True,
            )
            spread = pick_ref[s].astype(jnp.float32) * inner
            sums = [
                jnp.sum(spread[e * half : (e + 1) * half], axis=0, keepdims=True)
                for e in range(2)
            ]
            token_ref[source_at(s, ids_ref[1], count)] = jnp.concatenate(sums, axis=0)

    return call_kernel(
        kernel,
        [ids, *parts, outputs, pick],
        ["smem"] + ["vmem"] * (count + 2),
        [jax.ShapeDtypeStruct((count, 2, tokens), jnp.float32)],
        [],
        1 << 20,
        behind,
    )[0]


def run_d_copy(d_pre_gate, d_pre_up, gate_mats, up_mats, count, behind):
    _, total, units = d_pre_gate.shape
    width = gate_mats[0].shape[0]
    half = total // count
    tile = cut(width, 512)
    tiles = width // tile

    def kernel(d_gate_ref, d_up_ref, *refs):
        mats = refs[:4]
        out_ref, held, sems = refs[4:]
        copies = {}
        for e in range(2):
            for n in range(tiles):
                for m in range(2):
                    copies[e, n, m] = pltpu.make_async_copy(
                        mats[2 * m + e].at[n * tile : (n + 1) * tile, :],
                        held.at[e, n, m],
                        sems.at[e, n, m],
                    )
                    copies[e, n, m].start()
        for e in range(2):
            for n in range(tiles):
                copies[e, n, 0].wait()
                out = lax.dot_general(
                    d_gate_ref[e], held[e, n, 0], LAST, preferred_element_type=jnp.float32
                )
                copies[e, n, 1].wait()
                out = out + lax.dot_general(
                    d_up_ref[e], held[e, n, 1], LAST, preferred_element_type=jnp.float32
                )
                out_ref[:, e * half : (e + 1) * half, n * tile : (n + 1) * tile] = (
                    out.astype(jnp.bfloat16).reshape(count, half, tile)
                )

    return call_kernel(
        kernel,
        [d_pre_gate, d_pre_up, *gate_mats, *up_mats],
        ["vmem", "vmem"] + ["any"] * 4,
        [jax.ShapeDtypeStruct((count, 2 * half, width), jnp.bfloat16)],
        [
            pltpu.VMEM((2, tiles, 2, tile, units), jnp.bfloat16),
            pltpu.SemaphoreType.DMA((2, tiles, 2)),
        ],
        8 * total * width * units,
        behind,
    )[0]


def swap_cores(array):
    return lax.ppermute(array, "grp", [(0, 1), (1, 0)])


def body_ring(tokens, cotangent, routes, gates, w_gate, w_up, w_down):
    token_count = tokens.shape[0]
    width = tokens.shape[1]
    top_count = routes.shape[1]
    chips = lax.axis_size("ep")
    expert_count = lax.axis_size(("grp", "ep"))
    capacity = max(2, 3 * token_count * top_count // (2 * expert_count))
    f32, bf16 = jnp.float32, jnp.bfloat16

    core = lax.axis_index("grp")
    chip = lax.axis_index("ep")
    ids = jnp.stack([core, chip]).astype(jnp.int32)
    table = jnp.concatenate([routes.astype(f32), gates.astype(f32)], axis=1).T
    copies = jnp.broadcast_to(table[None], (chips,) + table.shape)
    tables = lax.all_to_all(copies, "ep", split_axis=0, concat_axis=0, tiled=True)
    gate_mats = (w_gate[0], swap_cores(w_gate[0]))
    up_mats = (w_up[0], swap_cores(w_up[0]))
    down_mats = (w_down[0], swap_cores(w_down[0]))
    pick, spread = run_routing(ids, tables, top_count, capacity, (gate_mats[1], up_mats[1]))

    swapped = (down_mats[1],)

    behind = {(step, 2): (tables,) for step in (1, -1)}
    behind.update({(step, 3): swapped for step in (1, -1)})
    in_shards, in_hops = ring_gather(tokens, chips, 1, behind)
    grad_later = run_hold(cotangent, (in_hops[1][1], in_hops[-1][1], *swapped))
    grad_shards, grad_hops = ring_gather(grad_later, chips, -1)

    def gather_rows(shards):
        return [
            jnp.dot(pick[s], shards[s], preferred_element_type=f32).astype(bf16)
            for s in range(chips)
        ]

    def scatter_rows(blocks):
        def share_of(s, partial, waits=(), add_waits=False):
            total = lax.dot_general(
                spread[s], blocks[s], (((0,), (0,)), ((), ())), preferred_element_type=f32
            )
            if partial is not None:
                total = total + partial.astype(f32)
            if add_waits:
                return (total + waits[0].astype(f32)).astype(bf16)
            return after(total.astype(bf16), *waits)

        return share_of

    rows_in = gather_rows(in_shards)
    hidden, slope, activated = run_hidden(
        rows_in, gate_mats, up_mats, [grad_hops[-1][1]]
    )
    outputs = run_down(hidden, down_mats, chips, [grad_hops[-1][2]])
    rows_grad = gather_rows(grad_shards)
    d_pre_gate, d_pre_up = run_d_hidden(rows_grad, slope, activated, down_mats)
    behind = {(-1, 0): (grad_hops[-1][-1],), (-1, 1): (d_pre_gate,)}
    mixed, mixed_hops = ring_reduce(scatter_rows(outputs), chips, 1, behind)
    d_copies = run_d_copy(
        d_pre_gate, d_pre_up, gate_mats, up_mats, chips, [mixed_hops[step][0] for step in (1, -1)]
    )

    per_token = run_d_gates(ids, rows_grad, outputs, pick, (d_pre_gate,))
    returned = lax.all_to_all(per_token, "ep", split_axis=0, concat_axis=0, tiled=True)
    behind = {
        (step, hop): (mixed_hops[step][hop + 1],)
        for step in (1, -1)
        for hop in range(len(mixed_hops[step]) - 1)
    }
    behind[-1, 1] += (per_token,)
    behind[-1, 2] = (returned,)
    d_tokens, _ = ring_reduce(scatter_rows(d_copies), chips, -1, behind)
    chip_ids = jnp.arange(chips, dtype=jnp.int32)
    served = jnp.stack([core * chips + chip_ids, (1 - core) * chips + chip_ids], axis=1)
    chosen = routes.T[None, None] == served[:, :, None, None]
    d_gates = jnp.sum(jnp.where(chosen, returned[:, :, None, :], 0.0), axis=(0, 1)).T
    return (mixed, d_tokens, d_gates)


def solution(mesh):
    plan = body_ring if mesh.shape["ep"] <= 8 and mesh.shape["grp"] == 2 else body_exchange
    return jax.shard_map(
        plan,
        mesh=mesh,
        in_specs=(
            P(("rep", "grp", "ep"), None),
            P(("rep", "grp", "ep"), None),
            P(("rep", "grp", "ep"), None),
            P(("rep", "grp", "ep"), None),
            P(("grp", "ep"), None, None),
            P(("grp", "ep"), None, None),
            P(("grp", "ep"), None, None),
        ),
        out_specs=(
            P(("rep", "grp", "ep"), None),
            P(("rep", "grp", "ep"), None),
            P(("rep", "grp", "ep"), None),
        ),
        check_vma=False,
    )
```
